32 devices in a mesh: grp: 2 (over y), die: 4 (over z), sub: 2 (over x), blk: 2 (over core).
Axes of the slice: x: 2, y: 2, z: 4, core: 2. Of those that a mesh axis runs over, the one named last changes fastest.
Arguments:
- history: float32 [1024, 3, 32, 128], P(('grp', 'die', 'sub', 'blk')), parts along dimension 0, may hold values from -2 to 2
- new_slot: int32 [1024], P(('grp', 'die', 'sub', 'blk')), parts along dimension 0, may hold values from 0 to 511, as said below
- partner: int32 [1024], P(('grp', 'die', 'sub', 'blk')), parts along dimension 0, may hold values from 0 to 511, as said below
- coupling: float32 [1024, 128, 128], P(('grp', 'die', 'sub', 'blk')), parts along dimension 0, as said below
- cap_rate: float32 [1024, 128], P(('grp', 'die', 'sub', 'blk')), parts along dimension 0, may hold values from 0.5 to 5
- device_gain: float32 [1024, 128], P(('grp', 'die', 'sub', 'blk')), parts along dimension 0, may hold values from 0.2 to 2
- wire_gain: float32 [1024, 128], P(('grp', 'die', 'sub', 'blk')), parts along dimension 0, may hold values from 0.2 to 2
- region_gain: float32 [1024, 128], P(('grp', 'die', 'sub', 'blk')), parts along dimension 0, may hold values from 0.2 to 1
- drive: float32 [1024, 32, 128], P(('grp', 'die', 'sub', 'blk')), parts along dimension 0, may hold values from -6 to 6
- region_inverse: float32 [8, 128, 128], P(('grp', 'die'), 'blk'), parts along dimension 0
Outputs:
- updated: float32 [1024, 32, 128], P(('grp', 'die', 'sub', 'blk')), parts along dimension 0
- residual: float32 [1024, 32, 128], P(('grp', 'die', 'sub', 'blk')), parts along dimension 0
The draws below stay inside these ranges and needn't reach their ends.
There are 2 independent parts, one for each index of `grp`. The reference program is written for one: setup_inputs(seed, part) draws one part's arguments, and reference() takes and returns one part's arrays. A program takes and returns all parts, laid end to end along the dimension named above; each array names one. Nothing has to cross between parts.
Inputs may be any that keep to these rules, and one draw needn't show every extreme that they name: `new_slot`: A permutation; a subcircuit moves only between devices that share the sub and blk index. The subcircuits leaving a device fill exactly the slots that its own leaving subcircuits vacate on the receiving side. At most 2 subcircuits of one device go to one other device, and this is reached on every device. Every partner lies on a device with the same sub and blk index. At most 16 subcircuits of one device read from blocks of one owner device, reached on every device. `coupling`: diagonal entries between 1.5 and 3.5.
All inputs are finite; a program needn't handle non-finite values.
Results may differ from the reference program's by a relative error of at most 0.00005.
Values sent between devices are 32-bit elements; how exact they have to be, the bound alone decides.
No kernel may reach another device: no remote copies, remote signals or barrier semaphores. Data moves between devices by JAX's collectives and lax.ppermute only.
A program may use at most 64 MiB of HBM per device.

```python
import math
import jax
import jax.numpy as jnp
from jax import lax

NODES = 128
SB = 32
NS = 32
CAP = 2
MOVED = 4
RCAP = 16
SUBS = 512
N_DIE = 4
N_SUB = 2
N_BLK = 2


def draw_new_slot(key, part):
    key = jax.random.fold_in(key, 11)
    ncol = N_SUB * N_BLK

    def one_column(column_key):
        first, second, third = jax.random.split(column_key, 3)
        shift = jax.random.permutation(first, N_DIE).astype(jnp.int32)
        order = jax.random.permutation(second, N_DIE).astype(jnp.int32)
        perms = jax.vmap(lambda k: jax.random.permutation(k, SB).astype(jnp.int32))(jax.random.split(third, N_DIE))
        slots = jnp.arange(SB, dtype=jnp.int32)
        dies = jnp.arange(N_DIE, dtype=jnp.int32)
        group = slots // CAP
        target = order[(shift[:, None] + group[None, :]) % N_DIE]
        target = jnp.where(slots[None, :] < MOVED, target, dies[:, None])
        target_loc = perms[target, jnp.broadcast_to(slots[None, :], (N_DIE, SB))]
        return (target, target_loc, perms)
    target, target_loc, perms = jax.vmap(one_column)(jax.random.split(key, ncol))
    columns = jnp.arange(ncol, dtype=jnp.int32)[:, None, None]
    dies = jnp.arange(N_DIE, dtype=jnp.int32)[None, :, None]
    value = (target * ncol + columns) * SB + target_loc
    where_at = (dies * ncol + columns) * SB + perms
    return jnp.zeros((SUBS,), jnp.int32).at[where_at.ravel()].set(value.ravel())


def draw_partner(key, part):
    key = jax.random.fold_in(key, 12)
    ncol = N_SUB * N_BLK

    def one_column(column_key):
        first, second, third, fourth = jax.random.split(column_key, 4)
        shift = jax.random.permutation(first, N_DIE).astype(jnp.int32)
        order = jax.random.permutation(second, N_DIE).astype(jnp.int32)
        perms = jax.vmap(lambda k: jax.random.permutation(k, SB).astype(jnp.int32))(jax.random.split(third, N_DIE))
        owner_loc = jax.random.randint(fourth, (N_DIE, SB), 0, SB).astype(jnp.int32)
        slots = jnp.arange(SB, dtype=jnp.int32)
        group = slots // RCAP
        owner = order[(shift[:, None] + group[None, :]) % N_DIE]
        return (owner, owner_loc, perms)
    owner, owner_loc, perms = jax.vmap(one_column)(jax.random.split(key, ncol))
    columns = jnp.arange(ncol, dtype=jnp.int32)[:, None, None]
    dies = jnp.arange(N_DIE, dtype=jnp.int32)[None, :, None]
    value = (owner * ncol + columns) * SB + owner_loc
    where_at = (dies * ncol + columns) * SB + perms
    return jnp.zeros((SUBS,), jnp.int32).at[where_at.ravel()].set(value.ravel())


def draw_coupling(key, part):
    key = jax.random.fold_in(key, 13)
    first, second = jax.random.split(key)
    shape = (SUBS, NODES, NODES)
    off = jax.random.normal(first, shape, jnp.float32) / jnp.sqrt(jnp.float32(NODES))
    main = jax.random.uniform(second, shape, jnp.float32, 1.5, 3.0)
    rows = lax.broadcasted_iota(jnp.int32, shape, 1)
    cols = lax.broadcasted_iota(jnp.int32, shape, 2)
    return jnp.where(rows == cols, main, off)


def draw_region_inverse(key, part):
    key = jax.random.fold_in(key, 14)
    first, second = jax.random.split(key)
    shape = (N_DIE, NODES, NODES)
    scale = 1.0 / jnp.sqrt(jnp.float32(SB * N_SUB * N_BLK))
    off = 0.5 * jax.random.normal(first, shape, jnp.float32) / jnp.sqrt(jnp.float32(NODES))
    main = jax.random.uniform(second, shape, jnp.float32, 0.5, 1.0)
    rows = lax.broadcasted_iota(jnp.int32, shape, 1)
    cols = lax.broadcasted_iota(jnp.int32, shape, 2)
    return scale * jnp.where(rows == cols, main, off)


def steps_of(key, dims, cuts, least, top_value):
    level, own = 1.0, jax.random.fold_in(key, 6)
    for axis_at, parts in cuts:
        draws = jnp.exp(jax.random.uniform(jax.random.fold_in(own, axis_at), (parts,), jnp.float32, least / len(cuts), top_value / len(cuts)))
        level = level * jnp.repeat(draws, dims[axis_at] // parts).reshape([-1 if axis == axis_at else 1 for axis in range(len(dims))])
    return level


def gaussian(rng, shape, scale, reach, shards=(), kind=jnp.bfloat16):
    level = steps_of(rng, shape, shards, -0.22, 0.18) if shards else 1.0
    array = jax.random.normal(rng, shape, jnp.float32) * scale * level
    return jnp.minimum(jnp.maximum(array, -reach), reach).astype(kind)


def setup_inputs(seed: int = 0, part: int = 0) -> dict:
    splits = jax.random.split(jax.random.key(seed), 11)
    part_splits = jax.random.split(jax.random.fold_in(splits[10], part), 11)
    history = gaussian(part_splits[0], (SUBS, 3, NS, NODES), 0.3, 2.0, ((0, 16),), jnp.float32)
    new_slot = draw_new_slot(jax.random.fold_in(jax.random.fold_in(splits[10], part), 71), part)
    partner = draw_partner(jax.random.fold_in(jax.random.fold_in(splits[10], part), 71), part)
    coupling = draw_coupling(jax.random.fold_in(jax.random.fold_in(splits[10], part), 71), part)
    cap_rate = jnp.clip(jnp.exp(math.log(5.0) - 2.3025851 * jax.random.uniform(part_splits[4], (SUBS, NODES), jnp.float32) ** steps_of(part_splits[4], (SUBS, NODES), ((0, 16),), -0.2, 0.2)), 0.5, 5.0)
    device_gain = jnp.clip(jnp.exp(math.log(2.0) - 2.3025851 * jax.random.uniform(part_splits[5], (SUBS, NODES), jnp.float32) ** steps_of(part_splits[5], (SUBS, NODES), ((0, 16),), -0.2, 0.2)), 0.2, 2.0)
    wire_gain = jnp.clip(jnp.exp(math.log(2.0) - 2.3025851 * jax.random.uniform(part_splits[6], (SUBS, NODES), jnp.float32) ** steps_of(part_splits[6], (SUBS, NODES), ((0, 16),), -0.2, 0.2)), 0.2, 2.0)
    region_gain = jnp.clip(jnp.exp(math.log(1.0) - 1.609438 * jax.random.uniform(part_splits[7], (SUBS, NODES), jnp.float32) ** steps_of(part_splits[7], (SUBS, NODES), ((0, 16),), -0.2, 0.2)), 0.2, 1.0)
    drive = gaussian(part_splits[8], (SUBS, NS, NODES), 1.0, 6.0, ((0, 16),), jnp.float32)
    region_inverse = draw_region_inverse(jax.random.fold_in(jax.random.fold_in(splits[10], part), 71), part)
    return {"history": history, "new_slot": new_slot, "partner": partner, "coupling": coupling, "cap_rate": cap_rate, "device_gain": device_gain, "wire_gain": wire_gain, "region_gain": region_gain, "drive": drive, "region_inverse": region_inverse}


def reference(history, new_slot, partner, coupling, cap_rate, device_gain, wire_gain, region_gain, drive, region_inverse):
    moved = jnp.zeros_like(history).at[new_slot].set(history)
    guess = 3.0 * moved[:, 0] - 3.0 * moved[:, 1] + moved[:, 2]
    memory = 4.0 * moved[:, 0] - moved[:, 1]
    neighbour = guess[partner]
    tnh = jnp.tanh(guess)
    through = jnp.einsum("snk,sik->sni", guess, coupling, precision=lax.Precision.HIGHEST)
    diagonal = jnp.diagonal(coupling, axis1=1, axis2=2)
    cap = cap_rate[:, None, :]
    gdev = device_gain[:, None, :]
    wire = wire_gain[:, None, :]
    gain = region_gain[:, None, :]
    pivot = 1.5 * cap + diagonal[:, None, :] + gdev * (1.0 - tnh * tnh) + wire
    residual = 0.5 * cap * (3.0 * guess - memory) + through + gdev * tnh + wire * (guess - neighbour) - drive
    scaled = residual / pivot
    regions = region_inverse.shape[0]
    share = jnp.sum((gain * scaled).reshape(regions, -1, NS, NODES), axis=1)
    region = jnp.einsum("dnk,dki->dni", share, region_inverse, precision=lax.Precision.HIGHEST)
    spread = jnp.repeat(region, SUBS // regions, axis=0)
    updated = guess + (gain * spread - residual) / pivot
    return updated, residual
```

```python
import functools

import jax
import jax.numpy as jnp
from jax import lax
from jax.experimental import pallas as pl
from jax.experimental.pallas import tpu as pltpu
from jax.sharding import PartitionSpec as P

CAP = 2
META = 128
VMEM = pl.BlockSpec(memory_space=pltpu.VMEM)
SMEM = pl.BlockSpec(memory_space=pltpu.SMEM)
ANY = pl.BlockSpec(memory_space=pl.ANY)
F32 = jnp.float32
I32 = jnp.int32


def divmod_static(value, size):
    if size & (size - 1) == 0:
        return lax.shift_right_logical(value, size.bit_length() - 1), value & (size - 1)
    whole = lax.div(value, size)
    return whole, value - whole * size


def wrap(value, n):
    return jnp.where(value >= n, value - n, value)


def bit_of(index):
    return lax.shift_left(jnp.int32(1), index)


def bits_set(x):
    x = x - (lax.shift_right_logical(x, 1) & 0x55555555)
    x = (x & 0x33333333) + (lax.shift_right_logical(x, 2) & 0x33333333)
    x = (x + lax.shift_right_logical(x, 4)) & 0x0F0F0F0F
    x = x + lax.shift_right_logical(x, 8)
    x = x + lax.shift_right_logical(x, 16)
    return x & 63


def lowest(mask):
    return bits_set((mask & -mask) - 1) & 31


def predict(raw):
    return 3.0 * raw[0] - 3.0 * raw[1] + raw[2]


def slope(raw, guess):
    return 3.0 * guess - (4.0 * raw[0] - raw[1])


def leave_kernel(n, span, here_ref, new_slot_ref, partner_ref, history_ref, meta_ref, *rest):
    outs, (source, count, raw, sems) = rest[: n - 1], rest[n - 1 :]
    blocks = history_ref.shape[0]
    die = here_ref[0]

    def clear(at, carry):
        meta_ref[at] = jnp.where(at > n, -1, 0)
        return carry

    lax.fori_loop(0, 1 + n + n * CAP, clear, 0)
    for at in range(n):
        count[at] = 0
    for at in range(n * CAP):
        source[at] = -1

    def step(at, stays):
        dest, local = divmod_static(new_slot_ref[at], span)
        local = divmod_static(local, blocks)[1]
        leaving = dest != die

        @pl.when(leaving)
        def _():
            rank = count[dest]
            count[dest] = rank + 1
            meta_ref[1 + n + dest * CAP + rank] = local
            turn = wrap(dest - die + n, n) * CAP + rank
            source[turn] = at
            pltpu.make_async_copy(history_ref.at[at], raw.at[turn], sems.at[turn]).start()

        owner, local_read = divmod_static(partner_ref[at], span)
        local_read = divmod_static(local_read, blocks)[1]
        meta_ref[1 + owner] = meta_ref[1 + owner] | bit_of(local_read)
        return stays | jnp.where(leaving, 0, bit_of(local))

    meta_ref[0] = ~lax.fori_loop(0, blocks, step, jnp.int32(0), unroll=True)
    for turn in range(CAP, n * CAP):

        @pl.when(source[turn] >= 0)
        def _(turn=turn):
            pltpu.make_async_copy(history_ref.at[0], raw.at[turn], sems.at[turn]).wait()
            guess = predict(raw.at[turn])
            outs[turn // CAP - 1][turn % CAP, 0] = guess
            outs[turn // CAP - 1][turn % CAP, 1] = slope(raw.at[turn], guess)


def predict_kernel(span, here_ref, new_slot_ref, history_ref, guess_ref, slope_ref):
    blocks = history_ref.shape[0]
    for at in range(blocks):
        dest, local = divmod_static(new_slot_ref[at], span)
        local = divmod_static(local, blocks)[1]

        @pl.when(dest == here_ref[0])
        def _(at=at, local=local):
            raw = history_ref.at[at]
            guess = predict(raw)
            guess_ref[local] = guess
            slope_ref[local] = slope(raw, guess)


def early_kernel(n, depth, here_ref, mine_ref, *rest):
    metas, guess_ref, outs = rest[: n - 1], rest[n - 1], rest[n:]
    die, moved = here_ref[0], mine_ref[0]
    for j in range(1, n):
        want = metas[j - 1][1 + die] & ~moved
        for slot in range(depth):
            outs[j - 1][slot] = guess_ref[lowest(want)]
            want = want & (want - 1)


def late_kernel(n, depth, rcap, here_ref, mine_ref, *rest):
    metas, rest = rest[: n - 1], rest[n - 1 :]
    arrived, rest = rest[: n - 1], rest[n - 1 :]
    old_guess, old_slope, guess_ref, slope_ref = rest[:4]
    outs = rest[4:]
    die, moved = here_ref[0], mine_ref[0]

    def keep(at, carry):
        guess_ref[at] = old_guess[at]
        slope_ref[at] = old_slope[at]
        return carry

    lax.fori_loop(0, guess_ref.shape[0], keep, 0, unroll=8)
    for k in range(1, n):
        for rank in range(CAP):
            place = metas[k - 1][1 + n + die * CAP + rank]

            @pl.when(place >= 0)
            def _(k=k, rank=rank, place=place):
                guess_ref[place] = arrived[k - 1][rank, 0]
                slope_ref[place] = arrived[k - 1][rank, 1]

    for j in range(1, n):
        want = metas[j - 1][1 + die]
        still = want & ~moved
        for slot in range(depth):
            still = still & (still - 1)
        late = want & moved
        for slot in range(depth, rcap):
            @pl.when(still != 0)
            def _(still=still, slot=slot):
                outs[j - 1][slot - depth] = guess_ref[lowest(still)]

            still = still & (still - 1)
        for slot in range(rcap - 1, depth - 1, -1):

            @pl.when(late != 0)
            def _(late=late, slot=slot):
                outs[j - 1][slot - depth] = guess_ref[lowest(late)]

            late = late & (late - 1)


def where_kernel(n, span, rcap, here_ref, partner_ref, mine_ref, *rest):
    metas, index_ref = rest[: n - 1], rest[n - 1]
    blocks = index_ref.shape[0]
    die = here_ref[0]
    table = rest[n]
    for k in range(1, n):
        table[k] = metas[n - k - 1][0]

    def step(at, carry):
        owner, local = divmod_static(partner_ref[at], span)
        local = divmod_static(local, blocks)[1]
        k = wrap(owner - die + n, n)
        want, moved = mine_ref[1 + owner], table[k]
        bit = bit_of(local)
        below = bit - 1
        early = bits_set(want & ~moved & below)
        late = rcap - 1 - bits_set(want & moved & below)
        slot = jnp.where((moved & bit) != 0, late, early)
        index_ref[at] = jnp.where(k == 0, (n - 1) * rcap + local, (k - 1) * rcap + slot)
        return carry

    table[0] = 0
    lax.fori_loop(0, blocks, step, 0)


def local_kernel(
    guess_ref, slope_ref, coupling_ref, cap_ref, gdev_ref, wire_ref, drive_ref, base_ref, inv_ref
):
    nodes = coupling_ref.shape[1]
    rows = lax.broadcasted_iota(I32, (nodes, nodes), 0)
    cols = lax.broadcasted_iota(I32, (nodes, nodes), 1)
    for at in range(guess_ref.shape[0]):
        guess = guess_ref[at]
        coupling = coupling_ref[at]
        cap = cap_ref[at : at + 1, :]
        gdev = gdev_ref[at : at + 1, :]
        wire = wire_ref[at : at + 1, :]
        through = lax.dot_general(
            guess,
            coupling,
            (((1,), (1,)), ((), ())),
            precision=lax.Precision.HIGHEST,
            preferred_element_type=F32,
        )
        diagonal = jnp.sum(jnp.where(rows == cols, coupling, 0.0), axis=0, keepdims=True)
        tnh = jnp.tanh(guess)
        inv_ref[at] = 1.0 / (1.5 * cap + diagonal + gdev * (1.0 - tnh * tnh) + wire)
        base_ref[at] = (
            0.5 * cap * slope_ref[at] + through + gdev * tnh + wire * guess - drive_ref[at]
        )


def residual_kernel(n, depth, rcap, index_ref, base_ref, inv_ref, guess_ref, wire_ref, gain_ref, *rest):
    early, rest = rest[: n - 1], rest[n - 1 :]
    late, rest = rest[: n - 1], rest[n - 1 :]
    residual_ref, share_ref, partial_ref, pool, sems = rest
    blocks = guess_ref.shape[0]
    copies = [pltpu.make_async_copy(guess_ref, pool.at[pl.ds((n - 1) * rcap, blocks)], sems.at[0])]
    for k in range(1, n):
        low = (k - 1) * rcap
        if depth:
            copies.append(
                pltpu.make_async_copy(early[k - 1], pool.at[pl.ds(low, depth)], sems.at[2 * k - 1])
            )
        copies.append(
            pltpu.make_async_copy(
                late[k - 1], pool.at[pl.ds(low + depth, rcap - depth)], sems.at[2 * k]
            )
        )
    for copy in copies:
        copy.start()
    for copy in copies:
        copy.wait()
    share = jnp.zeros(share_ref.shape, F32)
    for at in range(blocks):
        residual = base_ref[at] - wire_ref[at : at + 1, :] * pool[index_ref[at]]
        residual_ref[at] = residual
        scaled = residual * inv_ref[at]
        partial_ref[at] = guess_ref[at] - scaled
        share = share + gain_ref[at : at + 1, :] * scaled
    share_ref[...] = share


def update_kernel(m, nblk, blk_ref, *rest):
    shares, rest = rest[:m], rest[m:]
    inverses, (partial_ref, inv_ref, gain_ref, updated_ref, whole) = rest[:nblk], rest[nblk:]
    height = inverses[0].shape[0]
    for k in range(nblk):
        at = wrap(blk_ref[0] + k, nblk)
        whole[pl.ds(pl.multiple_of(at * height, height), height), :] = inverses[k][...]
    total = shares[0][...]
    for share in shares[1:]:
        total = total + share[...]
    region = jnp.dot(
        total, whole[...], precision=lax.Precision.HIGHEST, preferred_element_type=F32
    )
    for at in range(partial_ref.shape[0]):
        updated_ref[at] = partial_ref[at] + gain_ref[at : at + 1, :] * inv_ref[at] * region


def call(body, outs, ins, in_specs, out_specs, scratch=(), flops=0, limit=16):
    moved = sum(x.size * 4 for x in ins) + sum(x.size * 4 for x in outs)
    return pl.pallas_call(
        body,
        out_shape=outs,
        in_specs=in_specs,
        out_specs=out_specs,
        scratch_shapes=list(scratch),
        compiler_params=pltpu.CompilerParams(vmem_limit_bytes=limit << 20),
        cost_estimate=pl.CostEstimate(flops=flops, bytes_accessed=moved, transcendentals=0),
    )(*ins)


def turn(x, axes, n, k):
    return lax.ppermute(x, axes, [(d, (d + k) % n) for d in range(n)])


def shards(
    history,
    new_slot,
    partner,
    coupling,
    cap_rate,
    device_gain,
    wire_gain,
    region_gain,
    drive,
    region_inverse,
):
    blocks, _, scen, nodes = history.shape
    n = lax.axis_size("die")
    nblk = lax.axis_size("blk")
    ncol = lax.axis_size("sub") * nblk
    rcap = 2 * max(1, blocks // n)
    depth = max(0, rcap - CAP * (n - 1))
    span = ncol * blocks
    die = lax.axis_index("die")
    blk = lax.axis_index("blk")
    column = lax.axis_index("sub") * nblk + blk
    here = jnp.stack([die, (die * ncol + column) * blocks]).astype(I32)
    block = jax.ShapeDtypeStruct((blocks, scen, nodes), F32)

    inverses = [region_inverse[0]]
    inverses += [turn(region_inverse[0], "blk", nblk, nblk - k) for k in range(1, nblk)]

    pair = jax.ShapeDtypeStruct((CAP, 2, scen, nodes), F32)
    meta, *leaving = call(
        functools.partial(leave_kernel, n, span),
        [jax.ShapeDtypeStruct((META,), I32)] + [pair] * (n - 1),
        [here, new_slot, partner, history],
        [SMEM, SMEM, SMEM, ANY],
        [SMEM] + [VMEM] * (n - 1),
        [
            pltpu.SMEM((n * CAP,), I32),
            pltpu.SMEM((n,), I32),
            pltpu.VMEM((n * CAP, 3, scen, nodes), F32),
            pltpu.SemaphoreType.DMA((n * CAP,)),
        ],
    )
    metas = [turn(meta, "die", n, k) for k in range(1, n)]
    arrived = [turn(leaving[k - 1], "die", n, k) for k in range(1, n)]
    old_guess, old_slope = call(
        functools.partial(predict_kernel, span),
        [block, block],
        [here, new_slot, history],
        [SMEM, SMEM, VMEM],
        [VMEM, VMEM],
    )
    if depth:
        packed = call(
            functools.partial(early_kernel, n, depth),
            [jax.ShapeDtypeStruct((depth, scen, nodes), F32)] * (n - 1),
            [here, meta, *metas, old_guess],
            [SMEM] * (n + 1) + [VMEM],
            [VMEM] * (n - 1),
        )
        early = [turn(packed[k - 1], "die", n, n - k) for k in range(1, n)]
    else:
        early = [old_guess] * (n - 1)
    guess, slopes, *packed = call(
        functools.partial(late_kernel, n, depth, rcap),
        [block, block] + [jax.ShapeDtypeStruct((rcap - depth, scen, nodes), F32)] * (n - 1),
        [here, meta, *metas, *arrived, old_guess, old_slope],
        [SMEM] * (n + 1) + [VMEM] * (n + 1),
        [VMEM] * (n + 1),
    )
    late = [turn(packed[k - 1], "die", n, n - k) for k in range(1, n)]
    (index,) = call(
        functools.partial(where_kernel, n, span, rcap),
        [jax.ShapeDtypeStruct((blocks,), I32)],
        [here, partner, meta, *metas],
        [SMEM] * (n + 2),
        [SMEM],
        [pltpu.SMEM((n,), I32)],
    )
    step = 8 if blocks % 8 == 0 else blocks
    wide = pl.BlockSpec((step, scen, nodes), lambda i: (i, 0, 0))
    flat = pl.BlockSpec((step, nodes), lambda i: (i, 0))
    base, inv = pl.pallas_call(
        local_kernel,
        grid=(blocks // step,),
        out_shape=[block, block],
        in_specs=[
            wide,
            wide,
            pl.BlockSpec((step, nodes, nodes), lambda i: (i, 0, 0)),
            flat,
            flat,
            flat,
            wide,
        ],
        out_specs=[wide, wide],
        compiler_params=pltpu.CompilerParams(vmem_limit_bytes=16 << 20),
        cost_estimate=pl.CostEstimate(
            flops=12 * blocks * scen * nodes * nodes, bytes_accessed=5 << 20, transcendentals=0
        ),
    )(guess, slopes, coupling, cap_rate, device_gain, wire_gain, drive)
    residual, share, partial = call(
        functools.partial(residual_kernel, n, depth, rcap),
        [block, jax.ShapeDtypeStruct((scen, nodes), F32), block],
        [index, base, inv, guess, wire_gain, region_gain, *early, *late],
        [SMEM] + [VMEM] * 5 + [ANY] * (2 * n - 2),
        [VMEM] * 3,
        [
            pltpu.VMEM(((n - 1) * rcap + blocks, scen, nodes), F32),
            pltpu.SemaphoreType.DMA((2 * n,)),
        ],
    )
    shares = [share] + [turn(share, ("sub", "blk"), ncol, k) for k in range(1, ncol)]
    (updated,) = call(
        functools.partial(update_kernel, ncol, nblk),
        [block],
        [blk.reshape(1).astype(I32), *shares, *inverses, partial, inv, region_gain],
        [SMEM] + [VMEM] * (ncol + nblk + 3),
        [VMEM],
        [pltpu.VMEM((nodes, nodes), F32)],
        flops=12 * scen * nodes * nodes,
    )
    return (updated, residual)


def solution(mesh):
    every = ("grp", "die", "sub", "blk")
    in_specs = (
        P(every, None, None, None),
        P(every),
        P(every),
        P(every, None, None),
        P(every, None),
        P(every, None),
        P(every, None),
        P(every, None),
        P(every, None, None),
        P(("grp", "die"), "blk", None),
    )
    out_specs = (P(every, None, None), P(every, None, None))
    return jax.shard_map(shards, mesh=mesh, in_specs=in_specs, out_specs=out_specs, check_vma=False)
```

```python
import functools

import jax
import jax.numpy as jnp
from jax import lax
from jax.experimental import pallas as pl
from jax.experimental.pallas import tpu as pltpu
from jax.sharding import PartitionSpec as P

CAP = 2
META = 128
AHEAD = 4
EARLY = 64 << 20
LATE = 64 << 20
VMEM = pl.BlockSpec(memory_space=pltpu.VMEM)
SMEM = pl.BlockSpec(memory_space=pltpu.SMEM)
ANY = pl.BlockSpec(memory_space=pl.ANY)
HBM = pl.BlockSpec(memory_space=pltpu.HBM)
F32 = jnp.float32
I32 = jnp.int32


def divmod_static(value, size):
    if size & (size - 1) == 0:
        return lax.shift_right_logical(value, size.bit_length() - 1), value & (size - 1)
    whole = lax.div(value, size)
    return whole, value - whole * size


def bit_of(index):
    return lax.shift_left(jnp.int32(1), index)


def bits_set(x):
    x = x - (lax.shift_right_logical(x, 1) & 0x55555555)
    x = (x & 0x33333333) + (lax.shift_right_logical(x, 2) & 0x33333333)
    x = (x + lax.shift_right_logical(x, 4)) & 0x0F0F0F0F
    x = x + lax.shift_right_logical(x, 8)
    x = x + lax.shift_right_logical(x, 16)
    return x & 63


def lowest(mask):
    return bits_set((mask & -mask) - 1) & 31


def predict(raw):
    return 3.0 * raw[0] - 3.0 * raw[1] + raw[2]


def slope(raw, guess):
    return 3.0 * guess - (4.0 * raw[0] - raw[1])


def meta_kernel(n, span, here_ref, new_slot_ref, partner_ref, meta_ref, slots, reads, count, sems):
    blocks = new_slot_ref.shape[0]
    die = here_ref[0]
    copies = [
        pltpu.make_async_copy(new_slot_ref, slots, sems.at[0]),
        pltpu.make_async_copy(partner_ref, reads, sems.at[1]),
    ]
    for copy in copies:
        copy.start()
    for at in range(1 + n + n * CAP):
        meta_ref[at] = -1 if at > n else 0
    for at in range(n):
        count[at] = 0
    for copy in copies:
        copy.wait()

    stays = jnp.int32(0)
    for at in range(blocks):
        dest, local = divmod_static(slots[at], span)
        bit = bit_of(divmod_static(local, blocks)[1])
        leaving = dest != die

        @pl.when(leaving)
        def _(dest=dest, local=local):
            rank = count[dest]
            count[dest] = rank + 1
            meta_ref[1 + n + dest * CAP + rank] = divmod_static(local, blocks)[1]

        stays = stays | jnp.where(leaving, 0, bit)
        owner, local = divmod_static(reads[at], span)
        owner = 1 + owner
        meta_ref[owner] = meta_ref[owner] | bit_of(divmod_static(local, blocks)[1])
    meta_ref[0] = ~stays


def predict_kernel(_, history_ref, guess_ref, slope_ref):
    for at in range(history_ref.shape[0]):
        raw = history_ref.at[at]
        guess = predict(raw)
        guess_ref[at] = guess
        slope_ref[at] = slope(raw, guess)


def place_kernel(n, ahead, span, here_ref, mine_ref, new_slot_ref, old_guess, old_slope, *rest):
    metas, (guess_ref, slope_ref, *rest) = rest[: n - 1], rest[n - 1 :]
    outs, (source, count) = rest[: n - 1], rest[n - 1 :]
    blocks = old_guess.shape[0]
    die = here_ref[0]
    for at in range(n):
        count[at] = 0
    for at in range(n * CAP):
        source[at] = 0
    for at in range(blocks):
        dest, local = divmod_static(new_slot_ref[at], span)
        local = divmod_static(local, blocks)[1]

        @pl.when(dest == die)
        def _(at=at, local=local):
            guess_ref[local] = old_guess[at]
            slope_ref[local] = old_slope[at]

        @pl.when(dest != die)
        def _(at=at, dest=dest):
            rank = count[dest]
            count[dest] = rank + 1
            source[(dest ^ die) * CAP + rank] = at

    for turn in range(CAP, n * CAP):
        outs[turn // CAP - 1][turn % CAP] = old_guess[source[turn]]
        outs[turn // CAP - 1][CAP + turn % CAP] = old_slope[source[turn]]
    for meta, out, some in zip(metas, outs, ahead):
        want = meta[1 + die] & ~mine_ref[0]
        for slot in range(some):
            out[2 * CAP + slot] = guess_ref[lowest(want)]
            want = want & (want - 1)


def early_kernel(n, depth, ahead, here_ref, mine_ref, *rest):
    m = n - 2
    metas, guess_ref, outs = rest[:m], rest[m], rest[m + 1 :]
    die, moved = here_ref[0], mine_ref[0]
    for meta, out in zip(metas, outs):
        want = meta[1 + die] & ~moved
        for slot in range(ahead):
            want = want & (want - 1)
        for slot in range(depth - ahead):
            out[slot] = guess_ref[lowest(want)]
            want = want & (want - 1)


def late_kernel(n, depth, rcap, here_ref, mine_ref, *rest):
    metas, rest = rest[: n - 1], rest[n - 1 :]
    arrived, rest = rest[: n - 1], rest[n - 1 :]
    old_guess, old_slope, _, guess_ref, slope_ref = rest[:5]
    outs = rest[5:]
    die, moved = here_ref[0], mine_ref[0]

    for at in range(guess_ref.shape[0]):
        guess_ref[at] = old_guess[at]
        slope_ref[at] = old_slope[at]
    for k in range(1, n):
        for rank in range(CAP):
            place = metas[k - 1][1 + n + die * CAP + rank]

            @pl.when(place >= 0)
            def _(k=k, rank=rank, place=place):
                guess_ref[place] = arrived[k - 1][rank]
                slope_ref[place] = arrived[k - 1][CAP + rank]

    for meta, out in zip(metas, outs):
        want = meta[1 + die]
        still = want & ~moved
        late = want & moved
        for slot in range(depth):
            still = still & (still - 1)
        for slot in range(rcap - depth):

            @pl.when(still != 0)
            def _(out=out, still=still, slot=slot):
                out[slot] = guess_ref[lowest(still)]

            still = still & (still - 1)
        for slot in range(rcap - depth - 1, -1, -1):

            @pl.when(late != 0)
            def _(out=out, late=late, slot=slot):
                out[slot] = guess_ref[lowest(late)]

            late = late & (late - 1)


def where_kernel(n, span, depth, rcap, here_ref, partner_ref, mine_ref, _, *rest):
    metas, (index_ref, moves) = rest[: n - 1], rest[n - 1 :]
    blocks = index_ref.shape[0]
    die = here_ref[0]
    own = (n - 1) * depth
    moves[0] = 0
    for k in range(1, n):
        moves[k] = metas[k - 1][0]

    def step(at, carry):
        owner, local = divmod_static(partner_ref[at], span)
        local = divmod_static(local, blocks)[1]
        k = owner ^ die
        want, moved = mine_ref[1 + owner], moves[k]
        bit = bit_of(local)
        below = bit - 1
        stays = bits_set(want & ~moved & below)
        late = rcap - 1 - bits_set(want & moved & below)
        slot = jnp.where((moved & bit) != 0, late, stays)
        early = (k - 1) * depth + slot
        late = own + blocks + (k - 1) * (rcap - depth) + slot - depth
        index_ref[at] = jnp.where(k == 0, own + local, jnp.where(slot < depth, early, late))
        return carry

    lax.fori_loop(0, blocks, step, 0)


def local_kernel(
    guess_ref, slope_ref, coupling_ref, cap_ref, gdev_ref, wire_ref, gain_ref, drive_ref, base_ref, inv_ref, scale_ref
):
    nodes = coupling_ref.shape[1]
    rows = lax.broadcasted_iota(I32, (nodes, nodes), 0)
    cols = lax.broadcasted_iota(I32, (nodes, nodes), 1)
    for at in range(guess_ref.shape[0]):
        guess = guess_ref[at]
        coupling = coupling_ref[at]
        cap = cap_ref[at : at + 1, :]
        gdev = gdev_ref[at : at + 1, :]
        wire = wire_ref[at : at + 1, :]
        through = lax.dot_general(
            guess,
            coupling,
            (((1,), (1,)), ((), ())),
            precision=lax.Precision.HIGHEST,
            preferred_element_type=F32,
        )
        diagonal = jnp.sum(jnp.where(rows == cols, coupling, 0.0), axis=0, keepdims=True)
        tnh = jnp.tanh(guess)
        inv = 1.0 / (1.5 * cap + diagonal + gdev * (1.0 - tnh * tnh) + wire)
        inv_ref[at] = inv
        scale_ref[at] = gain_ref[at : at + 1, :] * inv
        base_ref[at] = (
            0.5 * cap * slope_ref[at] + through + gdev * tnh + wire * guess - drive_ref[at]
        )


def gather_kernel(depth, ahead, index_ref, *rest):
    m = len(ahead)
    first, rest = rest[:m], rest[m:]
    early, (guess_ref, _, near_ref, pool) = rest[: max(m - 1, 0)], rest[max(m - 1, 0) :]
    blocks = guess_ref.shape[0]
    for k in range(m):
        for slot in range(depth):
            block = first[k][2 * CAP + slot] if slot < ahead[k] else early[k - 1][slot - ahead[k]]
            pool[k * depth + slot] = block
    for at in range(blocks):
        pool[m * depth + at] = guess_ref[at]
    for at in range(blocks):
        near_ref[at] = pool[jnp.minimum(index_ref[at], m * depth + blocks - 1)]


def residual_kernel(n, nblk, head, index_ref, blk_ref, near_ref, base_ref, inv_ref, scale_ref, guess_ref, wire_ref, *rest):
    late, rest = rest[: n - 1], rest[n - 1 :]
    inverses, (residual_ref, share_ref, partial_ref, whole_ref, pool) = rest[:nblk], rest[nblk:]
    start = 0
    for ref in late:
        for slot in range(ref.shape[0]):
            pool[start + slot] = ref[slot]
        start += ref.shape[0]
    height = inverses[0].shape[0]
    for k in range(nblk):
        whole_ref[pl.ds(pl.multiple_of((blk_ref[0] ^ k) * height, height), height), :] = inverses[k][...]
    share = jnp.zeros(share_ref.shape, F32)
    for at in range(guess_ref.shape[0]):
        index = index_ref[at]
        other = jnp.where(index >= head, pool[jnp.maximum(index - head, 0)], near_ref[at])
        residual = base_ref[at] - wire_ref[at : at + 1, :] * other
        residual_ref[at] = residual
        partial_ref[at] = guess_ref[at] - residual * inv_ref[at]
        share = share + scale_ref[at] * residual
    share_ref[...] = share


def store_kernel(value_ref, out_ref, sem):
    copy = pltpu.make_async_copy(value_ref, out_ref, sem)
    copy.start()
    copy.wait()


def update_kernel(m, parts, *rest):
    shares, (whole_ref, partial_ref, scale_ref, updated_ref, held, sems) = rest[:m], rest[m:]
    total = shares[0][...]
    for share in shares[1:]:
        total = total + share[...]
    region = jnp.dot(
        total, whole_ref[...], precision=lax.Precision.HIGHEST, preferred_element_type=F32
    )
    step = partial_ref.shape[0] // parts
    copies = []
    for part in range(parts):
        for at in range(part * step, (part + 1) * step):
            held[at] = partial_ref[at] + scale_ref[at] * region
        span = pl.ds(part * step, step)
        copies.append(pltpu.make_async_copy(held.at[span], updated_ref.at[span], sems.at[part]))
        copies[-1].start()
    for copy in copies:
        copy.wait()


def call(body, outs, ins, in_specs, out_specs, scratch=(), flops=0, moved=0, limit=8):
    return pl.pallas_call(
        body,
        out_shape=outs,
        in_specs=in_specs,
        out_specs=out_specs,
        scratch_shapes=list(scratch),
        compiler_params=pltpu.CompilerParams(vmem_limit_bytes=limit << 20),
        cost_estimate=pl.CostEstimate(flops=flops, bytes_accessed=moved, transcendentals=0),
    )(*ins)


def swap(x, axes, n, k):
    return lax.ppermute(x, axes, [(d, d ^ k) for d in range(n)])


def shards(
    history,
    new_slot,
    partner,
    coupling,
    cap_rate,
    device_gain,
    wire_gain,
    region_gain,
    drive,
    region_inverse,
):
    blocks, _, scen, nodes = history.shape
    n = lax.axis_size("die")
    nblk = lax.axis_size("blk")
    ncol = lax.axis_size("sub") * nblk
    for size in (n, nblk, ncol):
        assert size & (size - 1) == 0
    assert blocks <= 32
    rcap = 2 * max(1, blocks // n)
    depth = max(0, rcap - CAP * (n - 1))
    some = min(AHEAD, depth)
    ahead = [depth] + [some] * (n - 2)
    span = ncol * blocks
    die = lax.axis_index("die").astype(I32).reshape(1)
    blk = lax.axis_index("blk").astype(I32).reshape(1)
    def tiles(count):
        return jax.ShapeDtypeStruct((count, scen, nodes), F32)

    block = tiles(blocks)
    square = jax.ShapeDtypeStruct((nodes, nodes), F32)

    (meta,) = call(
        functools.partial(meta_kernel, n, span),
        [jax.ShapeDtypeStruct((META,), I32)],
        [
            die,
            pltpu.with_memory_space_constraint(new_slot, pltpu.HBM),
            pltpu.with_memory_space_constraint(partner, pltpu.HBM),
        ],
        [SMEM, HBM, HBM],
        [SMEM],
        [
            pltpu.SMEM((blocks,), I32),
            pltpu.SMEM((blocks,), I32),
            pltpu.SMEM((n,), I32),
            pltpu.SemaphoreType.DMA((2,)),
        ],
    )
    metas = [swap(meta, "die", n, k) for k in range(1, n)]
    step = 8 if blocks % 8 == 0 else blocks
    wide = pl.BlockSpec((step, scen, nodes), lambda i: (i, 0, 0))
    flat = pl.BlockSpec((step, nodes), lambda i: (i, 0))
    raw_guess, raw_slope = pl.pallas_call(
        predict_kernel,
        grid=(blocks // step,),
        out_shape=[block, block],
        in_specs=[ANY, pl.BlockSpec((step, 3, scen, nodes), lambda i: (i, 0, 0, 0))],
        out_specs=[wide, wide],
        compiler_params=pltpu.CompilerParams(vmem_limit_bytes=8 << 20),
        cost_estimate=pl.CostEstimate(flops=0, bytes_accessed=0, transcendentals=0),
    )(meta, pltpu.with_memory_space_constraint(history, pltpu.HBM))
    old_guess, old_slope, *leaving = call(
        functools.partial(place_kernel, n, ahead, span),
        [block, block] + [tiles(2 * CAP + some) for some in ahead],
        [die, meta, new_slot, raw_guess, raw_slope, *metas],
        [SMEM] * 3 + [VMEM] * 2 + [SMEM] * (n - 1),
        [VMEM] * (n + 1),
        [pltpu.SMEM((n * CAP,), I32), pltpu.SMEM((n,), I32)],
    )
    arrived = [swap(leaving[k - 1], "die", n, k) for k in range(1, n)]
    early, order = [], old_guess
    if depth:
        packed = call(
            functools.partial(early_kernel, n, depth, some),
            [tiles(depth - some)] * (n - 2),
            [die, meta, *metas[1:], old_guess],
            [SMEM] * n + [VMEM],
            [VMEM] * (n - 2),
            moved=EARLY,
        )
        order = packed[0]
        early = [swap(packed[k - 2], "die", n, k) for k in range(2, n)]
    guess, slopes, *packed = call(
        functools.partial(late_kernel, n, depth, rcap),
        [block, block] + [tiles(rcap - depth)] * (n - 1),
        [die, meta, *metas, *arrived, old_guess, old_slope, order],
        [SMEM] * (n + 1) + [VMEM] * (n + 1) + [ANY],
        [VMEM] * (n + 1),
        moved=LATE,
    )
    late = [swap(packed[k - 1], "die", n, k) for k in range(1, n)]
    (index,) = call(
        functools.partial(where_kernel, n, span, depth, rcap),
        [jax.ShapeDtypeStruct((blocks,), I32)],
        [die, partner, meta, guess, *metas],
        [SMEM] * 3 + [ANY] + [SMEM] * (n - 1),
        [SMEM],
        [pltpu.SMEM((n,), I32)],
    )
    base, inv, scale = pl.pallas_call(
        local_kernel,
        grid=(blocks // step,),
        out_shape=[block, block, block],
        in_specs=[
            wide,
            wide,
            pl.BlockSpec((step, nodes, nodes), lambda i: (i, 0, 0)),
            flat,
            flat,
            flat,
            flat,
            wide,
        ],
        out_specs=[wide, wide, wide],
        compiler_params=pltpu.CompilerParams(vmem_limit_bytes=8 << 20),
        cost_estimate=pl.CostEstimate(
            flops=0, bytes_accessed=0, transcendentals=0
        ),
    )(guess, slopes, coupling, cap_rate, device_gain, wire_gain, region_gain, drive)
    head = (n - 1) * depth + blocks
    (near,) = call(
        functools.partial(gather_kernel, depth, ahead if depth else []),
        [block],
        [index, *(arrived + early if depth else []), guess, base],
        [SMEM] + [VMEM] * (2 * n - 2 if depth else 1) + [ANY],
        [VMEM],
        [pltpu.VMEM((head, scen, nodes), F32)],
    )
    inverses = [region_inverse[0]]
    inverses += [swap(region_inverse[0], "blk", nblk, k) for k in range(1, nblk)]
    residual, share, partial, whole = call(
        functools.partial(residual_kernel, n, nblk, head),
        [block, jax.ShapeDtypeStruct((scen, nodes), F32), block, square],
        [index, blk, near, base, inv, scale, guess, wire_gain, *late, *inverses],
        [SMEM] * 2 + [VMEM] * (6 + n - 1 + nblk),
        [VMEM] * 4,
        [pltpu.VMEM((sum(x.shape[0] for x in late), scen, nodes), F32)],
    )
    (stored,) = call(
        store_kernel, [block], [residual], [ANY], [HBM], [pltpu.SemaphoreType.DMA]
    )
    shares = [share] + [swap(share, ("sub", "blk"), ncol, k) for k in range(1, ncol)]
    parts = 4 if blocks % 4 == 0 else 1
    (updated,) = call(
        functools.partial(update_kernel, ncol, parts),
        [block],
        [*shares, whole, partial, scale],
        [VMEM] * (ncol + 3),
        [HBM],
        [pltpu.VMEM((blocks, scen, nodes), F32), pltpu.SemaphoreType.DMA((parts,))],
        flops=12 * scen * nodes * nodes,
    )
    return (updated, stored)


def solution(mesh):
    every = ("grp", "die", "sub", "blk")
    in_specs = (
        P(every, None, None, None),
        P(every),
        P(every),
        P(every, None, None),
        P(every, None),
        P(every, None),
        P(every, None),
        P(every, None),
        P(every, None, None),
        P(("grp", "die"), "blk", None),
    )
    out_specs = (P(every, None, None), P(every, None, None))
    return jax.shard_map(shards, mesh=mesh, in_specs=in_specs, out_specs=out_specs, check_vma=False)
```

```python
import functools

import jax
import jax.numpy as jnp
from jax import lax
from jax.experimental import pallas as pl
from jax.experimental.pallas import tpu as pltpu
from jax.sharding import PartitionSpec as P

CAP = 2
VMEM = pl.BlockSpec(memory_space=pltpu.VMEM)
SMEM = pl.BlockSpec(memory_space=pltpu.SMEM)
ANY = pl.BlockSpec(memory_space=pl.ANY)
HBM = pl.BlockSpec(memory_space=pltpu.HBM)
F32 = jnp.float32
I32 = jnp.int32


def divmod_static(value, size):
    if size & (size - 1) == 0:
        return lax.shift_right_logical(value, size.bit_length() - 1), value & (size - 1)
    whole = lax.div(value, size)
    return whole, value - whole * size


def bit_of(index):
    return lax.shift_left(jnp.int32(1), index)


def bits_set(x):
    x = x - (lax.shift_right_logical(x, 1) & 0x55555555)
    x = (x & 0x33333333) + (lax.shift_right_logical(x, 2) & 0x33333333)
    x = (x + lax.shift_right_logical(x, 4)) & 0x0F0F0F0F
    x = x + lax.shift_right_logical(x, 8)
    x = x + lax.shift_right_logical(x, 16)
    return x & 63


def lowest(mask):
    return bits_set((mask & -mask) - 1) & 31


def halves(mask):
    return [mask & 0xFFFF, lax.shift_right_logical(mask, 16)]


def joined(low, high):
    return low | lax.shift_left(high, 16)


def predict(raw):
    return 3.0 * raw[0] - 3.0 * raw[1] + raw[2]


def slope(raw, guess):
    return 3.0 * guess - (4.0 * raw[0] - raw[1])


def leave_kernel(
    n, span, here_ref, new_slot_ref, partner_ref, history_ref, rows_ref,
    slots, reads, mine_ref, raw_ref, inverse_ref, *rest
):
    outs, (source, place, count, sems) = rest[: n - 1], rest[n - 1 :]
    blocks, _, scen, nodes = history_ref.shape
    die = here_ref[0]
    copies = [
        pltpu.make_async_copy(new_slot_ref, slots, sems.at[0]),
        pltpu.make_async_copy(partner_ref, reads, sems.at[1]),
        pltpu.make_async_copy(history_ref, raw_ref, sems.at[2]),
        pltpu.make_async_copy(rows_ref, inverse_ref, sems.at[3]),
    ]
    for copy in copies:
        copy.start()
    for at in range(n):
        mine_ref[at] = 0
        count[at] = 0
    for at in range(n * CAP):
        source[at] = 0
        place[at] = -1
    copies[0].wait()
    copies[1].wait()

    for at in range(blocks):
        dest, local = divmod_static(slots[at], span)
        local = divmod_static(local, blocks)[1]

        @pl.when(dest != die)
        def _(at=at, dest=dest, local=local):
            rank = count[dest]
            count[dest] = rank + 1
            turn = (dest ^ die) * CAP + rank
            source[turn] = at
            place[turn] = local

        owner, local = divmod_static(reads[at], span)
        mine_ref[owner] = mine_ref[owner] | bit_of(divmod_static(local, blocks)[1])
    copies[2].wait()
    lane = lax.broadcasted_iota(I32, (8, nodes), 1)
    for k in range(1, n):
        out = outs[k - 1]
        for rank in range(CAP):
            raw = raw_ref.at[source[k * CAP + rank]]
            guess = predict(raw)
            out[pl.ds(rank * scen, scen), :] = guess
            out[pl.ds((CAP + rank) * scen, scen), :] = slope(raw, guess)
        row = jnp.zeros((8, nodes), I32)
        values = halves(mine_ref[die ^ k])
        values += [place[k * CAP + rank] for rank in range(CAP)]
        for j, value in enumerate(values):
            row = jnp.where(lane == j, value, row)
        out[pl.ds(2 * CAP * scen, 8), :] = row.astype(F32)
    copies[3].wait()


def place_kernel(span, here_ref, slots, raw_ref, guess_ref, slope_ref):
    blocks = raw_ref.shape[0]
    for at in range(blocks):
        dest, local = divmod_static(slots[at], span)
        local = divmod_static(local, blocks)[1]

        @pl.when(dest == here_ref[0])
        def _(at=at, local=local):
            raw = raw_ref.at[at]
            guess = predict(raw)
            guess_ref[local] = guess
            slope_ref[local] = slope(raw, guess)


def serve_kernel(n, rcap, nblk, blk_ref, *rest):
    arrived, rest = rest[: n - 1], rest[n - 1 :]
    inverses, rest = rest[:nblk], rest[nblk:]
    old_guess, old_slope, guess_ref, slope_ref, whole_ref, *rest = rest
    outs, (ints, meta, sem) = rest[: n - 1], rest[n - 1 :]
    blocks, scen, nodes = guess_ref.shape
    for k in range(1, n):
        ints[k - 1] = arrived[k - 1][pl.ds(2 * CAP * scen, 8), :].astype(I32)
    copy = pltpu.make_async_copy(ints, meta, sem)
    copy.start()
    for at in range(blocks):
        guess_ref[at] = old_guess[at]
        slope_ref[at] = old_slope[at]
    height = inverses[0].shape[0]
    for k in range(nblk):
        at = pl.multiple_of((blk_ref[0] ^ k) * height, height)
        whole_ref[pl.ds(at, height), :] = inverses[k][...]
    copy.wait()
    for k in range(1, n):
        for rank in range(CAP):
            place = meta[k - 1, 0, 2 + rank]

            @pl.when(place >= 0)
            def _(k=k, rank=rank, place=place):
                guess_ref[place] = arrived[k - 1][pl.ds(rank * scen, scen), :]
                slope_ref[place] = arrived[k - 1][pl.ds((CAP + rank) * scen, scen), :]

    for k in range(1, n):
        want = joined(meta[k - 1, 0, 0], meta[k - 1, 0, 1])
        for slot in range(rcap):
            outs[k - 1][slot] = guess_ref[lowest(want)]
            want = want & (want - 1)


def where_kernel(n, span, rcap, here_ref, reads, mine_ref, _, index_ref):
    blocks = index_ref.shape[0]
    die = here_ref[0]

    def step(at, carry):
        owner, local = divmod_static(reads[at], span)
        local = divmod_static(local, blocks)[1]
        k = owner ^ die
        slot = bits_set(mine_ref[owner] & (bit_of(local) - 1))
        index_ref[at] = jnp.where(k == 0, local - blocks, (k - 1) * rcap + slot)
        return carry

    lax.fori_loop(0, blocks, step, 0)


def local_kernel(
    guess_ref, slope_ref, coupling_ref, cap_ref, gdev_ref, wire_ref, gain_ref, drive_ref,
    base_ref, inv_ref, scale_ref, kept_ref
):
    nodes = coupling_ref.shape[1]
    rows = lax.broadcasted_iota(I32, (nodes, nodes), 0)
    cols = lax.broadcasted_iota(I32, (nodes, nodes), 1)
    for at in range(guess_ref.shape[0]):
        guess = guess_ref[at]
        coupling = coupling_ref[at]
        cap = cap_ref[at : at + 1, :]
        gdev = gdev_ref[at : at + 1, :]
        wire = wire_ref[at : at + 1, :]
        through = lax.dot_general(
            guess,
            coupling,
            (((1,), (1,)), ((), ())),
            precision=lax.Precision.HIGHEST,
            preferred_element_type=F32,
        )
        diagonal = jnp.sum(jnp.where(rows == cols, coupling, 0.0), axis=0, keepdims=True)
        tnh = jnp.tanh(guess)
        inv = 1.0 / (1.5 * cap + diagonal + gdev * (1.0 - tnh * tnh) + wire)
        inv_ref[at] = inv
        kept_ref[at : at + 1, :] = wire
        scale_ref[at] = gain_ref[at : at + 1, :] * inv
        base_ref[at] = (
            0.5 * cap * slope_ref[at] + through + gdev * tnh + wire * guess - drive_ref[at]
        )


def residual_kernel(n, index_ref, base_ref, inv_ref, scale_ref, guess_ref, wire_ref, *rest):
    blocks_in, (residual_ref, share_ref, partial_ref, pool) = rest[: n - 1], rest[n - 1 :]
    blocks = guess_ref.shape[0]
    start = 0
    for ref in blocks_in:
        for slot in range(ref.shape[0]):
            pool[start + slot] = ref[slot]
        start += ref.shape[0]
    share = jnp.zeros(share_ref.shape, F32)
    for at in range(blocks):
        index = index_ref[at]
        own = index < 0
        near = guess_ref[jnp.where(own, index + blocks, 0)]
        other = jnp.where(own, near, pool[jnp.maximum(index, 0)])
        residual = base_ref[at] - wire_ref[at : at + 1, :] * other
        residual_ref[at] = residual
        partial_ref[at] = guess_ref[at] - residual * inv_ref[at]
        share = share + scale_ref[at] * residual
    share_ref[...] = share


def store_kernel(value_ref, out_ref, sem):
    copy = pltpu.make_async_copy(value_ref, out_ref, sem)
    copy.start()
    copy.wait()


def update_kernel(m, parts, *rest):
    shares, (whole_ref, partial_ref, scale_ref, updated_ref, held, sems) = rest[:m], rest[m:]
    total = shares[0][...]
    for share in shares[1:]:
        total = total + share[...]
    region = jnp.dot(
        total, whole_ref[...], precision=lax.Precision.HIGHEST, preferred_element_type=F32
    )
    step = partial_ref.shape[0] // parts
    copies = []
    for part in range(parts):
        for at in range(part * step, (part + 1) * step):
            held[at] = partial_ref[at] + scale_ref[at] * region
        span = pl.ds(part * step, step)
        copies.append(pltpu.make_async_copy(held.at[span], updated_ref.at[span], sems.at[part]))
        copies[-1].start()
    for copy in copies:
        copy.wait()


def call(body, outs, ins, in_specs, out_specs, scratch=(), limit=8):
    return pl.pallas_call(
        body,
        out_shape=outs,
        in_specs=in_specs,
        out_specs=out_specs,
        scratch_shapes=list(scratch),
        compiler_params=pltpu.CompilerParams(vmem_limit_bytes=limit << 20),
        cost_estimate=pl.CostEstimate(flops=0, bytes_accessed=0, transcendentals=0),
    )(*ins)


def in_hbm(x):
    return pltpu.with_memory_space_constraint(x, pltpu.HBM)


def swap(x, axes, n, k):
    return lax.ppermute(x, axes, [(d, d ^ k) for d in range(n)])


def shards(
    history,
    new_slot,
    partner,
    coupling,
    cap_rate,
    device_gain,
    wire_gain,
    region_gain,
    drive,
    region_inverse,
):
    blocks, _, scen, nodes = history.shape
    n = lax.axis_size("die")
    nblk = lax.axis_size("blk")
    ncol = lax.axis_size("sub") * nblk
    for size in (n, nblk, ncol):
        assert size & (size - 1) == 0
    assert blocks <= 32
    rcap = 2 * max(1, blocks // n)
    span = ncol * blocks
    die = lax.axis_index("die").astype(I32).reshape(1)
    blk = lax.axis_index("blk").astype(I32).reshape(1)

    def tiles(count):
        return jax.ShapeDtypeStruct((count, scen, nodes), F32)

    def ints(count):
        return jax.ShapeDtypeStruct((count,), I32)

    block = tiles(blocks)
    square = jax.ShapeDtypeStruct((nodes, nodes), F32)
    rows = region_inverse[0]
    message = jax.ShapeDtypeStruct((2 * CAP * scen + 8, nodes), F32)

    slots, reads, mine, raw, rows, *leaving = call(
        functools.partial(leave_kernel, n, span),
        [
            ints(blocks),
            ints(blocks),
            ints(n),
            jax.ShapeDtypeStruct(history.shape, F32),
            jax.ShapeDtypeStruct(rows.shape, F32),
        ]
        + [message] * (n - 1),
        [die, in_hbm(new_slot), in_hbm(partner), in_hbm(history), in_hbm(rows)],
        [SMEM] + [HBM] * 4,
        [SMEM] * 3 + [VMEM] * (n + 1),
        [pltpu.SMEM((n * CAP,), I32)] * 2
        + [pltpu.SMEM((n,), I32), pltpu.SemaphoreType.DMA((4,))],
    )
    arrived = [swap(leaving[k - 1], "die", n, k) for k in range(1, n)]
    inverses = [rows] + [swap(rows, "blk", nblk, k) for k in range(1, nblk)]
    old_guess, old_slope = call(
        functools.partial(place_kernel, span),
        [block, block],
        [die, slots, raw],
        [SMEM, SMEM, VMEM],
        [VMEM, VMEM],
    )
    guess, slopes, whole, *served = call(
        functools.partial(serve_kernel, n, rcap, nblk),
        [block, block, square] + [tiles(rcap)] * (n - 1),
        [blk, *arrived, *inverses, old_guess, old_slope],
        [SMEM] + [VMEM] * (n - 1 + nblk + 2),
        [VMEM] * (n + 2),
        [
            pltpu.VMEM((n - 1, 8, nodes), I32),
            pltpu.SMEM((n - 1, 8, nodes), I32),
            pltpu.SemaphoreType.DMA,
        ],
    )
    others = [swap(served[k - 1], "die", n, k) for k in range(1, n)]
    (index,) = call(
        functools.partial(where_kernel, n, span, rcap),
        [ints(blocks)],
        [die, reads, mine, guess],
        [SMEM] * 3 + [ANY],
        [SMEM],
    )
    step = 8 if blocks % 8 == 0 else blocks
    wide = pl.BlockSpec((step, scen, nodes), lambda i: (i, 0, 0))
    flat = pl.BlockSpec((step, nodes), lambda i: (i, 0))
    base, inv, scale, wire = pl.pallas_call(
        local_kernel,
        grid=(blocks // step,),
        out_shape=[block, block, block, jax.ShapeDtypeStruct((blocks, nodes), F32)],
        in_specs=[
            wide,
            wide,
            pl.BlockSpec((step, nodes, nodes), lambda i: (i, 0, 0)),
            flat,
            flat,
            flat,
            flat,
            wide,
        ],
        out_specs=[wide, wide, wide, flat],
        compiler_params=pltpu.CompilerParams(vmem_limit_bytes=8 << 20),
        cost_estimate=pl.CostEstimate(flops=0, bytes_accessed=0, transcendentals=0),
    )(
        guess,
        slopes,
        in_hbm(coupling),
        in_hbm(cap_rate),
        in_hbm(device_gain),
        in_hbm(wire_gain),
        in_hbm(region_gain),
        in_hbm(drive),
    )
    residual, share, partial = call(
        functools.partial(residual_kernel, n),
        [block, jax.ShapeDtypeStruct((scen, nodes), F32), block],
        [index, base, inv, scale, guess, wire, *others],
        [SMEM] + [VMEM] * (5 + n - 1),
        [VMEM] * 3,
        [pltpu.VMEM(((n - 1) * rcap, scen, nodes), F32)],
    )
    (stored,) = call(
        store_kernel, [block], [residual], [ANY], [HBM], [pltpu.SemaphoreType.DMA]
    )
    shares = [share] + [swap(share, ("sub", "blk"), ncol, k) for k in range(1, ncol)]
    parts = 4 if blocks % 4 == 0 else 1
    (updated,) = call(
        functools.partial(update_kernel, ncol, parts),
        [block],
        [*shares, whole, partial, scale],
        [VMEM] * (ncol + 3),
        [HBM],
        [pltpu.VMEM((blocks, scen, nodes), F32), pltpu.SemaphoreType.DMA((parts,))],
    )
    return (updated, stored)


def solution(mesh):
    every = ("grp", "die", "sub", "blk")
    in_specs = (
        P(every, None, None, None),
        P(every),
        P(every),
        P(every, None, None),
        P(every, None),
        P(every, None),
        P(every, None),
        P(every, None),
        P(every, None, None),
        P(("grp", "die"), "blk", None),
    )
    out_specs = (P(every, None, None), P(every, None, None))
    return jax.shard_map(shards, mesh=mesh, in_specs=in_specs, out_specs=out_specs, check_vma=False)
```

```python
import functools

import jax
import jax.numpy as jnp
from jax import lax
from jax.experimental import pallas as pl
from jax.experimental.pallas import tpu as pltpu
from jax.sharding import PartitionSpec as P

CAP = 2
VMEM = pl.BlockSpec(memory_space=pltpu.VMEM)
SMEM = pl.BlockSpec(memory_space=pltpu.SMEM)
ANY = pl.BlockSpec(memory_space=pl.ANY)
HBM = pl.BlockSpec(memory_space=pltpu.HBM)
F32 = jnp.float32
I32 = jnp.int32


def divmod_static(value, size):
    if size & (size - 1) == 0:
        return lax.shift_right_logical(value, size.bit_length() - 1), value & (size - 1)
    whole = lax.div(value, size)
    return whole, value - whole * size


def bit_of(index):
    return lax.shift_left(jnp.int32(1), index)


def bits_set(x):
    x = x - (lax.shift_right_logical(x, 1) & 0x55555555)
    x = (x & 0x33333333) + (lax.shift_right_logical(x, 2) & 0x33333333)
    x = (x + lax.shift_right_logical(x, 4)) & 0x0F0F0F0F
    x = x + lax.shift_right_logical(x, 8)
    x = x + lax.shift_right_logical(x, 16)
    return x & 63


def lowest(mask):
    return bits_set((mask & -mask) - 1) & 31


def halves(mask):
    return [mask & 0xFFFF, lax.shift_right_logical(mask, 16)]


def joined(low, high):
    return low | lax.shift_left(high, 16)


def predict(raw):
    return 3.0 * raw[0] - 3.0 * raw[1] + raw[2]


def slope(raw, guess):
    return 3.0 * guess - (4.0 * raw[0] - raw[1])


def leave_kernel(
    n, span, here_ref, new_slot_ref, partner_ref, history_ref, rows_ref,
    slots, reads, mine_ref, raw_ref, inverse_ref, *rest
):
    outs, (source, place, count, sems) = rest[: n - 1], rest[n - 1 :]
    blocks, _, scen, nodes = history_ref.shape
    die = here_ref[0]
    copies = [
        pltpu.make_async_copy(new_slot_ref, slots, sems.at[0]),
        pltpu.make_async_copy(partner_ref, reads, sems.at[1]),
        pltpu.make_async_copy(history_ref, raw_ref, sems.at[2]),
        pltpu.make_async_copy(rows_ref, inverse_ref, sems.at[3]),
    ]
    for copy in copies:
        copy.start()
    for at in range(n):
        count[at] = 0
    for at in range(n * CAP):
        source[at] = 0
        place[at] = -1
    copies[0].wait()
    copies[1].wait()

    wants = [jnp.int32(0)] * n
    for at in range(n):
        mine_ref[at] = 0
    for at in range(blocks):
        dest, local = divmod_static(slots[at], span)
        local = divmod_static(local, blocks)[1]

        @pl.when(dest != die)
        def _(at=at, dest=dest, local=local):
            rank = count[dest]
            count[dest] = rank + 1
            turn = (dest ^ die) * CAP + rank
            source[turn] = at
            place[turn] = local

        owner, local = divmod_static(reads[at], span)
        bit = bit_of(divmod_static(local, blocks)[1])
        for other in range(n if n <= 8 else 0):
            wants[other] = wants[other] | jnp.where(owner == other, bit, 0)
        if n > 8:
            mine_ref[owner] = mine_ref[owner] | bit
    if n <= 8:
        for at in range(n):
            mine_ref[at] = wants[at]
    copies[2].wait()
    lane = lax.broadcasted_iota(I32, (8, nodes), 1)
    for k in range(1, n):
        out = outs[k - 1]
        for rank in range(CAP):
            raw = raw_ref.at[source[k * CAP + rank]]
            guess = predict(raw)
            out[pl.ds(rank * scen, scen), :] = guess
            out[pl.ds((CAP + rank) * scen, scen), :] = slope(raw, guess)
        row = jnp.zeros((8, nodes), I32)
        values = halves(mine_ref[die ^ k])
        values += [place[k * CAP + rank] for rank in range(CAP)]
        for j, value in enumerate(values):
            row = jnp.where(lane == j, value, row)
        out[pl.ds(2 * CAP * scen, 8), :] = row.astype(F32)
    copies[3].wait()


def place_kernel(span, here_ref, slots, raw_ref, guess_ref, slope_ref):
    blocks = raw_ref.shape[0]
    for at in range(blocks):
        dest, local = divmod_static(slots[at], span)
        local = divmod_static(local, blocks)[1]

        @pl.when(dest == here_ref[0])
        def _(at=at, local=local):
            raw = raw_ref.at[at]
            guess = predict(raw)
            guess_ref[local] = guess
            slope_ref[local] = slope(raw, guess)


def serve_kernel(rounds, rcap, nblk, blk_ref, *rest):
    n = len(rounds) + 1
    arrived, rest = rest[: n - 1], rest[n - 1 :]
    inverses, rest = rest[:nblk], rest[nblk:]
    old_guess, old_slope, guess_ref, slope_ref, whole_ref, *rest = rest
    outs, (ints, meta, sem) = rest[: n - 1], rest[n - 1 :]
    blocks, scen, nodes = guess_ref.shape
    for k in range(1, n):
        ints[k - 1] = arrived[k - 1][pl.ds(2 * CAP * scen, 8), :].astype(I32)
    copy = pltpu.make_async_copy(ints, meta, sem)
    copy.start()
    for at in range(blocks):
        guess_ref[at] = old_guess[at]
        slope_ref[at] = old_slope[at]
    height = inverses[0].shape[0]
    for k in range(nblk):
        at = pl.multiple_of((blk_ref[0] ^ k) * height, height)
        whole_ref[pl.ds(at, height), :] = inverses[k][...]
    copy.wait()
    for k in range(1, n):
        for rank in range(CAP):
            place = meta[k - 1, 0, 2 + rank]

            @pl.when(place >= 0)
            def _(k=k, rank=rank, place=place):
                guess_ref[place] = arrived[k - 1][pl.ds(rank * scen, scen), :]
                slope_ref[place] = arrived[k - 1][pl.ds((CAP + rank) * scen, scen), :]

    for k, out in zip(rounds, outs):
        want = joined(meta[k - 1, 0, 0], meta[k - 1, 0, 1])
        for slot in range(rcap):
            out[slot] = guess_ref[lowest(want)]
            want = want & (want - 1)


def where_kernel(rounds, span, rcap, here_ref, reads, mine_ref, _, index_ref, starts):
    blocks = index_ref.shape[0]
    die = here_ref[0]
    starts[0] = 0
    for at, k in enumerate(rounds):
        starts[k] = at * rcap

    def step(at, carry):
        owner, local = divmod_static(reads[at], span)
        local = divmod_static(local, blocks)[1]
        k = owner ^ die
        slot = bits_set(mine_ref[owner] & (bit_of(local) - 1))
        index_ref[at] = jnp.where(k == 0, local - blocks, starts[k] + slot)
        return carry

    lax.fori_loop(0, blocks, step, 0)


def local_kernel(
    guess_ref, slope_ref, coupling_ref, cap_ref, gdev_ref, wire_ref, gain_ref, drive_ref,
    base_ref, inv_ref, scale_ref, kept_ref
):
    nodes = coupling_ref.shape[1]
    rows = lax.broadcasted_iota(I32, (nodes, nodes), 0)
    cols = lax.broadcasted_iota(I32, (nodes, nodes), 1)
    for at in range(guess_ref.shape[0]):
        guess = guess_ref[at]
        coupling = coupling_ref[at]
        cap = cap_ref[at : at + 1, :]
        gdev = gdev_ref[at : at + 1, :]
        wire = wire_ref[at : at + 1, :]
        through = lax.dot_general(
            guess,
            coupling,
            (((1,), (1,)), ((), ())),
            precision=lax.Precision.HIGHEST,
            preferred_element_type=F32,
        )
        diagonal = jnp.sum(jnp.where(rows == cols, coupling, 0.0), axis=0, keepdims=True)
        tnh = jnp.tanh(guess)
        inv = 1.0 / (1.5 * cap + diagonal + gdev * (1.0 - tnh * tnh) + wire)
        inv_ref[at] = inv
        kept_ref[at : at + 1, :] = wire
        scale_ref[at] = gain_ref[at : at + 1, :] * inv
        base_ref[at] = (
            0.5 * cap * slope_ref[at] + through + gdev * tnh + wire * guess - drive_ref[at]
        )


def residual_kernel(n, index_ref, base_ref, inv_ref, scale_ref, guess_ref, wire_ref, *rest):
    blocks_in, (residual_ref, share_ref, partial_ref, pool) = rest[: n - 1], rest[n - 1 :]
    blocks = guess_ref.shape[0]
    start = 0
    for ref in blocks_in:
        for slot in range(ref.shape[0]):
            pool[start + slot] = ref[slot]
        start += ref.shape[0]
    share = jnp.zeros(share_ref.shape, F32)
    for at in range(blocks):
        index = index_ref[at]
        own = index < 0
        near = guess_ref[jnp.where(own, index + blocks, 0)]
        other = jnp.where(own, near, pool[jnp.maximum(index, 0)])
        residual = base_ref[at] - wire_ref[at : at + 1, :] * other
        residual_ref[at] = residual
        partial_ref[at] = guess_ref[at] - residual * inv_ref[at]
        share = share + scale_ref[at] * residual
    share_ref[...] = share


def store_kernel(value_ref, out_ref, sem):
    copy = pltpu.make_async_copy(value_ref, out_ref, sem)
    copy.start()
    copy.wait()


def update_kernel(m, parts, *rest):
    shares, (whole_ref, partial_ref, scale_ref, updated_ref, held, sems) = rest[:m], rest[m:]
    total = shares[0][...]
    for share in shares[1:]:
        total = total + share[...]
    region = jnp.dot(
        total, whole_ref[...], precision=lax.Precision.HIGHEST, preferred_element_type=F32
    )
    step = partial_ref.shape[0] // parts
    copies = []
    for part in range(parts):
        for at in range(part * step, (part + 1) * step):
            held[at] = partial_ref[at] + scale_ref[at] * region
        span = pl.ds(part * step, step)
        copies.append(pltpu.make_async_copy(held.at[span], updated_ref.at[span], sems.at[part]))
        copies[-1].start()
    for copy in copies:
        copy.wait()


def call(body, outs, ins, in_specs, out_specs, scratch=(), limit=8):
    return pl.pallas_call(
        body,
        out_shape=outs,
        in_specs=in_specs,
        out_specs=out_specs,
        scratch_shapes=list(scratch),
        compiler_params=pltpu.CompilerParams(vmem_limit_bytes=limit << 20),
        cost_estimate=pl.CostEstimate(flops=0, bytes_accessed=0, transcendentals=0),
    )(*ins)


def in_hbm(x):
    return pltpu.with_memory_space_constraint(x, pltpu.HBM)


def swap(x, axes, n, k):
    return lax.ppermute(x, axes, [(d, d ^ k) for d in range(n)])


def shards(
    history,
    new_slot,
    partner,
    coupling,
    cap_rate,
    device_gain,
    wire_gain,
    region_gain,
    drive,
    region_inverse,
):
    blocks, _, scen, nodes = history.shape
    n = lax.axis_size("die")
    nblk = lax.axis_size("blk")
    ncol = lax.axis_size("sub") * nblk
    for size in (n, nblk, ncol):
        assert size & (size - 1) == 0
    assert blocks <= 32
    rcap = 2 * max(1, blocks // n)
    span = ncol * blocks
    die = lax.axis_index("die").astype(I32).reshape(1)
    blk = lax.axis_index("blk").astype(I32).reshape(1)

    def tiles(count):
        return jax.ShapeDtypeStruct((count, scen, nodes), F32)

    def ints(count):
        return jax.ShapeDtypeStruct((count,), I32)

    block = tiles(blocks)
    square = jax.ShapeDtypeStruct((nodes, nodes), F32)
    rows = region_inverse[0]
    message = jax.ShapeDtypeStruct((2 * CAP * scen + 8, nodes), F32)

    slots, reads, mine, raw, rows, *leaving = call(
        functools.partial(leave_kernel, n, span),
        [
            ints(blocks),
            ints(blocks),
            ints(n),
            jax.ShapeDtypeStruct(history.shape, F32),
            jax.ShapeDtypeStruct(rows.shape, F32),
        ]
        + [message] * (n - 1),
        [die, in_hbm(new_slot), in_hbm(partner), in_hbm(history), in_hbm(rows)],
        [SMEM] + [HBM] * 4,
        [SMEM] * 3 + [VMEM] * (n + 1),
        [pltpu.SMEM((n * CAP,), I32)] * 2
        + [pltpu.SMEM((n,), I32), pltpu.SemaphoreType.DMA((4,))],
    )
    arrived = [swap(leaving[k - 1], "die", n, k) for k in range(1, n)]
    inverses = [rows] + [swap(rows, "blk", nblk, k) for k in range(1, nblk)]
    old_guess, old_slope = call(
        functools.partial(place_kernel, span),
        [block, block],
        [die, slots, raw],
        [SMEM, SMEM, VMEM],
        [VMEM, VMEM],
    )
    rounds = [*range(2, n), 1]
    guess, slopes, whole, *served = call(
        functools.partial(serve_kernel, rounds, rcap, nblk),
        [block, block, square] + [tiles(rcap)] * (n - 1),
        [blk, *arrived, *inverses, old_guess, old_slope],
        [SMEM] + [VMEM] * (n - 1 + nblk + 2),
        [VMEM] * (n + 2),
        [
            pltpu.VMEM((n - 1, 8, nodes), I32),
            pltpu.SMEM((n - 1, 8, nodes), I32),
            pltpu.SemaphoreType.DMA,
        ],
    )
    others = [swap(x, "die", n, k) for x, k in zip(served, rounds)]
    (index,) = call(
        functools.partial(where_kernel, rounds, span, rcap),
        [ints(blocks)],
        [die, reads, mine, guess],
        [SMEM] * 3 + [ANY],
        [SMEM],
        [pltpu.SMEM((n,), I32)],
    )
    step = 8 if blocks % 8 == 0 else blocks
    wide = pl.BlockSpec((step, scen, nodes), lambda i: (i, 0, 0))
    flat = pl.BlockSpec((step, nodes), lambda i: (i, 0))
    base, inv, scale, wire = pl.pallas_call(
        local_kernel,
        grid=(blocks // step,),
        out_shape=[block, block, block, jax.ShapeDtypeStruct((blocks, nodes), F32)],
        in_specs=[
            wide,
            wide,
            pl.BlockSpec((step, nodes, nodes), lambda i: (i, 0, 0)),
            flat,
            flat,
            flat,
            flat,
            wide,
        ],
        out_specs=[wide, wide, wide, flat],
        compiler_params=pltpu.CompilerParams(vmem_limit_bytes=8 << 20),
        cost_estimate=pl.CostEstimate(flops=0, bytes_accessed=0, transcendentals=0),
    )(
        guess,
        slopes,
        in_hbm(coupling),
        in_hbm(cap_rate),
        in_hbm(device_gain),
        in_hbm(wire_gain),
        in_hbm(region_gain),
        in_hbm(drive),
    )
    residual, share, partial = call(
        functools.partial(residual_kernel, n),
        [block, jax.ShapeDtypeStruct((scen, nodes), F32), block],
        [index, base, inv, scale, guess, wire, *others],
        [SMEM] + [VMEM] * (5 + n - 1),
        [VMEM] * 3,
        [pltpu.VMEM(((n - 1) * rcap, scen, nodes), F32)],
    )
    (stored,) = call(
        store_kernel, [block], [residual], [ANY], [HBM], [pltpu.SemaphoreType.DMA]
    )
    shares = [share] + [swap(share, ("sub", "blk"), ncol, k) for k in range(1, ncol)]
    parts = 4 if blocks % 4 == 0 else 1
    (updated,) = call(
        functools.partial(update_kernel, ncol, parts),
        [block],
        [*shares, whole, partial, scale],
        [VMEM] * (ncol + 3),
        [HBM],
        [pltpu.VMEM((blocks, scen, nodes), F32), pltpu.SemaphoreType.DMA((parts,))],
    )
    return (updated, stored)


def solution(mesh):
    every = ("grp", "die", "sub", "blk")
    in_specs = (
        P(every, None, None, None),
        P(every),
        P(every),
        P(every, None, None),
        P(every, None),
        P(every, None),
        P(every, None),
        P(every, None),
        P(every, None, None),
        P(("grp", "die"), "blk", None),
    )
    out_specs = (P(every, None, None), P(every, None, None))
    return jax.shard_map(shards, mesh=mesh, in_specs=in_specs, out_specs=out_specs, check_vma=False)
```

```python
import functools

import jax
import jax.numpy as jnp
from jax import lax
from jax.experimental import pallas as pl
from jax.experimental.pallas import tpu as pltpu
from jax.sharding import PartitionSpec as P

CAP = 2
VMEM = pl.BlockSpec(memory_space=pltpu.VMEM)
SMEM = pl.BlockSpec(memory_space=pltpu.SMEM)
ANY = pl.BlockSpec(memory_space=pl.ANY)
HBM = pl.BlockSpec(memory_space=pltpu.HBM)
F32 = jnp.float32
I32 = jnp.int32


def divmod_static(value, size):
    if size & (size - 1) == 0:
        return lax.shift_right_logical(value, size.bit_length() - 1), value & (size - 1)
    whole = lax.div(value, size)
    return whole, value - whole * size


def bit_of(index):
    return lax.shift_left(jnp.int32(1), index)


def bits_set(x):
    x = x - (lax.shift_right_logical(x, 1) & 0x55555555)
    x = (x & 0x33333333) + (lax.shift_right_logical(x, 2) & 0x33333333)
    x = (x + lax.shift_right_logical(x, 4)) & 0x0F0F0F0F
    x = x + lax.shift_right_logical(x, 8)
    x = x + lax.shift_right_logical(x, 16)
    return x & 63


def lowest(mask):
    return (31 - lax.clz(mask & -mask)) & 31


def halves(mask):
    return [mask & 0xFFFF, lax.shift_right_logical(mask, 16)]


def joined(low, high):
    return low | lax.shift_left(high, 16)


def predict(raw):
    return 3.0 * raw[0] - 3.0 * raw[1] + raw[2]


def slope(raw, guess):
    return 3.0 * guess - (4.0 * raw[0] - raw[1])


def leave_kernel(
    rounds, span, here_ref, new_slot_ref, partner_ref, history_ref, rows_ref,
    slots, reads, mine_ref, raw_ref, inverse_ref, *rest
):
    n = len(rounds) + 1
    outs, (source, place, count, sems) = rest[: n - 1], rest[n - 1 :]
    blocks, _, scen, nodes = history_ref.shape
    pieces = 4 if blocks % 4 == 0 else 1
    piece = blocks // pieces
    die = here_ref[0]
    copies = [
        pltpu.make_async_copy(new_slot_ref, slots, sems.at[0]),
        pltpu.make_async_copy(partner_ref, reads, sems.at[1]),
        pltpu.make_async_copy(rows_ref, inverse_ref, sems.at[2]),
    ]
    for at in range(pieces):
        some = pl.ds(at * piece, piece)
        copies.append(
            pltpu.make_async_copy(history_ref.at[some], raw_ref.at[some], sems.at[3 + at])
        )
    for copy in copies:
        copy.start()
    for at in range(n):
        count[at] = 0
    for at in range(n * CAP):
        source[at] = 0
        place[at] = -1
    copies[0].wait()
    copies[1].wait()

    wants = [jnp.int32(0)] * n
    for at in range(n):
        mine_ref[at] = 0
    for at in range(blocks):
        dest, local = divmod_static(slots[at], span)
        local = divmod_static(local, blocks)[1]

        @pl.when(dest != die)
        def _(at=at, dest=dest, local=local):
            rank = count[dest]
            count[dest] = rank + 1
            turn = (dest ^ die) * CAP + rank
            source[turn] = at
            place[turn] = local

        owner, local = divmod_static(reads[at], span)
        bit = bit_of(divmod_static(local, blocks)[1])
        for other in range(n if n <= 8 else 0):
            wants[other] = wants[other] | jnp.where(owner == other, bit, 0)
        if n > 8:
            mine_ref[owner] = mine_ref[owner] | bit
    if n <= 8:
        for at in range(n):
            mine_ref[at] = wants[at]
    for copy in copies[2:]:
        copy.wait()
    lane = lax.broadcasted_iota(I32, (8, nodes), 1)
    for k, out in zip(rounds, outs):
        for rank in range(CAP):
            raw = raw_ref.at[source[k * CAP + rank]]
            guess = predict(raw)
            out[pl.ds(rank * scen, scen), :] = guess
            out[pl.ds((CAP + rank) * scen, scen), :] = slope(raw, guess)
        row = jnp.zeros((8, nodes), I32)
        values = halves(mine_ref[die ^ k])
        values += [place[k * CAP + rank] for rank in range(CAP)]
        for j, value in enumerate(values):
            row = jnp.where(lane == j, value, row)
        out[pl.ds(2 * CAP * scen, 8), :] = row.astype(F32)


def place_kernel(span, here_ref, slots, raw_ref, guess_ref, slope_ref):
    blocks = raw_ref.shape[0]
    for at in range(blocks):
        dest, local = divmod_static(slots[at], span)
        local = divmod_static(local, blocks)[1]

        @pl.when(dest == here_ref[0])
        def _(at=at, local=local):
            raw = raw_ref.at[at]
            guess = predict(raw)
            guess_ref[local] = guess
            slope_ref[local] = slope(raw, guess)


def serve_kernel(n, rcap, nblk, blk_ref, *rest):
    arrived, rest = rest[: n - 1], rest[n - 1 :]
    inverses, rest = rest[:nblk], rest[nblk:]
    old_guess, old_slope, guess_ref, slope_ref, whole_ref, *rest = rest
    outs, (ints, meta, sem) = rest[: n - 1], rest[n - 1 :]
    blocks, scen, nodes = guess_ref.shape
    for k in range(n - 1):
        ints[k] = arrived[k][pl.ds(2 * CAP * scen, 8), :].astype(I32)
    copy = pltpu.make_async_copy(ints, meta, sem)
    copy.start()
    for at in range(blocks):
        guess_ref[at] = old_guess[at]
        slope_ref[at] = old_slope[at]
    height = inverses[0].shape[0]
    for k in range(nblk):
        at = pl.multiple_of((blk_ref[0] ^ k) * height, height)
        whole_ref[pl.ds(at, height), :] = inverses[k][...]
    copy.wait()
    for k in range(n - 1):
        for rank in range(CAP):
            place = meta[k, 0, 2 + rank]

            @pl.when(place >= 0)
            def _(k=k, rank=rank, place=place):
                guess_ref[place] = arrived[k][pl.ds(rank * scen, scen), :]
                slope_ref[place] = arrived[k][pl.ds((CAP + rank) * scen, scen), :]

    for k, out in enumerate(outs):
        want = joined(meta[k, 0, 0], meta[k, 0, 1])
        for slot in range(rcap):
            out[slot] = guess_ref[lowest(want)]
            want = want & (want - 1)


def where_kernel(rounds, span, rcap, here_ref, reads, mine_ref, _, index_ref, starts):
    blocks = index_ref.shape[0]
    die = here_ref[0]
    starts[0] = 0
    for at, k in enumerate(rounds):
        starts[k] = at * rcap

    def step(at, carry):
        owner, local = divmod_static(reads[at], span)
        local = divmod_static(local, blocks)[1]
        k = owner ^ die
        slot = bits_set(mine_ref[owner] & (bit_of(local) - 1))
        index_ref[at] = jnp.where(k == 0, local - blocks, starts[k] + slot)
        return carry

    lax.fori_loop(0, blocks, step, 0)


def local_kernel(
    guess_ref, slope_ref, coupling_ref, cap_ref, gdev_ref, wire_ref, gain_ref, drive_ref,
    base_ref, inv_ref, scale_ref, kept_ref
):
    nodes = coupling_ref.shape[1]
    rows = lax.broadcasted_iota(I32, (nodes, nodes), 0)
    cols = lax.broadcasted_iota(I32, (nodes, nodes), 1)
    for at in range(guess_ref.shape[0]):
        guess = guess_ref[at]
        coupling = coupling_ref[at]
        cap = cap_ref[at : at + 1, :]
        gdev = gdev_ref[at : at + 1, :]
        wire = wire_ref[at : at + 1, :]
        through = lax.dot_general(
            guess,
            coupling,
            (((1,), (1,)), ((), ())),
            precision=lax.Precision.HIGHEST,
            preferred_element_type=F32,
        )
        diagonal = jnp.sum(jnp.where(rows == cols, coupling, 0.0), axis=0, keepdims=True)
        tnh = jnp.tanh(guess)
        inv = 1.0 / (1.5 * cap + diagonal + gdev * (1.0 - tnh * tnh) + wire)
        inv_ref[at] = inv
        kept_ref[at : at + 1, :] = wire
        scale_ref[at] = gain_ref[at : at + 1, :] * inv
        base_ref[at] = (
            0.5 * cap * slope_ref[at] + through + gdev * tnh + wire * guess - drive_ref[at]
        )


def residual_kernel(n, index_ref, base_ref, inv_ref, scale_ref, guess_ref, wire_ref, *rest):
    blocks_in, (residual_ref, share_ref, partial_ref, pool) = rest[: n - 1], rest[n - 1 :]
    blocks = guess_ref.shape[0]
    start = 0
    for ref in blocks_in:
        for slot in range(ref.shape[0]):
            pool[start + slot] = ref[slot]
        start += ref.shape[0]
    share = jnp.zeros(share_ref.shape, F32)
    for at in range(blocks):
        index = index_ref[at]
        own = index < 0
        near = guess_ref[jnp.where(own, index + blocks, 0)]
        other = jnp.where(own, near, pool[jnp.maximum(index, 0)])
        residual = base_ref[at] - wire_ref[at : at + 1, :] * other
        residual_ref[at] = residual
        partial_ref[at] = guess_ref[at] - residual * inv_ref[at]
        share = share + scale_ref[at] * residual
    share_ref[...] = share


def store_kernel(value_ref, out_ref, sem):
    copy = pltpu.make_async_copy(value_ref, out_ref, sem)
    copy.start()
    copy.wait()


def update_kernel(m, parts, *rest):
    shares, (whole_ref, partial_ref, scale_ref, updated_ref, held, sems) = rest[:m], rest[m:]
    total = shares[0][...]
    for share in shares[1:]:
        total = total + share[...]
    region = jnp.dot(
        total, whole_ref[...], precision=lax.Precision.HIGHEST, preferred_element_type=F32
    )
    step = partial_ref.shape[0] // parts
    copies = []
    for part in range(parts):
        for at in range(part * step, (part + 1) * step):
            held[at] = partial_ref[at] + scale_ref[at] * region
        span = pl.ds(part * step, step)
        copies.append(pltpu.make_async_copy(held.at[span], updated_ref.at[span], sems.at[part]))
        copies[-1].start()
    for copy in copies:
        copy.wait()


def call(body, outs, ins, in_specs, out_specs, scratch=(), limit=8):
    return pl.pallas_call(
        body,
        out_shape=outs,
        in_specs=in_specs,
        out_specs=out_specs,
        scratch_shapes=list(scratch),
        compiler_params=pltpu.CompilerParams(vmem_limit_bytes=limit << 20),
        cost_estimate=pl.CostEstimate(flops=0, bytes_accessed=0, transcendentals=0),
    )(*ins)


def in_hbm(x):
    return pltpu.with_memory_space_constraint(x, pltpu.HBM)


def swap(x, axes, n, k):
    return lax.ppermute(x, axes, [(d, d ^ k) for d in range(n)])


def shards(
    history,
    new_slot,
    partner,
    coupling,
    cap_rate,
    device_gain,
    wire_gain,
    region_gain,
    drive,
    region_inverse,
):
    blocks, _, scen, nodes = history.shape
    n = lax.axis_size("die")
    nblk = lax.axis_size("blk")
    ncol = lax.axis_size("sub") * nblk
    for size in (n, nblk, ncol):
        assert size & (size - 1) == 0
    assert blocks <= 32
    rcap = 2 * max(1, blocks // n)
    span = ncol * blocks
    die = lax.axis_index("die").astype(I32).reshape(1)
    blk = lax.axis_index("blk").astype(I32).reshape(1)

    def tiles(count):
        return jax.ShapeDtypeStruct((count, scen, nodes), F32)

    def ints(count):
        return jax.ShapeDtypeStruct((count,), I32)

    block = tiles(blocks)
    square = jax.ShapeDtypeStruct((nodes, nodes), F32)
    rows = region_inverse[0]
    message = jax.ShapeDtypeStruct((2 * CAP * scen + 8, nodes), F32)

    rounds = [*range(2, n), 1]
    slots, reads, mine, raw, rows, *leaving = call(
        functools.partial(leave_kernel, rounds, span),
        [
            ints(blocks),
            ints(blocks),
            ints(n),
            jax.ShapeDtypeStruct(history.shape, F32),
            jax.ShapeDtypeStruct(rows.shape, F32),
        ]
        + [message] * (n - 1),
        [die, in_hbm(new_slot), in_hbm(partner), in_hbm(history), in_hbm(rows)],
        [SMEM] + [HBM] * 4,
        [SMEM] * 3 + [VMEM] * (n + 1),
        [pltpu.SMEM((n * CAP,), I32)] * 2
        + [pltpu.SMEM((n,), I32), pltpu.SemaphoreType.DMA((7,))],
    )
    arrived = [swap(x, "die", n, k) for x, k in zip(leaving, rounds)]
    inverses = [rows] + [swap(rows, "blk", nblk, k) for k in range(1, nblk)]
    old_guess, old_slope = call(
        functools.partial(place_kernel, span),
        [block, block],
        [die, slots, raw],
        [SMEM, SMEM, VMEM],
        [VMEM, VMEM],
    )
    guess, slopes, whole, *served = call(
        functools.partial(serve_kernel, n, rcap, nblk),
        [block, block, square] + [tiles(rcap)] * (n - 1),
        [blk, *arrived, *inverses, old_guess, old_slope],
        [SMEM] + [VMEM] * (n - 1 + nblk + 2),
        [VMEM] * (n + 2),
        [
            pltpu.VMEM((n - 1, 8, nodes), I32),
            pltpu.SMEM((n - 1, 8, nodes), I32),
            pltpu.SemaphoreType.DMA,
        ],
    )
    others = [swap(x, "die", n, k) for x, k in zip(served, rounds)]
    (index,) = call(
        functools.partial(where_kernel, rounds, span, rcap),
        [ints(blocks)],
        [die, reads, mine, guess],
        [SMEM] * 3 + [ANY],
        [SMEM],
        [pltpu.SMEM((n,), I32)],
    )
    step = 8 if blocks % 8 == 0 else blocks
    wide = pl.BlockSpec((step, scen, nodes), lambda i: (i, 0, 0))
    flat = pl.BlockSpec((step, nodes), lambda i: (i, 0))
    base, inv, scale, wire = pl.pallas_call(
        local_kernel,
        grid=(blocks // step,),
        out_shape=[block, block, block, jax.ShapeDtypeStruct((blocks, nodes), F32)],
        in_specs=[
            wide,
            wide,
            pl.BlockSpec((step, nodes, nodes), lambda i: (i, 0, 0)),
            flat,
            flat,
            flat,
            flat,
            wide,
        ],
        out_specs=[wide, wide, wide, flat],
        compiler_params=pltpu.CompilerParams(vmem_limit_bytes=8 << 20),
        cost_estimate=pl.CostEstimate(flops=0, bytes_accessed=0, transcendentals=0),
    )(
        guess,
        slopes,
        in_hbm(coupling),
        in_hbm(cap_rate),
        in_hbm(device_gain),
        in_hbm(wire_gain),
        in_hbm(region_gain),
        in_hbm(drive),
    )
    residual, share, partial = call(
        functools.partial(residual_kernel, n),
        [block, jax.ShapeDtypeStruct((scen, nodes), F32), block],
        [index, base, inv, scale, guess, wire, *others],
        [SMEM] + [VMEM] * (5 + n - 1),
        [VMEM] * 3,
        [pltpu.VMEM(((n - 1) * rcap, scen, nodes), F32)],
    )
    (stored,) = call(
        store_kernel, [block], [residual], [ANY], [HBM], [pltpu.SemaphoreType.DMA]
    )
    shares = [share] + [swap(share, ("sub", "blk"), ncol, k) for k in range(1, ncol)]
    parts = 4 if blocks % 4 == 0 else 1
    (updated,) = call(
        functools.partial(update_kernel, ncol, parts),
        [block],
        [*shares, whole, partial, scale],
        [VMEM] * (ncol + 3),
        [HBM],
        [pltpu.VMEM((blocks, scen, nodes), F32), pltpu.SemaphoreType.DMA((parts,))],
    )
    return (updated, stored)


def solution(mesh):
    every = ("grp", "die", "sub", "blk")
    in_specs = (
        P(every, None, None, None),
        P(every),
        P(every),
        P(every, None, None),
        P(every, None),
        P(every, None),
        P(every, None),
        P(every, None),
        P(every, None, None),
        P(("grp", "die"), "blk", None),
    )
    out_specs = (P(every, None, None), P(every, None, None))
    return jax.shard_map(shards, mesh=mesh, in_specs=in_specs, out_specs=out_specs, check_vma=False)
```

```python
import functools

import jax
import jax.numpy as jnp
from jax import lax
from jax.experimental import pallas as pl
from jax.experimental.pallas import tpu as pltpu
from jax.sharding import PartitionSpec as P

CAP = 2
VMEM = pl.BlockSpec(memory_space=pltpu.VMEM)
SMEM = pl.BlockSpec(memory_space=pltpu.SMEM)
ANY = pl.BlockSpec(memory_space=pl.ANY)
HBM = pl.BlockSpec(memory_space=pltpu.HBM)
F32 = jnp.float32
I32 = jnp.int32


def divmod_static(value, size):
    if size & (size - 1) == 0:
        return lax.shift_right_logical(value, size.bit_length() - 1), value & (size - 1)
    whole = lax.div(value, size)
    return whole, value - whole * size


def bit_of(index):
    return lax.shift_left(jnp.int32(1), index)


def bits_set(x):
    x = x - (lax.shift_right_logical(x, 1) & 0x55555555)
    x = (x & 0x33333333) + (lax.shift_right_logical(x, 2) & 0x33333333)
    x = (x + lax.shift_right_logical(x, 4)) & 0x0F0F0F0F
    x = x + lax.shift_right_logical(x, 8)
    x = x + lax.shift_right_logical(x, 16)
    return x & 63


def lowest(mask):
    return (31 - lax.clz(mask & -mask)) & 31


def halves(mask):
    return [mask & 0xFFFF, lax.shift_right_logical(mask, 16)]


def joined(low, high):
    return low | lax.shift_left(high, 16)


def predict(raw):
    return 3.0 * raw[0] - 3.0 * raw[1] + raw[2]


def slope(raw, guess):
    return 3.0 * guess - (4.0 * raw[0] - raw[1])


def read_masks(n, span, blocks, reads, mine):
    wants = [jnp.int32(0)] * n
    for at in range(n):
        mine[at] = 0
    for at in range(blocks):
        owner, local = divmod_static(reads[at], span)
        bit = bit_of(divmod_static(local, blocks)[1])
        if n > 8:
            mine[owner] = mine[owner] | bit
        else:
            wants = [want | jnp.where(owner == o, bit, 0) for o, want in enumerate(wants)]
    if n <= 8:
        for at in range(n):
            mine[at] = wants[at]


def leave_kernel(
    rounds, span, new_slot_ref, partner_ref, history_ref, rows_ref, raw_ref, inverse_ref, *rest
):
    n = len(rounds) + 1
    outs, (slots, reads, mine, source, place, count, sems) = rest[: n - 1], rest[n - 1 :]
    blocks, _, scen, nodes = history_ref.shape
    pieces = 4 if blocks % 4 == 0 else 1
    piece = blocks // pieces
    die = lax.axis_index("die")
    copies = [
        pltpu.make_async_copy(new_slot_ref, slots, sems.at[0]),
        pltpu.make_async_copy(partner_ref, reads, sems.at[1]),
        pltpu.make_async_copy(rows_ref, inverse_ref, sems.at[2]),
    ]
    for at in range(pieces):
        some = pl.ds(at * piece, piece)
        copies.append(
            pltpu.make_async_copy(history_ref.at[some], raw_ref.at[some], sems.at[3 + at])
        )
    for copy in copies:
        copy.start()
    for at in range(n):
        count[at] = 0
    for at in range(n * CAP):
        source[at] = 0
        place[at] = -1
    copies[0].wait()
    copies[1].wait()

    for at in range(blocks):
        dest, local = divmod_static(slots[at], span)
        local = divmod_static(local, blocks)[1]

        @pl.when(dest != die)
        def _(at=at, dest=dest, local=local):
            rank = count[dest]
            count[dest] = rank + 1
            turn = (dest ^ die) * CAP + rank
            source[turn] = at
            place[turn] = local

    read_masks(n, span, blocks, reads, mine)
    for copy in copies[2:]:
        copy.wait()
    lane = lax.broadcasted_iota(I32, (8, nodes), 1)
    for k, out in zip(rounds, outs):
        for rank in range(CAP):
            raw = raw_ref.at[source[k * CAP + rank]]
            guess = predict(raw)
            out[pl.ds(rank * scen, scen), :] = guess
            out[pl.ds((CAP + rank) * scen, scen), :] = slope(raw, guess)
        row = jnp.zeros((8, nodes), I32)
        values = halves(mine[die ^ k])
        values += [place[k * CAP + rank] for rank in range(CAP)]
        for j, value in enumerate(values):
            row = jnp.where(lane == j, value, row)
        out[pl.ds(2 * CAP * scen, 8), :] = row.astype(F32)


def place_kernel(span, new_slot_ref, raw_ref, guess_ref, slope_ref, slots, sem):
    blocks = raw_ref.shape[0]
    die = lax.axis_index("die")
    copy = pltpu.make_async_copy(new_slot_ref, slots, sem)
    copy.start()
    copy.wait()
    for at in range(blocks):
        dest, local = divmod_static(slots[at], span)
        local = divmod_static(local, blocks)[1]

        @pl.when(dest == die)
        def _(at=at, local=local):
            raw = raw_ref.at[at]
            guess = predict(raw)
            guess_ref[local] = guess
            slope_ref[local] = slope(raw, guess)


def pack(meta, guess_ref, out):
    want = joined(meta[0], meta[1])
    for slot in range(out.shape[0]):
        out[slot] = guess_ref[lowest(want)]
        want = want & (want - 1)


def serve_kernel(n, nblk, *rest):
    arrived, rest = rest[: n - 1], rest[n - 1 :]
    inverses, rest = rest[:nblk], rest[nblk:]
    old_guess, old_slope, guess_ref, slope_ref, whole_ref, *rest = rest
    outs, (ints, meta, sem) = rest[: n - 2], rest[n - 2 :]
    blocks, scen, nodes = guess_ref.shape
    for k in range(n - 1):
        ints[k] = arrived[k][pl.ds(2 * CAP * scen, 8), :].astype(I32)
    copy = pltpu.make_async_copy(ints, meta, sem)
    copy.start()
    for at in range(blocks):
        guess_ref[at] = old_guess[at]
        slope_ref[at] = old_slope[at]
    height = inverses[0].shape[0]
    for k in range(nblk):
        at = pl.multiple_of((lax.axis_index("blk") ^ k) * height, height)
        whole_ref[pl.ds(at, height), :] = inverses[k][...]
    copy.wait()
    for k in range(n - 1):
        for rank in range(CAP):
            place = meta[k, 0, 2 + rank]

            @pl.when(place >= 0)
            def _(k=k, rank=rank, place=place):
                guess_ref[place] = arrived[k][pl.ds(rank * scen, scen), :]
                slope_ref[place] = arrived[k][pl.ds((CAP + rank) * scen, scen), :]

    for k, out in enumerate(outs):
        pack([meta[k, 0, 0], meta[k, 0, 1]], guess_ref, out)


def nearest_kernel(arrived, guess_ref, _, out, ints, meta, sem):
    ints[...] = arrived[pl.ds(arrived.shape[0] - 8, 8), :].astype(I32)
    copy = pltpu.make_async_copy(ints, meta, sem)
    copy.start()
    copy.wait()
    pack([meta[0, 0], meta[0, 1]], guess_ref, out)


def where_kernel(rounds, span, rcap, partner_ref, _, index_ref, reads, mine, starts, sem):
    n = len(rounds) + 1
    blocks = index_ref.shape[0]
    die = lax.axis_index("die")
    copy = pltpu.make_async_copy(partner_ref, reads, sem)
    copy.start()
    starts[0] = 0
    for at, k in enumerate(rounds):
        starts[k] = at * rcap
    copy.wait()
    read_masks(n, span, blocks, reads, mine)

    def step(at, carry):
        owner, local = divmod_static(reads[at], span)
        local = divmod_static(local, blocks)[1]
        k = owner ^ die
        slot = bits_set(mine[owner] & (bit_of(local) - 1))
        index_ref[at] = jnp.where(k == 0, local - blocks, starts[k] + slot)
        return carry

    lax.fori_loop(0, blocks, step, 0)


def local_kernel(
    guess_ref, slope_ref, coupling_ref, cap_ref, gdev_ref, wire_ref, gain_ref, drive_ref,
    base_ref, inv_ref, scale_ref, kept_ref
):
    nodes = coupling_ref.shape[1]
    rows = lax.broadcasted_iota(I32, (nodes, nodes), 0)
    cols = lax.broadcasted_iota(I32, (nodes, nodes), 1)
    for at in range(guess_ref.shape[0]):
        guess = guess_ref[at]
        coupling = coupling_ref[at]
        cap = cap_ref[at : at + 1, :]
        gdev = gdev_ref[at : at + 1, :]
        wire = wire_ref[at : at + 1, :]
        through = lax.dot_general(
            guess,
            coupling,
            (((1,), (1,)), ((), ())),
            precision=lax.Precision.HIGHEST,
            preferred_element_type=F32,
        )
        diagonal = jnp.sum(jnp.where(rows == cols, coupling, 0.0), axis=0, keepdims=True)
        tnh = jnp.tanh(guess)
        inv = 1.0 / (1.5 * cap + diagonal + gdev * (1.0 - tnh * tnh) + wire)
        inv_ref[at] = inv
        kept_ref[at : at + 1, :] = wire
        scale_ref[at] = gain_ref[at : at + 1, :] * inv
        base_ref[at] = (
            0.5 * cap * slope_ref[at] + through + gdev * tnh + wire * guess - drive_ref[at]
        )


def residual_kernel(n, index_ref, base_ref, inv_ref, scale_ref, guess_ref, wire_ref, *rest):
    blocks_in, (residual_ref, share_ref, partial_ref, pool) = rest[: n - 1], rest[n - 1 :]
    blocks = guess_ref.shape[0]
    start = 0
    for ref in blocks_in:
        for slot in range(ref.shape[0]):
            pool[start + slot] = ref[slot]
        start += ref.shape[0]
    share = jnp.zeros(share_ref.shape, F32)
    for at in range(blocks):
        index = index_ref[at]
        own = index < 0
        near = guess_ref[jnp.where(own, index + blocks, 0)]
        other = jnp.where(own, near, pool[jnp.maximum(index, 0)])
        residual = base_ref[at] - wire_ref[at : at + 1, :] * other
        residual_ref[at] = residual
        partial_ref[at] = guess_ref[at] - residual * inv_ref[at]
        share = share + scale_ref[at] * residual
    share_ref[...] = share


def store_kernel(value_ref, out_ref, sem):
    copy = pltpu.make_async_copy(value_ref, out_ref, sem)
    copy.start()
    copy.wait()


def update_kernel(m, parts, *rest):
    shares, (whole_ref, partial_ref, scale_ref, updated_ref, held, sems) = rest[:m], rest[m:]
    total = shares[0][...]
    for share in shares[1:]:
        total = total + share[...]
    region = jnp.dot(
        total, whole_ref[...], precision=lax.Precision.HIGHEST, preferred_element_type=F32
    )
    step = partial_ref.shape[0] // parts
    copies = []
    for part in range(parts):
        for at in range(part * step, (part + 1) * step):
            held[at] = partial_ref[at] + scale_ref[at] * region
        span = pl.ds(part * step, step)
        copies.append(pltpu.make_async_copy(held.at[span], updated_ref.at[span], sems.at[part]))
        copies[-1].start()
    for copy in copies:
        copy.wait()


def call(body, outs, ins, in_specs, out_specs, scratch=(), limit=8):
    return pl.pallas_call(
        body,
        out_shape=outs,
        in_specs=in_specs,
        out_specs=out_specs,
        scratch_shapes=list(scratch),
        compiler_params=pltpu.CompilerParams(vmem_limit_bytes=limit << 20),
        cost_estimate=pl.CostEstimate(flops=0, bytes_accessed=0, transcendentals=0),
    )(*ins)


def in_hbm(x):
    return pltpu.with_memory_space_constraint(x, pltpu.HBM)


def swap(x, axes, n, k):
    return lax.ppermute(x, axes, [(d, d ^ k) for d in range(n)])


def shards(
    history,
    new_slot,
    partner,
    coupling,
    cap_rate,
    device_gain,
    wire_gain,
    region_gain,
    drive,
    region_inverse,
):
    blocks, _, scen, nodes = history.shape
    n = lax.axis_size("die")
    nblk = lax.axis_size("blk")
    ncol = lax.axis_size("sub") * nblk
    for size in (n, nblk, ncol):
        assert size & (size - 1) == 0
    assert blocks <= 32
    rcap = 2 * max(1, blocks // n)
    span = ncol * blocks

    def tiles(count):
        return jax.ShapeDtypeStruct((count, scen, nodes), F32)

    def scalars(count):
        return pltpu.SMEM((count,), I32)

    block = tiles(blocks)
    square = jax.ShapeDtypeStruct((nodes, nodes), F32)
    rows = region_inverse[0]
    message = jax.ShapeDtypeStruct((2 * CAP * scen + 8, nodes), F32)

    rounds = [*range(2, n), 1]
    new_slot, partner = in_hbm(new_slot), in_hbm(partner)
    raw, rows, *leaving = call(
        functools.partial(leave_kernel, rounds, span),
        [jax.ShapeDtypeStruct(history.shape, F32), jax.ShapeDtypeStruct(rows.shape, F32)]
        + [message] * (n - 1),
        [new_slot, partner, in_hbm(history), in_hbm(rows)],
        [HBM] * 4,
        [VMEM] * (n + 1),
        [scalars(blocks)] * 2
        + [scalars(n)]
        + [scalars(n * CAP)] * 2
        + [scalars(n), pltpu.SemaphoreType.DMA((7,))],
    )
    arrived = [swap(x, "die", n, k) for x, k in zip(leaving, rounds)]
    inverses = [rows] + [swap(rows, "blk", nblk, k) for k in range(1, nblk)]
    old_guess, old_slope = call(
        functools.partial(place_kernel, span),
        [block, block],
        [new_slot, raw],
        [HBM, VMEM],
        [VMEM, VMEM],
        [scalars(blocks), pltpu.SemaphoreType.DMA],
    )
    guess, slopes, whole, *served = call(
        functools.partial(serve_kernel, n, nblk),
        [block, block, square] + [tiles(rcap)] * (n - 2),
        [*arrived, *inverses, old_guess, old_slope],
        [VMEM] * (n - 1 + nblk + 2),
        [VMEM] * (n + 1),
        [
            pltpu.VMEM((n - 1, 8, nodes), I32),
            pltpu.SMEM((n - 1, 8, nodes), I32),
            pltpu.SemaphoreType.DMA,
        ],
    )
    others = [swap(x, "die", n, k) for x, k in zip(served, rounds)]
    (index,) = call(
        functools.partial(where_kernel, rounds, span, rcap),
        [jax.ShapeDtypeStruct((blocks,), I32)],
        [partner, guess],
        [HBM, ANY],
        [SMEM],
        [scalars(blocks), scalars(n), scalars(n), pltpu.SemaphoreType.DMA],
    )
    step = 8 if blocks % 8 == 0 else blocks
    wide = pl.BlockSpec((step, scen, nodes), lambda i: (i, 0, 0))
    flat = pl.BlockSpec((step, nodes), lambda i: (i, 0))
    base, inv, scale, wire = pl.pallas_call(
        local_kernel,
        grid=(blocks // step,),
        out_shape=[block, block, block, jax.ShapeDtypeStruct((blocks, nodes), F32)],
        in_specs=[
            wide,
            wide,
            pl.BlockSpec((step, nodes, nodes), lambda i: (i, 0, 0)),
            flat,
            flat,
            flat,
            flat,
            wide,
        ],
        out_specs=[wide, wide, wide, flat],
        compiler_params=pltpu.CompilerParams(vmem_limit_bytes=8 << 20),
        cost_estimate=pl.CostEstimate(flops=0, bytes_accessed=0, transcendentals=0),
    )(
        guess,
        slopes,
        in_hbm(coupling),
        in_hbm(cap_rate),
        in_hbm(device_gain),
        in_hbm(wire_gain),
        in_hbm(region_gain),
        in_hbm(drive),
    )
    (near,) = call(
        nearest_kernel,
        [tiles(rcap)],
        [arrived[-1], guess, base],
        [VMEM, VMEM, ANY],
        [VMEM],
        [pltpu.VMEM((8, nodes), I32), pltpu.SMEM((8, nodes), I32), pltpu.SemaphoreType.DMA],
    )
    others.append(swap(near, "die", n, rounds[-1]))
    residual, share, partial = call(
        functools.partial(residual_kernel, n),
        [block, jax.ShapeDtypeStruct((scen, nodes), F32), block],
        [index, base, inv, scale, guess, wire, *others],
        [SMEM] + [VMEM] * (5 + n - 1),
        [VMEM] * 3,
        [pltpu.VMEM(((n - 1) * rcap, scen, nodes), F32)],
    )
    (stored,) = call(
        store_kernel, [block], [residual], [ANY], [HBM], [pltpu.SemaphoreType.DMA]
    )
    shares = [share] + [swap(share, ("sub", "blk"), ncol, k) for k in range(1, ncol)]
    parts = 4 if blocks % 4 == 0 else 1
    (updated,) = call(
        functools.partial(update_kernel, ncol, parts),
        [block],
        [*shares, whole, partial, scale],
        [VMEM] * (ncol + 3),
        [HBM],
        [pltpu.VMEM((blocks, scen, nodes), F32), pltpu.SemaphoreType.DMA((parts,))],
    )
    return (updated, stored)


def solution(mesh):
    every = ("grp", "die", "sub", "blk")
    in_specs = (
        P(every, None, None, None),
        P(every),
        P(every),
        P(every, None, None),
        P(every, None),
        P(every, None),
        P(every, None),
        P(every, None),
        P(every, None, None),
        P(("grp", "die"), "blk", None),
    )
    out_specs = (P(every, None, None), P(every, None, None))
    return jax.shard_map(shards, mesh=mesh, in_specs=in_specs, out_specs=out_specs, check_vma=False)
```

```python
import functools

import jax
import jax.numpy as jnp
from jax import lax
from jax.experimental import pallas as pl
from jax.experimental.pallas import tpu as pltpu
from jax.sharding import PartitionSpec as P

CAP = 2
VMEM = pl.BlockSpec(memory_space=pltpu.VMEM)
SMEM = pl.BlockSpec(memory_space=pltpu.SMEM)
ANY = pl.BlockSpec(memory_space=pl.ANY)
HBM = pl.BlockSpec(memory_space=pltpu.HBM)
F32 = jnp.float32
I32 = jnp.int32


def divmod_static(value, size):
    if size & (size - 1) == 0:
        return lax.shift_right_logical(value, size.bit_length() - 1), value & (size - 1)
    whole = lax.div(value, size)
    return whole, value - whole * size


def bit_of(index):
    return lax.shift_left(jnp.int32(1), index)


def bits_set(x):
    x = x - (lax.shift_right_logical(x, 1) & 0x55555555)
    x = (x & 0x33333333) + (lax.shift_right_logical(x, 2) & 0x33333333)
    x = (x + lax.shift_right_logical(x, 4)) & 0x0F0F0F0F
    x = x + lax.shift_right_logical(x, 8)
    x = x + lax.shift_right_logical(x, 16)
    return x & 63


def lowest(mask):
    return (31 - lax.clz(mask & -mask)) & 31


def cut(x):
    high = x.astype(jnp.bfloat16)
    return high, (x - high.astype(F32)).astype(jnp.bfloat16)


def halves(mask):
    return [mask & 0xFFFF, lax.shift_right_logical(mask, 16)]


def joined(low, high):
    return low | lax.shift_left(high, 16)


def predict(raw):
    return 3.0 * raw[0] - 3.0 * raw[1] + raw[2]


def slope(raw, guess):
    return 3.0 * guess - (4.0 * raw[0] - raw[1])


def read_masks(n, span, blocks, reads, mine):
    wants = [jnp.int32(0)] * n
    for at in range(n):
        mine[at] = 0
    for at in range(blocks):
        owner, local = divmod_static(reads[at], span)
        bit = bit_of(divmod_static(local, blocks)[1])
        if n > 8:
            mine[owner] = mine[owner] | bit
        else:
            wants = [want | jnp.where(owner == o, bit, 0) for o, want in enumerate(wants)]
    if n <= 8:
        for at in range(n):
            mine[at] = wants[at]


def leave_kernel(
    rounds, span, new_slot_ref, partner_ref, history_ref, rows_ref, raw_ref, inverse_ref, *rest
):
    n = len(rounds) + 1
    outs, (slots, reads, mine, source, place, count, sems) = rest[: n - 1], rest[n - 1 :]
    blocks, _, scen, nodes = history_ref.shape
    pieces = 4 if blocks % 4 == 0 else 1
    piece = blocks // pieces
    die = lax.axis_index("die")
    copies = [
        pltpu.make_async_copy(new_slot_ref, slots, sems.at[0]),
        pltpu.make_async_copy(partner_ref, reads, sems.at[1]),
        pltpu.make_async_copy(rows_ref, inverse_ref, sems.at[2]),
    ]
    for at in range(pieces):
        some = pl.ds(at * piece, piece)
        copies.append(
            pltpu.make_async_copy(history_ref.at[some], raw_ref.at[some], sems.at[3 + at])
        )
    for copy in copies:
        copy.start()
    for at in range(n):
        count[at] = 0
    for at in range(n * CAP):
        source[at] = 0
        place[at] = -1
    copies[0].wait()
    copies[1].wait()

    for at in range(blocks):
        dest, local = divmod_static(slots[at], span)
        local = divmod_static(local, blocks)[1]

        @pl.when(dest != die)
        def _(at=at, dest=dest, local=local):
            rank = count[dest]
            count[dest] = rank + 1
            turn = (dest ^ die) * CAP + rank
            source[turn] = at
            place[turn] = local

    read_masks(n, span, blocks, reads, mine)
    for copy in copies[2:]:
        copy.wait()
    lane = lax.broadcasted_iota(I32, (8, nodes), 1)
    for k, out in zip(rounds, outs):
        for rank in range(CAP):
            raw = raw_ref.at[source[k * CAP + rank]]
            guess = predict(raw)
            out[pl.ds(rank * scen, scen), :] = guess
            out[pl.ds((CAP + rank) * scen, scen), :] = slope(raw, guess)
        row = jnp.zeros((8, nodes), I32)
        values = halves(mine[die ^ k])
        values += [place[k * CAP + rank] for rank in range(CAP)]
        for j, value in enumerate(values):
            row = jnp.where(lane == j, value, row)
        out[pl.ds(2 * CAP * scen, 8), :] = row.astype(F32)


def place_kernel(span, new_slot_ref, raw_ref, guess_ref, slope_ref, slots, sem):
    blocks = raw_ref.shape[0]
    die = lax.axis_index("die")
    copy = pltpu.make_async_copy(new_slot_ref, slots, sem)
    copy.start()
    copy.wait()
    for at in range(blocks):
        dest, local = divmod_static(slots[at], span)
        local = divmod_static(local, blocks)[1]

        @pl.when(dest == die)
        def _(at=at, local=local):
            raw = raw_ref.at[at]
            guess = predict(raw)
            guess_ref[local] = guess
            slope_ref[local] = slope(raw, guess)


def pack(meta, guess_ref, out):
    want = joined(meta[0], meta[1])
    for slot in range(out.shape[0]):
        out[slot] = guess_ref[lowest(want)]
        want = want & (want - 1)


def serve_kernel(n, nblk, *rest):
    arrived, rest = rest[: n - 1], rest[n - 1 :]
    inverses, rest = rest[:nblk], rest[nblk:]
    old_guess, old_slope, guess_ref, slope_ref, whole_ref, *rest = rest
    outs, (ints, meta, sem) = rest[: n - 1], rest[n - 1 :]
    blocks, scen, nodes = guess_ref.shape
    for k in range(n - 1):
        ints[k] = arrived[k][pl.ds(2 * CAP * scen, 8), :].astype(I32)
    copy = pltpu.make_async_copy(ints, meta, sem)
    copy.start()
    for at in range(blocks):
        guess_ref[at] = old_guess[at]
        slope_ref[at] = old_slope[at]
    height = inverses[0].shape[0]
    for k in range(nblk):
        at = pl.multiple_of((lax.axis_index("blk") ^ k) * height, height)
        high, low = cut(inverses[k][...])
        whole_ref[pl.ds(at, height), :] = high
        whole_ref[pl.ds(nodes + at, height), :] = low
    copy.wait()
    for k in range(n - 1):
        for rank in range(CAP):
            place = meta[k, 0, 2 + rank]

            @pl.when(place >= 0)
            def _(k=k, rank=rank, place=place):
                guess_ref[place] = arrived[k][pl.ds(rank * scen, scen), :]
                slope_ref[place] = arrived[k][pl.ds((CAP + rank) * scen, scen), :]

    for k, out in enumerate(outs):
        pack([meta[k, 0, 0], meta[k, 0, 1]], guess_ref, out)


def where_kernel(rounds, span, rcap, partner_ref, _, index_ref, reads, mine, starts, sem):
    n = len(rounds) + 1
    blocks = index_ref.shape[0]
    die = lax.axis_index("die")
    copy = pltpu.make_async_copy(partner_ref, reads, sem)
    copy.start()
    starts[0] = 0
    for at, k in enumerate(rounds):
        starts[k] = at * rcap
    copy.wait()
    read_masks(n, span, blocks, reads, mine)

    def step(at, carry):
        owner, local = divmod_static(reads[at], span)
        local = divmod_static(local, blocks)[1]
        k = owner ^ die
        slot = bits_set(mine[owner] & (bit_of(local) - 1))
        index_ref[at] = jnp.where(k == 0, local - blocks, starts[k] + slot)
        return carry

    lax.fori_loop(0, blocks, step, 0)


def local_kernel(
    guess_ref, slope_ref, coupling_ref, cap_ref, gdev_ref, wire_ref, gain_ref, drive_ref,
    base_ref, inv_ref, scale_ref, kept_ref
):
    nodes = coupling_ref.shape[1]
    rows = lax.broadcasted_iota(I32, (nodes, nodes), 0)
    cols = lax.broadcasted_iota(I32, (nodes, nodes), 1)
    for at in range(guess_ref.shape[0]):
        guess = guess_ref[at]
        coupling = coupling_ref[at]
        cap = cap_ref[at : at + 1, :]
        gdev = gdev_ref[at : at + 1, :]
        wire = wire_ref[at : at + 1, :]
        through = lax.dot_general(
            guess,
            coupling,
            (((1,), (1,)), ((), ())),
            precision=lax.Precision.HIGHEST,
            preferred_element_type=F32,
        )
        diagonal = jnp.sum(jnp.where(rows == cols, coupling, 0.0), axis=0, keepdims=True)
        tnh = jnp.tanh(guess)
        inv = 1.0 / (1.5 * cap + diagonal + gdev * (1.0 - tnh * tnh) + wire)
        inv_ref[at] = inv
        kept_ref[at : at + 1, :] = wire
        scale_ref[at] = gain_ref[at : at + 1, :] * inv
        base_ref[at] = (
            0.5 * cap * slope_ref[at] + through + gdev * tnh + wire * guess - drive_ref[at]
        )


def share_kernel(n, index_ref, base_ref, scale_ref, guess_ref, wire_ref, *rest):
    blocks_in, (share_ref, near_ref, pool) = rest[: n - 1], rest[n - 1 :]
    blocks = guess_ref.shape[0]
    start = 0
    for ref in blocks_in:
        for slot in range(ref.shape[0]):
            pool[start + slot] = ref[slot]
        start += ref.shape[0]
    share = jnp.zeros(share_ref.shape, F32)
    for at in range(blocks):
        index = index_ref[at]
        own = index < 0
        near = guess_ref[jnp.where(own, index + blocks, 0)]
        near = jnp.where(own, near, pool[jnp.maximum(index, 0)])
        near_ref[at] = near
        share = share + scale_ref[at] * (base_ref[at] - wire_ref[at : at + 1, :] * near)
    share_ref[...] = share


def residual_kernel(parts, near_ref, base_ref, inv_ref, guess_ref, wire_ref, partial_ref, out_ref, held, sems):
    step = guess_ref.shape[0] // parts
    copies = []
    for part in range(parts):
        for at in range(part * step, (part + 1) * step):
            residual = base_ref[at] - wire_ref[at : at + 1, :] * near_ref[at]
            held[at] = residual
            partial_ref[at] = guess_ref[at] - residual * inv_ref[at]
        some = pl.ds(part * step, step)
        copies.append(pltpu.make_async_copy(held.at[some], out_ref.at[some], sems.at[part]))
        copies[-1].start()
    for copy in copies:
        copy.wait()


def update_kernel(m, parts, *rest):
    shares, (whole_ref, partial_ref, scale_ref, updated_ref, held, sems) = rest[:m], rest[m:]
    total = shares[0][...]
    for share in shares[1:]:
        total = total + share[...]
    nodes = total.shape[1]
    high, low = cut(total)
    region = jnp.dot(high, whole_ref[:nodes, :], preferred_element_type=F32)
    region += jnp.dot(low, whole_ref[:nodes, :], preferred_element_type=F32)
    region += jnp.dot(high, whole_ref[nodes:, :], preferred_element_type=F32)
    step = partial_ref.shape[0] // parts
    copies = []
    for part in range(parts):
        for at in range(part * step, (part + 1) * step):
            held[at] = partial_ref[at] + scale_ref[at] * region
        span = pl.ds(part * step, step)
        copies.append(pltpu.make_async_copy(held.at[span], updated_ref.at[span], sems.at[part]))
        copies[-1].start()
    for copy in copies:
        copy.wait()


def call(body, outs, ins, in_specs, out_specs, scratch=(), limit=8):
    return pl.pallas_call(
        body,
        out_shape=outs,
        in_specs=in_specs,
        out_specs=out_specs,
        scratch_shapes=list(scratch),
        compiler_params=pltpu.CompilerParams(vmem_limit_bytes=limit << 20),
        cost_estimate=pl.CostEstimate(flops=0, bytes_accessed=0, transcendentals=0),
    )(*ins)


def in_hbm(x):
    return pltpu.with_memory_space_constraint(x, pltpu.HBM)


def swap(x, axes, n, k):
    return lax.ppermute(x, axes, [(d, d ^ k) for d in range(n)])


def shards(
    history,
    new_slot,
    partner,
    coupling,
    cap_rate,
    device_gain,
    wire_gain,
    region_gain,
    drive,
    region_inverse,
):
    blocks, _, scen, nodes = history.shape
    n = lax.axis_size("die")
    nblk = lax.axis_size("blk")
    ncol = lax.axis_size("sub") * nblk
    for size in (n, nblk, ncol):
        assert size & (size - 1) == 0
    assert blocks <= 32
    rcap = 2 * max(1, blocks // n)
    span = ncol * blocks

    def tiles(count):
        return jax.ShapeDtypeStruct((count, scen, nodes), F32)

    def scalars(count):
        return pltpu.SMEM((count,), I32)

    block = tiles(blocks)
    square = jax.ShapeDtypeStruct((2 * nodes, nodes), jnp.bfloat16)
    rows = region_inverse[0]
    message = jax.ShapeDtypeStruct((2 * CAP * scen + 8, nodes), F32)

    rounds = [*range(2, n), 1]
    new_slot, partner = in_hbm(new_slot), in_hbm(partner)
    raw, rows, *leaving = call(
        functools.partial(leave_kernel, rounds, span),
        [jax.ShapeDtypeStruct(history.shape, F32), jax.ShapeDtypeStruct(rows.shape, F32)]
        + [message] * (n - 1),
        [new_slot, partner, in_hbm(history), in_hbm(rows)],
        [HBM] * 4,
        [VMEM] * (n + 1),
        [scalars(blocks)] * 2
        + [scalars(n)]
        + [scalars(n * CAP)] * 2
        + [scalars(n), pltpu.SemaphoreType.DMA((7,))],
    )
    arrived = [swap(x, "die", n, k) for x, k in zip(leaving, rounds)]
    inverses = [rows] + [swap(rows, "blk", nblk, k) for k in range(1, nblk)]
    old_guess, old_slope = call(
        functools.partial(place_kernel, span),
        [block, block],
        [new_slot, raw],
        [HBM, VMEM],
        [VMEM, VMEM],
        [scalars(blocks), pltpu.SemaphoreType.DMA],
    )
    guess, slopes, whole, *served = call(
        functools.partial(serve_kernel, n, nblk),
        [block, block, square] + [tiles(rcap)] * (n - 1),
        [*arrived, *inverses, old_guess, old_slope],
        [VMEM] * (n - 1 + nblk + 2),
        [VMEM] * (n + 2),
        [
            pltpu.VMEM((n - 1, 8, nodes), I32),
            pltpu.SMEM((n - 1, 8, nodes), I32),
            pltpu.SemaphoreType.DMA,
        ],
    )
    others = [swap(x, "die", n, k) for x, k in zip(served, rounds)]
    (index,) = call(
        functools.partial(where_kernel, rounds, span, rcap),
        [jax.ShapeDtypeStruct((blocks,), I32)],
        [partner, guess],
        [HBM, ANY],
        [SMEM],
        [scalars(blocks), scalars(n), scalars(n), pltpu.SemaphoreType.DMA],
    )
    step = 8 if blocks % 8 == 0 else blocks
    wide = pl.BlockSpec((step, scen, nodes), lambda i: (i, 0, 0))
    flat = pl.BlockSpec((step, nodes), lambda i: (i, 0))
    base, inv, scale, wire = pl.pallas_call(
        local_kernel,
        grid=(blocks // step,),
        out_shape=[block, block, block, jax.ShapeDtypeStruct((blocks, nodes), F32)],
        in_specs=[
            wide,
            wide,
            pl.BlockSpec((step, nodes, nodes), lambda i: (i, 0, 0)),
            flat,
            flat,
            flat,
            flat,
            wide,
        ],
        out_specs=[wide, wide, wide, flat],
        compiler_params=pltpu.CompilerParams(vmem_limit_bytes=8 << 20),
        cost_estimate=pl.CostEstimate(flops=0, bytes_accessed=0, transcendentals=0),
    )(
        guess,
        slopes,
        in_hbm(coupling),
        in_hbm(cap_rate),
        in_hbm(device_gain),
        in_hbm(wire_gain),
        in_hbm(region_gain),
        in_hbm(drive),
    )
    share, near = call(
        functools.partial(share_kernel, n),
        [jax.ShapeDtypeStruct((scen, nodes), F32), block],
        [index, base, scale, guess, wire, *others],
        [SMEM] + [VMEM] * (4 + n - 1),
        [VMEM] * 2,
        [pltpu.VMEM(((n - 1) * rcap, scen, nodes), F32)],
    )
    parts = 4 if blocks % 4 == 0 else 1
    partial, residual = call(
        functools.partial(residual_kernel, parts),
        [block, block],
        [near, base, inv, guess, wire],
        [VMEM] * 5,
        [VMEM, HBM],
        [pltpu.VMEM((blocks, scen, nodes), F32), pltpu.SemaphoreType.DMA((parts,))],
    )
    shares = [share] + [swap(share, ("sub", "blk"), ncol, k) for k in range(1, ncol)]
    (updated,) = call(
        functools.partial(update_kernel, ncol, parts),
        [block],
        [*shares, whole, partial, scale],
        [VMEM] * (ncol + 3),
        [HBM],
        [pltpu.VMEM((blocks, scen, nodes), F32), pltpu.SemaphoreType.DMA((parts,))],
    )
    return (updated, residual)


def solution(mesh):
    every = ("grp", "die", "sub", "blk")
    in_specs = (
        P(every, None, None, None),
        P(every),
        P(every),
        P(every, None, None),
        P(every, None),
        P(every, None),
        P(every, None),
        P(every, None),
        P(every, None, None),
        P(("grp", "die"), "blk", None),
    )
    out_specs = (P(every, None, None), P(every, None, None))
    return jax.shard_map(shards, mesh=mesh, in_specs=in_specs, out_specs=out_specs, check_vma=False)
```

```python
import functools

import jax
import jax.numpy as jnp
from jax import lax
from jax.experimental import pallas as pl
from jax.experimental.pallas import tpu as pltpu
from jax.sharding import PartitionSpec as P

CAP = 2
VMEM = pl.BlockSpec(memory_space=pltpu.VMEM)
SMEM = pl.BlockSpec(memory_space=pltpu.SMEM)
ANY = pl.BlockSpec(memory_space=pl.ANY)
HBM = pl.BlockSpec(memory_space=pltpu.HBM)
F32 = jnp.float32
I32 = jnp.int32


def divmod_static(value, size):
    if size & (size - 1) == 0:
        return lax.shift_right_logical(value, size.bit_length() - 1), value & (size - 1)
    whole = lax.div(value, size)
    return whole, value - whole * size


def bit_of(index):
    return lax.shift_left(jnp.int32(1), index)


def bits_set(x):
    x = x - (lax.shift_right_logical(x, 1) & 0x55555555)
    x = (x & 0x33333333) + (lax.shift_right_logical(x, 2) & 0x33333333)
    x = (x + lax.shift_right_logical(x, 4)) & 0x0F0F0F0F
    x = x + lax.shift_right_logical(x, 8)
    x = x + lax.shift_right_logical(x, 16)
    return x & 63


def lowest(mask):
    return jnp.maximum(31 - lax.clz(mask & -mask), 0)


def halves(mask):
    return [mask & 0xFFFF, lax.shift_right_logical(mask, 16)]


def joined(low, high):
    return low | lax.shift_left(high, 16)


def predict(raw):
    return 3.0 * raw[0] - 3.0 * raw[1] + raw[2]


def slope(raw, guess):
    return 3.0 * guess - (4.0 * raw[0] - raw[1])


def read_masks(n, span, blocks, reads, mine):
    wants = [jnp.int32(0)] * n
    for at in range(n):
        mine[at] = 0
    for at in range(blocks):
        owner, local = divmod_static(reads[at], span)
        bit = bit_of(divmod_static(local, blocks)[1])
        if n > 8:
            mine[owner] = mine[owner] | bit
        else:
            wants = [want | jnp.where(owner == o, bit, 0) for o, want in enumerate(wants)]
    if n <= 8:
        for at in range(n):
            mine[at] = wants[at]


def leave_kernel(
    rounds, span, new_slot_ref, partner_ref, history_ref, rows_ref, raw_ref, inverse_ref, *rest
):
    n = len(rounds) + 1
    outs, (slots, reads, mine, source, place, count, sems) = rest[: n - 1], rest[n - 1 :]
    blocks, _, scen, nodes = history_ref.shape
    pieces = 4 if blocks % 4 == 0 else 1
    piece = blocks // pieces
    die = lax.axis_index("die")
    copies = [
        pltpu.make_async_copy(new_slot_ref, slots, sems.at[0]),
        pltpu.make_async_copy(partner_ref, reads, sems.at[1]),
        pltpu.make_async_copy(rows_ref, inverse_ref, sems.at[2]),
    ]
    for at in range(pieces):
        some = pl.ds(at * piece, piece)
        copies.append(
            pltpu.make_async_copy(history_ref.at[some], raw_ref.at[some], sems.at[3 + at])
        )
    for copy in copies:
        copy.start()
    for at in range(n):
        count[at] = 0
    for at in range(n * CAP):
        source[at] = 0
        place[at] = -1
    copies[0].wait()
    copies[1].wait()

    for at in range(blocks):
        dest, local = divmod_static(slots[at], span)
        local = divmod_static(local, blocks)[1]

        @pl.when(dest != die)
        def _(at=at, dest=dest, local=local):
            rank = count[dest]
            count[dest] = rank + 1
            turn = (dest ^ die) * CAP + rank
            source[turn] = at
            place[turn] = local

    read_masks(n, span, blocks, reads, mine)
    for copy in copies[2:]:
        copy.wait()
    line = lax.broadcasted_iota(I32, (8, nodes), 0)
    for k, out in zip(rounds, outs):
        for rank in range(CAP):
            raw = raw_ref.at[source[k * CAP + rank]]
            guess = predict(raw)
            out[pl.ds(rank * scen, scen), :] = guess
            out[pl.ds((CAP + rank) * scen, scen), :] = slope(raw, guess)
        row = jnp.zeros((8, nodes), I32)
        values = halves(mine[die ^ k])
        values += [place[k * CAP + rank] for rank in range(CAP)]
        for j, value in enumerate(values):
            row = jnp.where(line == j, value, row)
        out[pl.ds(2 * CAP * scen, 8), :] = row.astype(F32)


def place_kernel(span, new_slot_ref, raw_ref, guess_ref, slope_ref, slots, sem):
    blocks = raw_ref.shape[0]
    die = lax.axis_index("die")
    copy = pltpu.make_async_copy(new_slot_ref, slots, sem)
    copy.start()
    copy.wait()
    for at in range(blocks):
        dest, local = divmod_static(slots[at], span)
        local = divmod_static(local, blocks)[1]

        @pl.when(dest == die)
        def _(at=at, local=local):
            raw = raw_ref.at[at]
            guess = predict(raw)
            guess_ref[local] = guess
            slope_ref[local] = slope(raw, guess)


def serve_kernel(picks, nblk, *rest):
    n = len(picks) + 1
    arrived, rest = rest[: n - 1], rest[n - 1 :]
    inverses, rest = rest[:nblk], rest[nblk:]
    old_guess, old_slope, guess_ref, slope_ref, whole_ref, *rest = rest
    outs = rest
    blocks, scen, nodes = guess_ref.shape

    def told(k, j):
        return arrived[k][2 * CAP * scen + j, 0].astype(I32)

    for at in range(blocks):
        guess_ref[at] = old_guess[at]
        slope_ref[at] = old_slope[at]
    height = inverses[0].shape[0]
    for k in range(nblk):
        at = pl.multiple_of((lax.axis_index("blk") ^ k) * height, height)
        whole_ref[pl.ds(at, height), :] = inverses[k][...]
    for k in range(n - 1):
        for rank in range(CAP):
            place = told(k, 2 + rank)

            @pl.when(place >= 0)
            def _(k=k, rank=rank, place=place):
                guess_ref[place] = arrived[k][pl.ds(rank * scen, scen), :]
                slope_ref[place] = arrived[k][pl.ds((CAP + rank) * scen, scen), :]

    for k, out in zip(picks, outs):
        want = joined(told(k, 0), told(k, 1))
        for slot in range(out.shape[0]):
            out[slot] = guess_ref[lowest(want)]
            want = want & (want - 1)


def where_kernel(rounds, span, rcap, last, partner_ref, _, index_ref, late_ref, reads, mine, starts, sem):
    n = len(rounds) + 1
    blocks = index_ref.shape[0]
    die = lax.axis_index("die")
    copy = pltpu.make_async_copy(partner_ref, reads, sem)
    copy.start()
    starts[0] = 0
    for at, k in enumerate(rounds):
        starts[k] = at * rcap
    copy.wait()
    read_masks(n, span, blocks, reads, mine)

    def step(at, count):
        owner, local = divmod_static(reads[at], span)
        local = divmod_static(local, blocks)[1]
        k = owner ^ die
        slot = bits_set(mine[owner] & (bit_of(local) - 1))
        index_ref[at] = jnp.where(k == 0, local - blocks, starts[k] + slot)
        late_ref[1 + count] = at
        return count + jnp.where(k == rounds[last], 1, 0)

    for at in range(1 + blocks):
        late_ref[at] = 0
    late_ref[0] = lax.fori_loop(0, blocks, step, jnp.int32(0))


def local_kernel(
    guess_ref, slope_ref, coupling_ref, cap_ref, gdev_ref, wire_ref, gain_ref, drive_ref,
    base_ref, inv_ref, scale_ref, kept_ref
):
    nodes = coupling_ref.shape[1]
    rows = lax.broadcasted_iota(I32, (nodes, nodes), 0)
    cols = lax.broadcasted_iota(I32, (nodes, nodes), 1)
    for at in range(guess_ref.shape[0]):
        guess = guess_ref[at]
        coupling = coupling_ref[at]
        cap = cap_ref[at : at + 1, :]
        gdev = gdev_ref[at : at + 1, :]
        wire = wire_ref[at : at + 1, :]
        through = lax.dot_general(
            guess,
            coupling,
            (((1,), (1,)), ((), ())),
            precision=lax.Precision.HIGHEST,
            preferred_element_type=F32,
        )
        diagonal = jnp.sum(jnp.where(rows == cols, coupling, 0.0), axis=0, keepdims=True)
        tnh = jnp.tanh(guess)
        inv = 1.0 / (1.5 * cap + diagonal + gdev * (1.0 - tnh * tnh) + wire)
        inv_ref[at] = inv
        kept_ref[at : at + 1, :] = wire
        scale_ref[at] = gain_ref[at : at + 1, :] * inv
        base_ref[at] = (
            0.5 * cap * slope_ref[at] + through + gdev * tnh + wire * guess - drive_ref[at]
        )


def gather_kernel(rcap, last, index_ref, base_ref, scale_ref, guess_ref, wire_ref, *rest):
    blocks_in, (near_ref, share_ref, pool) = rest[:-3], rest[-3:]
    blocks = guess_ref.shape[0]
    for at, ref in enumerate(blocks_in):
        for slot in range(rcap):
            pool[(at + (at >= last)) * rcap + slot] = ref[slot]
    share = jnp.zeros(share_ref.shape, F32)
    for at in range(blocks):
        index = index_ref[at]
        own = index < 0
        near = guess_ref[jnp.where(own, index + blocks, 0)]
        near = jnp.where(own, near, pool[jnp.maximum(index, 0)])
        missing = (index >= last * rcap) & (index < (last + 1) * rcap)
        near = jnp.where(missing, 0.0, near)
        near_ref[at] = near
        share = share + scale_ref[at] * (base_ref[at] - wire_ref[at : at + 1, :] * near)
    share_ref[...] = share


def share_kernel(rcap, last, index_ref, late_ref, scale_ref, wire_ref, part_ref, block_ref, share_ref):
    share = part_ref[...]
    for slot in range(min(rcap, wire_ref.shape[0])):
        at = late_ref[1 + slot]
        there = slot < late_ref[0]
        block = block_ref[jnp.where(there, index_ref[at] - last * rcap, 0)]
        share = share - jnp.where(there, scale_ref[at] * wire_ref[pl.ds(at, 1), :] * block, 0.0)
    share_ref[...] = share


def residual_kernel(
    rcap, last, parts, index_ref, near_ref, block_ref, base_ref, inv_ref, guess_ref, wire_ref,
    partial_ref, out_ref, held, sems
):
    step = guess_ref.shape[0] // parts
    copies = []
    for part in range(parts):
        for at in range(part * step, (part + 1) * step):
            slot = index_ref[at] - last * rcap
            missing = (slot >= 0) & (slot < rcap)
            near = jnp.where(missing, block_ref[jnp.where(missing, slot, 0)], near_ref[at])
            residual = base_ref[at] - wire_ref[at : at + 1, :] * near
            held[at] = residual
            partial_ref[at] = guess_ref[at] - residual * inv_ref[at]
        some = pl.ds(part * step, step)
        copies.append(pltpu.make_async_copy(held.at[some], out_ref.at[some], sems.at[part]))
        copies[-1].start(priority=part % 2)
    for copy in copies:
        copy.wait()


def update_kernel(m, parts, *rest):
    shares, (whole_ref, partial_ref, scale_ref, updated_ref, held, sems) = rest[:m], rest[m:]
    total = shares[0][...]
    for share in shares[1:]:
        total = total + share[...]
    region = jnp.dot(
        total, whole_ref[...], precision=lax.Precision.HIGHEST, preferred_element_type=F32
    )
    step = partial_ref.shape[0] // parts
    copies = []
    for part in range(parts):
        for at in range(part * step, (part + 1) * step):
            held[at] = partial_ref[at] + scale_ref[at] * region
        span = pl.ds(part * step, step)
        copies.append(pltpu.make_async_copy(held.at[span], updated_ref.at[span], sems.at[part]))
        copies[-1].start(priority=part % 2)
    for copy in copies:
        copy.wait()


def call(body, outs, ins, in_specs, out_specs, scratch=(), limit=8):
    return pl.pallas_call(
        body,
        out_shape=outs,
        in_specs=in_specs,
        out_specs=out_specs,
        scratch_shapes=list(scratch),
        compiler_params=pltpu.CompilerParams(vmem_limit_bytes=limit << 20),
        cost_estimate=pl.CostEstimate(flops=0, bytes_accessed=0, transcendentals=0),
    )(*ins)


def in_hbm(x):
    return pltpu.with_memory_space_constraint(x, pltpu.HBM)


def swap(x, axes, n, k):
    return lax.ppermute(x, axes, [(d, d ^ k) for d in range(n)])


def shards(
    history,
    new_slot,
    partner,
    coupling,
    cap_rate,
    device_gain,
    wire_gain,
    region_gain,
    drive,
    region_inverse,
):
    blocks, _, scen, nodes = history.shape
    n = lax.axis_size("die")
    nblk = lax.axis_size("blk")
    ncol = lax.axis_size("sub") * nblk
    for size in (n, nblk, ncol):
        assert size & (size - 1) == 0
    assert blocks <= 32
    rcap = 2 * max(1, blocks // n)
    span = ncol * blocks

    def tiles(count):
        return jax.ShapeDtypeStruct((count, scen, nodes), F32)

    def scalars(count):
        return pltpu.SMEM((count,), I32)

    block = tiles(blocks)
    square = jax.ShapeDtypeStruct((nodes, nodes), F32)
    rows = region_inverse[0]
    message = jax.ShapeDtypeStruct((2 * CAP * scen + 8, nodes), F32)

    rounds = [*range(2, n), 1]
    replies = [*range(n - 1, 2, -1), 1, 2] if n > 2 else [1]
    new_slot, partner = in_hbm(new_slot), in_hbm(partner)
    raw, rows, *leaving = call(
        functools.partial(leave_kernel, rounds, span),
        [jax.ShapeDtypeStruct(history.shape, F32), jax.ShapeDtypeStruct(rows.shape, F32)]
        + [message] * (n - 1),
        [new_slot, partner, in_hbm(history), in_hbm(rows)],
        [HBM] * 4,
        [VMEM] * (n + 1),
        [scalars(blocks)] * 2
        + [scalars(n)]
        + [scalars(n * CAP)] * 2
        + [scalars(n), pltpu.SemaphoreType.DMA((7,))],
    )
    arrived = [swap(x, "die", n, k) for x, k in zip(leaving, rounds)]
    inverses = [rows] + [swap(rows, "blk", nblk, k) for k in range(1, nblk)]
    old_guess, old_slope = call(
        functools.partial(place_kernel, span),
        [block, block],
        [new_slot, raw],
        [HBM, VMEM],
        [VMEM, VMEM],
        [scalars(blocks), pltpu.SemaphoreType.DMA],
    )
    guess, slopes, whole, *served = call(
        functools.partial(serve_kernel, [rounds.index(k) for k in replies], nblk),
        [block, block, square] + [tiles(rcap)] * (n - 1),
        [*arrived, *inverses, old_guess, old_slope],
        [VMEM] * (n - 1 + nblk + 2),
        [VMEM] * (n + 2),
    )
    others = [swap(x, "die", n, k) for x, k in zip(served, replies)]
    last = n - 2
    index, late = call(
        functools.partial(where_kernel, replies, span, rcap, last),
        [scalars(blocks), scalars(1 + blocks)],
        [partner, guess],
        [HBM, ANY],
        [SMEM, SMEM],
        [scalars(blocks), scalars(n), scalars(n), pltpu.SemaphoreType.DMA],
    )
    step = 8 if blocks % 8 == 0 else blocks
    wide = pl.BlockSpec((step, scen, nodes), lambda i: (i, 0, 0))
    flat = pl.BlockSpec((step, nodes), lambda i: (i, 0))
    base, inv, scale, wire = pl.pallas_call(
        local_kernel,
        grid=(blocks // step,),
        out_shape=[block, block, block, jax.ShapeDtypeStruct((blocks, nodes), F32)],
        in_specs=[
            wide,
            wide,
            pl.BlockSpec((step, nodes, nodes), lambda i: (i, 0, 0)),
            flat,
            flat,
            flat,
            flat,
            wide,
        ],
        out_specs=[wide, wide, wide, flat],
        compiler_params=pltpu.CompilerParams(vmem_limit_bytes=8 << 20),
        cost_estimate=pl.CostEstimate(flops=0, bytes_accessed=0, transcendentals=0),
    )(
        guess,
        slopes,
        in_hbm(coupling),
        in_hbm(cap_rate),
        in_hbm(device_gain),
        in_hbm(wire_gain),
        in_hbm(region_gain),
        in_hbm(drive),
    )
    index = pltpu.with_memory_space_constraint(index, pltpu.SMEM)
    late = pltpu.with_memory_space_constraint(late, pltpu.SMEM)
    flat_share = jax.ShapeDtypeStruct((scen, nodes), F32)
    first = others[:last] + others[last + 1 :]
    near, part = call(
        functools.partial(gather_kernel, rcap, last),
        [block, flat_share],
        [index, base, scale, guess, wire, *first],
        [SMEM] + [VMEM] * (4 + len(first)),
        [VMEM] * 2,
        [pltpu.VMEM(((n - 1) * rcap, scen, nodes), F32)],
    )
    (share,) = call(
        functools.partial(share_kernel, rcap, last),
        [flat_share],
        [index, late, scale, wire, part, others[last]],
        [SMEM] * 2 + [VMEM] * 4,
        [VMEM],
    )
    parts = 8 if blocks % 8 == 0 else 1
    partial, residual = call(
        functools.partial(residual_kernel, rcap, last, parts),
        [block, block],
        [index, near, others[last], base, inv, guess, wire],
        [SMEM] + [VMEM] * 6,
        [VMEM, HBM],
        [pltpu.VMEM((blocks, scen, nodes), F32), pltpu.SemaphoreType.DMA((parts,))],
    )
    shares = [share] + [swap(share, ("sub", "blk"), ncol, k) for k in range(1, ncol)]
    (updated,) = call(
        functools.partial(update_kernel, ncol, parts),
        [block],
        [*shares, whole, partial, scale],
        [VMEM] * (ncol + 3),
        [HBM],
        [pltpu.VMEM((blocks, scen, nodes), F32), pltpu.SemaphoreType.DMA((parts,))],
    )
    return (updated, residual)


def solution(mesh):
    every = ("grp", "die", "sub", "blk")
    in_specs = (
        P(every, None, None, None),
        P(every),
        P(every),
        P(every, None, None),
        P(every, None),
        P(every, None),
        P(every, None),
        P(every, None),
        P(every, None, None),
        P(("grp", "die"), "blk", None),
    )
    out_specs = (P(every, None, None), P(every, None, None))
    return jax.shard_map(shards, mesh=mesh, in_specs=in_specs, out_specs=out_specs, check_vma=False)
```

```python
import functools

import jax
import jax.numpy as jnp
from jax import lax
from jax.experimental import pallas as pl
from jax.experimental.pallas import tpu as pltpu
from jax.sharding import PartitionSpec as P

CAP = 2
VMEM = pl.BlockSpec(memory_space=pltpu.VMEM)
SMEM = pl.BlockSpec(memory_space=pltpu.SMEM)
ANY = pl.BlockSpec(memory_space=pl.ANY)
HBM = pl.BlockSpec(memory_space=pltpu.HBM)
F32 = jnp.float32
I32 = jnp.int32


def divmod_static(value, size):
    if size & (size - 1) == 0:
        return lax.shift_right_logical(value, size.bit_length() - 1), value & (size - 1)
    whole = lax.div(value, size)
    return whole, value - whole * size


def bit_of(index):
    return lax.shift_left(jnp.int32(1), index)


def bits_set(x):
    x = x - (lax.shift_right_logical(x, 1) & 0x55555555)
    x = (x & 0x33333333) + (lax.shift_right_logical(x, 2) & 0x33333333)
    x = (x + lax.shift_right_logical(x, 4)) & 0x0F0F0F0F
    x = x + lax.shift_right_logical(x, 8)
    x = x + lax.shift_right_logical(x, 16)
    return x & 63


def lowest(mask):
    return jnp.maximum(31 - lax.clz(mask & -mask), 0)


def halves(mask):
    return [mask & 0xFFFF, lax.shift_right_logical(mask, 16)]


def joined(low, high):
    return low | lax.shift_left(high, 16)


def predict(raw):
    return 3.0 * raw[0] - 3.0 * raw[1] + raw[2]


def slope(raw, guess):
    return 3.0 * guess - (4.0 * raw[0] - raw[1])


def read_masks(n, span, blocks, reads, mine):
    wants = [jnp.int32(0)] * n
    for at in range(n):
        mine[at] = 0
    for at in range(blocks):
        owner, local = divmod_static(reads[at], span)
        bit = bit_of(divmod_static(local, blocks)[1])
        if n > 8:
            mine[owner] = mine[owner] | bit
        else:
            wants = [want | jnp.where(owner == o, bit, 0) for o, want in enumerate(wants)]
    if n <= 8:
        for at in range(n):
            mine[at] = wants[at]


def leave_kernel(
    rounds, span, new_slot_ref, partner_ref, history_ref, rows_ref, raw_ref, inverse_ref, *rest
):
    n = len(rounds) + 1
    outs, (slots, reads, mine, source, place, count, sems) = rest[: n - 1], rest[n - 1 :]
    blocks, _, scen, nodes = history_ref.shape
    pieces = 4 if blocks % 4 == 0 else 1
    piece = blocks // pieces
    die = lax.axis_index("die")
    copies = [
        pltpu.make_async_copy(new_slot_ref, slots, sems.at[0]),
        pltpu.make_async_copy(partner_ref, reads, sems.at[1]),
        pltpu.make_async_copy(rows_ref, inverse_ref, sems.at[2]),
    ]
    for at in range(pieces):
        some = pl.ds(at * piece, piece)
        copies.append(
            pltpu.make_async_copy(history_ref.at[some], raw_ref.at[some], sems.at[3 + at])
        )
    for copy in copies:
        copy.start()
    for at in range(n):
        count[at] = 0
    for at in range(n * CAP):
        source[at] = 0
        place[at] = -1
    copies[0].wait()
    copies[1].wait()

    for at in range(blocks):
        dest, local = divmod_static(slots[at], span)
        local = divmod_static(local, blocks)[1]

        @pl.when(dest != die)
        def _(at=at, dest=dest, local=local):
            rank = count[dest]
            count[dest] = rank + 1
            turn = (dest ^ die) * CAP + rank
            source[turn] = at
            place[turn] = local

    read_masks(n, span, blocks, reads, mine)
    for copy in copies[2:]:
        copy.wait()
    line = lax.broadcasted_iota(I32, (8, nodes), 0)
    for k, out in zip(rounds, outs):
        for rank in range(CAP):
            raw = raw_ref.at[source[k * CAP + rank]]
            guess = predict(raw)
            out[pl.ds(rank * scen, scen), :] = guess
            out[pl.ds((CAP + rank) * scen, scen), :] = slope(raw, guess)
        row = jnp.zeros((8, nodes), I32)
        values = halves(mine[die ^ k])
        values += [place[k * CAP + rank] for rank in range(CAP)]
        for j, value in enumerate(values):
            row = jnp.where(line == j, value, row)
        out[pl.ds(2 * CAP * scen, 8), :] = row.astype(F32)


def place_kernel(span, new_slot_ref, raw_ref, guess_ref, slope_ref, slots, sem):
    blocks = raw_ref.shape[0]
    die = lax.axis_index("die")
    copy = pltpu.make_async_copy(new_slot_ref, slots, sem)
    copy.start()
    copy.wait()
    for at in range(blocks):
        dest, local = divmod_static(slots[at], span)
        local = divmod_static(local, blocks)[1]

        @pl.when(dest == die)
        def _(at=at, local=local):
            raw = raw_ref.at[at]
            guess = predict(raw)
            guess_ref[local] = guess
            slope_ref[local] = slope(raw, guess)


def serve_kernel(n, nblk, *rest):
    arrived, rest = rest[: n - 1], rest[n - 1 :]
    inverses, rest = rest[:nblk], rest[nblk:]
    old_guess, old_slope, guess_ref, slope_ref, whole_ref, *rest = rest
    outs = rest
    blocks, scen, nodes = guess_ref.shape

    def told(k, j):
        return arrived[k][2 * CAP * scen + j, 0].astype(I32)

    for at in range(blocks):
        guess_ref[at] = old_guess[at]
        slope_ref[at] = old_slope[at]
    height = inverses[0].shape[0]
    for k in range(nblk):
        at = pl.multiple_of((lax.axis_index("blk") ^ k) * height, height)
        whole_ref[pl.ds(at, height), :] = inverses[k][...]
    for k in range(n - 1):
        for rank in range(CAP):
            place = told(k, 2 + rank)

            @pl.when(place >= 0)
            def _(k=k, rank=rank, place=place):
                guess_ref[place] = arrived[k][pl.ds(rank * scen, scen), :]
                slope_ref[place] = arrived[k][pl.ds((CAP + rank) * scen, scen), :]

    for k, out in enumerate(outs):
        want = joined(told(k, 0), told(k, 1))
        for slot in range(out.shape[0]):
            out[slot] = guess_ref[lowest(want)]
            want = want & (want - 1)


def where_kernel(rounds, span, rcap, last, partner_ref, _, index_ref, late_ref, reads, mine, starts, sem):
    n = len(rounds) + 1
    blocks = index_ref.shape[0]
    die = lax.axis_index("die")
    copy = pltpu.make_async_copy(partner_ref, reads, sem)
    copy.start()
    starts[0] = 0
    for at, k in enumerate(rounds):
        starts[k] = at * rcap
    copy.wait()
    read_masks(n, span, blocks, reads, mine)

    def step(at, count):
        owner, local = divmod_static(reads[at], span)
        local = divmod_static(local, blocks)[1]
        k = owner ^ die
        slot = bits_set(mine[owner] & (bit_of(local) - 1))
        index_ref[at] = jnp.where(k == 0, local - blocks, starts[k] + slot)
        late_ref[1 + count] = at
        return count + jnp.where(k == rounds[last], 1, 0)

    for at in range(1 + blocks):
        late_ref[at] = 0
    late_ref[0] = lax.fori_loop(0, blocks, step, jnp.int32(0))


def local_kernel(
    guess_ref, slope_ref, coupling_ref, cap_ref, gdev_ref, wire_ref, gain_ref, drive_ref,
    base_ref, inv_ref, scale_ref, kept_ref
):
    nodes = coupling_ref.shape[1]
    rows = lax.broadcasted_iota(I32, (nodes, nodes), 0)
    cols = lax.broadcasted_iota(I32, (nodes, nodes), 1)
    for at in range(guess_ref.shape[0]):
        guess = guess_ref[at]
        coupling = coupling_ref[at]
        cap = cap_ref[at : at + 1, :]
        gdev = gdev_ref[at : at + 1, :]
        wire = wire_ref[at : at + 1, :]
        through = lax.dot_general(
            guess,
            coupling,
            (((1,), (1,)), ((), ())),
            precision=lax.Precision.HIGHEST,
            preferred_element_type=F32,
        )
        diagonal = jnp.sum(jnp.where(rows == cols, coupling, 0.0), axis=0, keepdims=True)
        tnh = jnp.tanh(guess)
        inv = 1.0 / (1.5 * cap + diagonal + gdev * (1.0 - tnh * tnh) + wire)
        inv_ref[at] = inv
        kept_ref[at : at + 1, :] = wire
        scale_ref[at] = gain_ref[at : at + 1, :] * inv
        base_ref[at] = (
            0.5 * cap * slope_ref[at] + through + gdev * tnh + wire * guess - drive_ref[at]
        )


def gather_kernel(rcap, last, index_ref, base_ref, scale_ref, guess_ref, wire_ref, *rest):
    blocks_in, (near_ref, share_ref, pool) = rest[:-3], rest[-3:]
    blocks = guess_ref.shape[0]
    for at, ref in enumerate(blocks_in):
        for slot in range(rcap):
            pool[(at + (at >= last)) * rcap + slot] = ref[slot]
    share = jnp.zeros(share_ref.shape, F32)
    for at in range(blocks):
        index = index_ref[at]
        own = index < 0
        near = guess_ref[jnp.where(own, index + blocks, 0)]
        near = jnp.where(own, near, pool[jnp.maximum(index, 0)])
        missing = (index >= last * rcap) & (index < (last + 1) * rcap)
        near = jnp.where(missing, 0.0, near)
        near_ref[at] = near
        share = share + scale_ref[at] * (base_ref[at] - wire_ref[at : at + 1, :] * near)
    share_ref[...] = share


def share_kernel(rcap, last, index_ref, late_ref, scale_ref, wire_ref, part_ref, block_ref, share_ref):
    share = part_ref[...]
    for slot in range(min(rcap, wire_ref.shape[0])):
        at = late_ref[1 + slot]
        there = slot < late_ref[0]
        block = block_ref[jnp.where(there, index_ref[at] - last * rcap, 0)]
        share = share - jnp.where(there, scale_ref[at] * wire_ref[pl.ds(at, 1), :] * block, 0.0)
    share_ref[...] = share


def residual_kernel(
    rcap, last, parts, index_ref, near_ref, block_ref, base_ref, inv_ref, guess_ref, wire_ref,
    partial_ref, out_ref, held, sems
):
    step = guess_ref.shape[0] // parts
    copies = []
    for part in range(parts):
        for at in range(part * step, (part + 1) * step):
            slot = index_ref[at] - last * rcap
            missing = (slot >= 0) & (slot < rcap)
            near = jnp.where(missing, block_ref[jnp.where(missing, slot, 0)], near_ref[at])
            residual = base_ref[at] - wire_ref[at : at + 1, :] * near
            held[at] = residual
            partial_ref[at] = guess_ref[at] - residual * inv_ref[at]
        some = pl.ds(part * step, step)
        copies.append(pltpu.make_async_copy(held.at[some], out_ref.at[some], sems.at[part]))
        copies[-1].start(priority=part % 2)
    for copy in copies:
        copy.wait()


def update_kernel(m, parts, *rest):
    shares, (whole_ref, partial_ref, scale_ref, updated_ref, held, sems) = rest[:m], rest[m:]
    total = shares[0][...]
    for share in shares[1:]:
        total = total + share[...]
    region = jnp.dot(
        total, whole_ref[...], precision=lax.Precision.HIGHEST, preferred_element_type=F32
    )
    step = partial_ref.shape[0] // parts
    copies = []
    for part in range(parts):
        for at in range(part * step, (part + 1) * step):
            held[at] = partial_ref[at] + scale_ref[at] * region
        span = pl.ds(part * step, step)
        copies.append(pltpu.make_async_copy(held.at[span], updated_ref.at[span], sems.at[part]))
        copies[-1].start(priority=part % 2)
    for copy in copies:
        copy.wait()


def call(body, outs, ins, in_specs, out_specs, scratch=(), limit=8):
    return pl.pallas_call(
        body,
        out_shape=outs,
        in_specs=in_specs,
        out_specs=out_specs,
        scratch_shapes=list(scratch),
        compiler_params=pltpu.CompilerParams(vmem_limit_bytes=limit << 20),
        cost_estimate=pl.CostEstimate(flops=0, bytes_accessed=0, transcendentals=0),
    )(*ins)


def in_hbm(x):
    return pltpu.with_memory_space_constraint(x, pltpu.HBM)


def swap(x, axes, n, k):
    return lax.ppermute(x, axes, [(d, d ^ k) for d in range(n)])


def shards(
    history,
    new_slot,
    partner,
    coupling,
    cap_rate,
    device_gain,
    wire_gain,
    region_gain,
    drive,
    region_inverse,
):
    blocks, _, scen, nodes = history.shape
    n = lax.axis_size("die")
    nblk = lax.axis_size("blk")
    ncol = lax.axis_size("sub") * nblk
    for size in (n, nblk, ncol):
        assert size & (size - 1) == 0
    assert blocks <= 32
    rcap = 2 * max(1, blocks // n)
    span = ncol * blocks

    def tiles(count):
        return jax.ShapeDtypeStruct((count, scen, nodes), F32)

    def scalars(count):
        return pltpu.SMEM((count,), I32)

    block = tiles(blocks)
    square = jax.ShapeDtypeStruct((nodes, nodes), F32)
    rows = region_inverse[0]
    message = jax.ShapeDtypeStruct((2 * CAP * scen + 8, nodes), F32)

    rounds = [*range(2, n), 1]
    new_slot, partner = in_hbm(new_slot), in_hbm(partner)
    raw, rows, *leaving = call(
        functools.partial(leave_kernel, rounds, span),
        [jax.ShapeDtypeStruct(history.shape, F32), jax.ShapeDtypeStruct(rows.shape, F32)]
        + [message] * (n - 1),
        [new_slot, partner, in_hbm(history), in_hbm(rows)],
        [HBM] * 4,
        [VMEM] * (n + 1),
        [scalars(blocks)] * 2
        + [scalars(n)]
        + [scalars(n * CAP)] * 2
        + [scalars(n), pltpu.SemaphoreType.DMA((7,))],
    )
    arrived = [swap(x, "die", n, k) for x, k in zip(leaving, rounds)]
    inverses = [rows] + [swap(rows, "blk", nblk, k) for k in range(1, nblk)]
    old_guess, old_slope = call(
        functools.partial(place_kernel, span),
        [block, block],
        [new_slot, raw],
        [HBM, VMEM],
        [VMEM, VMEM],
        [scalars(blocks), pltpu.SemaphoreType.DMA],
    )
    guess, slopes, whole, *served = call(
        functools.partial(serve_kernel, n, nblk),
        [block, block, square] + [tiles(rcap)] * (n - 1),
        [*arrived, *inverses, old_guess, old_slope],
        [VMEM] * (n - 1 + nblk + 2),
        [VMEM] * (n + 2),
    )
    others = [swap(x, "die", n, k) for x, k in zip(served, rounds)]
    last = n - 2
    index, late = call(
        functools.partial(where_kernel, rounds, span, rcap, last),
        [scalars(blocks), scalars(1 + blocks)],
        [partner, guess],
        [HBM, ANY],
        [SMEM, SMEM],
        [scalars(blocks), scalars(n), scalars(n), pltpu.SemaphoreType.DMA],
    )
    step = 8 if blocks % 8 == 0 else blocks
    wide = pl.BlockSpec((step, scen, nodes), lambda i: (i, 0, 0))
    flat = pl.BlockSpec((step, nodes), lambda i: (i, 0))
    base, inv, scale, wire = pl.pallas_call(
        local_kernel,
        grid=(blocks // step,),
        out_shape=[block, block, block, jax.ShapeDtypeStruct((blocks, nodes), F32)],
        in_specs=[
            wide,
            wide,
            pl.BlockSpec((step, nodes, nodes), lambda i: (i, 0, 0)),
            flat,
            flat,
            flat,
            flat,
            wide,
        ],
        out_specs=[wide, wide, wide, flat],
        compiler_params=pltpu.CompilerParams(vmem_limit_bytes=8 << 20),
        cost_estimate=pl.CostEstimate(flops=0, bytes_accessed=0, transcendentals=0),
    )(
        guess,
        slopes,
        in_hbm(coupling),
        in_hbm(cap_rate),
        in_hbm(device_gain),
        in_hbm(wire_gain),
        in_hbm(region_gain),
        in_hbm(drive),
    )
    index = pltpu.with_memory_space_constraint(index, pltpu.SMEM)
    late = pltpu.with_memory_space_constraint(late, pltpu.SMEM)
    flat_share = jax.ShapeDtypeStruct((scen, nodes), F32)
    first = others[:last] + others[last + 1 :]
    near, part = call(
        functools.partial(gather_kernel, rcap, last),
        [block, flat_share],
        [index, base, scale, guess, wire, *first],
        [SMEM] + [VMEM] * (4 + len(first)),
        [VMEM] * 2,
        [pltpu.VMEM(((n - 1) * rcap, scen, nodes), F32)],
    )
    (share,) = call(
        functools.partial(share_kernel, rcap, last),
        [flat_share],
        [index, late, scale, wire, part, others[last]],
        [SMEM] * 2 + [VMEM] * 4,
        [VMEM],
    )
    parts = 8 if blocks % 8 == 0 else 1
    partial, residual = call(
        functools.partial(residual_kernel, rcap, last, parts),
        [block, block],
        [index, near, others[last], base, inv, guess, wire],
        [SMEM] + [VMEM] * 6,
        [VMEM, HBM],
        [pltpu.VMEM((blocks, scen, nodes), F32), pltpu.SemaphoreType.DMA((parts,))],
    )
    shares = [share] + [swap(share, ("sub", "blk"), ncol, k) for k in range(1, ncol)]
    (updated,) = call(
        functools.partial(update_kernel, ncol, parts),
        [block],
        [*shares, whole, partial, scale],
        [VMEM] * (ncol + 3),
        [HBM],
        [pltpu.VMEM((blocks, scen, nodes), F32), pltpu.SemaphoreType.DMA((parts,))],
    )
    return (updated, residual)


def solution(mesh):
    every = ("grp", "die", "sub", "blk")
    in_specs = (
        P(every, None, None, None),
        P(every),
        P(every),
        P(every, None, None),
        P(every, None),
        P(every, None),
        P(every, None),
        P(every, None),
        P(every, None, None),
        P(("grp", "die"), "blk", None),
    )
    out_specs = (P(every, None, None), P(every, None, None))
    return jax.shard_map(shards, mesh=mesh, in_specs=in_specs, out_specs=out_specs, check_vma=False)
```

```python
import functools

import jax
import jax.numpy as jnp
from jax import lax
from jax.experimental import pallas as pl
from jax.experimental.pallas import tpu as pltpu
from jax.sharding import PartitionSpec as P

CAP = 2
VMEM = pl.BlockSpec(memory_space=pltpu.VMEM)
SMEM = pl.BlockSpec(memory_space=pltpu.SMEM)
ANY = pl.BlockSpec(memory_space=pl.ANY)
HBM = pl.BlockSpec(memory_space=pltpu.HBM)
F32 = jnp.float32
I32 = jnp.int32


def divmod_static(value, size):
    if size & (size - 1) == 0:
        return lax.shift_right_logical(value, size.bit_length() - 1), value & (size - 1)
    whole = lax.div(value, size)
    return whole, value - whole * size


def bit_of(index):
    return lax.shift_left(jnp.int32(1), index)


def bits_set(x):
    x = x - (lax.shift_right_logical(x, 1) & 0x55555555)
    x = (x & 0x33333333) + (lax.shift_right_logical(x, 2) & 0x33333333)
    x = (x + lax.shift_right_logical(x, 4)) & 0x0F0F0F0F
    x = x + lax.shift_right_logical(x, 8)
    x = x + lax.shift_right_logical(x, 16)
    return x & 63


def lowest(mask):
    return jnp.maximum(31 - lax.clz(mask & -mask), 0)


def halves(mask):
    return [mask & 0xFFFF, lax.shift_right_logical(mask, 16)]


def joined(low, high):
    return low | lax.shift_left(high, 16)


def predict(raw):
    return 3.0 * raw[0] - 3.0 * raw[1] + raw[2]


def slope(raw, guess):
    return 3.0 * guess - (4.0 * raw[0] - raw[1])


def read_masks(n, span, blocks, reads, mine):
    wants = [jnp.int32(0)] * n
    for at in range(n):
        mine[at] = 0
    for at in range(blocks):
        owner, local = divmod_static(reads[at], span)
        bit = bit_of(divmod_static(local, blocks)[1])
        if n > 8:
            mine[owner] = mine[owner] | bit
        else:
            wants = [want | jnp.where(owner == o, bit, 0) for o, want in enumerate(wants)]
    if n <= 8:
        for at in range(n):
            mine[at] = wants[at]


def leave_kernel(
    rounds, span, new_slot_ref, partner_ref, history_ref, rows_ref, raw_ref, inverse_ref, *rest
):
    n = len(rounds) + 1
    outs, (slots, reads, sems) = rest[: n - 1], rest[n - 1 :]
    blocks, _, scen, nodes = history_ref.shape
    pieces = 4 if blocks % 4 == 0 else 1
    piece = blocks // pieces
    die = lax.axis_index("die")
    copies = [
        pltpu.make_async_copy(new_slot_ref, slots, sems.at[0]),
        pltpu.make_async_copy(partner_ref, reads, sems.at[1]),
        pltpu.make_async_copy(rows_ref, inverse_ref, sems.at[2]),
    ]
    for at in range(pieces):
        some = pl.ds(at * piece, piece)
        copies.append(
            pltpu.make_async_copy(history_ref.at[some], raw_ref.at[some], sems.at[3 + at])
        )
    for copy in copies:
        copy.start()
    height = max(8, n)
    turn = lax.broadcasted_iota(I32, (height, blocks), 0)
    lane = lax.broadcasted_iota(I32, (height, blocks), 1)
    line = lax.broadcasted_iota(I32, (8, nodes), 0)
    copies[0].wait()
    copies[1].wait()

    dest, local = divmod_static(jnp.broadcast_to(slots[...], (height, blocks)), span)
    local = divmod_static(local, blocks)[1]
    goes = turn == (dest ^ die)
    key = (lane * blocks + local).astype(F32)
    none = float(blocks * blocks)
    least = jnp.min(jnp.where(goes, key, none), axis=1, keepdims=True).astype(I32)
    most = jnp.max(jnp.where(goes, key, -1.0), axis=1, keepdims=True).astype(I32)
    keys = [jnp.where(least < blocks * blocks, least, -1), jnp.where(most > least, most, -1)]
    owner, local = divmod_static(jnp.broadcast_to(reads[...], (height, blocks)), span)
    bits = bit_of(divmod_static(local, blocks)[1])
    bits = jnp.where(turn == (owner ^ die), bits, 0)
    bits = jnp.concatenate([bits, jnp.zeros((height, nodes - blocks), I32)], axis=1)
    shift = 1
    while shift < blocks:
        bits = bits | pltpu.roll(bits, nodes - shift, 1)
        shift *= 2
    values = halves(bits) + [jnp.where(key < 0, -1, key & (blocks - 1)) for key in keys]
    values = [jnp.broadcast_to(value, (height, nodes)) for value in values]
    for k, out in zip(rounds, outs):
        told = jnp.zeros((8, nodes), I32)
        for j, value in enumerate(values):
            told = jnp.where(line == j, value[k : k + 1, :], told)
        out[pl.ds(2 * CAP * scen, 8), :] = told.astype(F32)
    for copy in copies[2:]:
        copy.wait()
    for k, out in zip(rounds, outs):
        for rank, key in enumerate(keys):
            raw = raw_ref.at[lax.shift_right_logical(jnp.maximum(key[k, 0], 0), blocks.bit_length() - 1)]
            guess = predict(raw)
            out[pl.ds(rank * scen, scen), :] = guess
            out[pl.ds((CAP + rank) * scen, scen), :] = slope(raw, guess)


def place_kernel(span, new_slot_ref, raw_ref, guess_ref, slope_ref, slots, sem):
    blocks = raw_ref.shape[0]
    die = lax.axis_index("die")
    copy = pltpu.make_async_copy(new_slot_ref, slots, sem)
    copy.start()
    copy.wait()
    for at in range(blocks):
        dest, local = divmod_static(slots[at], span)
        local = divmod_static(local, blocks)[1]

        @pl.when(dest == die)
        def _(at=at, local=local):
            raw = raw_ref.at[at]
            guess = predict(raw)
            guess_ref[local] = guess
            slope_ref[local] = slope(raw, guess)


def serve_kernel(n, nblk, *rest):
    arrived, rest = rest[: n - 1], rest[n - 1 :]
    inverses, rest = rest[:nblk], rest[nblk:]
    old_guess, old_slope, guess_ref, slope_ref, whole_ref, *rest = rest
    outs = rest
    blocks, scen, nodes = guess_ref.shape

    def told(k, j):
        return arrived[k][2 * CAP * scen + j, 0].astype(I32)

    for at in range(blocks):
        guess_ref[at] = old_guess[at]
        slope_ref[at] = old_slope[at]
    height = inverses[0].shape[0]
    for k in range(nblk):
        at = pl.multiple_of((lax.axis_index("blk") ^ k) * height, height)
        whole_ref[pl.ds(at, height), :] = inverses[k][...]
    for k in range(n - 1):
        for rank in range(CAP):
            place = told(k, 2 + rank)

            @pl.when(place >= 0)
            def _(k=k, rank=rank, place=place):
                guess_ref[place] = arrived[k][pl.ds(rank * scen, scen), :]
                slope_ref[place] = arrived[k][pl.ds((CAP + rank) * scen, scen), :]

    for k, out in enumerate(outs):
        want = joined(told(k, 0), told(k, 1))
        for slot in range(out.shape[0]):
            out[slot] = guess_ref[lowest(want)]
            want = want & (want - 1)


def where_kernel(rounds, span, rcap, last, partner_ref, _, index_ref, late_ref, reads, mine, starts, sem):
    n = len(rounds) + 1
    blocks = index_ref.shape[0]
    die = lax.axis_index("die")
    copy = pltpu.make_async_copy(partner_ref, reads, sem)
    copy.start()
    starts[0] = 0
    for at, k in enumerate(rounds):
        starts[k] = at * rcap
    copy.wait()
    read_masks(n, span, blocks, reads, mine)

    def step(at, count):
        owner, local = divmod_static(reads[at], span)
        local = divmod_static(local, blocks)[1]
        k = owner ^ die
        slot = bits_set(mine[owner] & (bit_of(local) - 1))
        index_ref[at] = jnp.where(k == 0, local - blocks, starts[k] + slot)
        late_ref[1 + count] = at
        return count + jnp.where(k == rounds[last], 1, 0)

    for at in range(1 + blocks):
        late_ref[at] = 0
    late_ref[0] = lax.fori_loop(0, blocks, step, jnp.int32(0))


def local_kernel(
    guess_ref, slope_ref, coupling_ref, cap_ref, gdev_ref, wire_ref, gain_ref, drive_ref,
    base_ref, inv_ref, scale_ref, kept_ref
):
    nodes = coupling_ref.shape[1]
    rows = lax.broadcasted_iota(I32, (nodes, nodes), 0)
    cols = lax.broadcasted_iota(I32, (nodes, nodes), 1)
    for at in range(guess_ref.shape[0]):
        guess = guess_ref[at]
        coupling = coupling_ref[at]
        cap = cap_ref[at : at + 1, :]
        gdev = gdev_ref[at : at + 1, :]
        wire = wire_ref[at : at + 1, :]
        through = lax.dot_general(
            guess,
            coupling,
            (((1,), (1,)), ((), ())),
            precision=lax.Precision.HIGHEST,
            preferred_element_type=F32,
        )
        diagonal = jnp.sum(jnp.where(rows == cols, coupling, 0.0), axis=0, keepdims=True)
        tnh = jnp.tanh(guess)
        inv = 1.0 / (1.5 * cap + diagonal + gdev * (1.0 - tnh * tnh) + wire)
        inv_ref[at] = inv
        kept_ref[at : at + 1, :] = wire
        scale_ref[at] = gain_ref[at : at + 1, :] * inv
        base_ref[at] = (
            0.5 * cap * slope_ref[at] + through + gdev * tnh + wire * guess - drive_ref[at]
        )


def gather_kernel(rcap, last, index_ref, base_ref, scale_ref, guess_ref, wire_ref, *rest):
    blocks_in, (near_ref, share_ref, pool) = rest[:-3], rest[-3:]
    blocks = guess_ref.shape[0]
    for at, ref in enumerate(blocks_in):
        for slot in range(rcap):
            pool[(at + (at >= last)) * rcap + slot] = ref[slot]
    share = jnp.zeros(share_ref.shape, F32)
    for at in range(blocks):
        index = index_ref[at]
        own = index < 0
        near = guess_ref[jnp.where(own, index + blocks, 0)]
        near = jnp.where(own, near, pool[jnp.maximum(index, 0)])
        missing = (index >= last * rcap) & (index < (last + 1) * rcap)
        near = jnp.where(missing, 0.0, near)
        near_ref[at] = near
        share = share + scale_ref[at] * (base_ref[at] - wire_ref[at : at + 1, :] * near)
    share_ref[...] = share


def share_kernel(rcap, last, index_ref, late_ref, scale_ref, wire_ref, part_ref, block_ref, share_ref):
    share = part_ref[...]
    for slot in range(min(rcap, wire_ref.shape[0])):
        at = late_ref[1 + slot]
        there = slot < late_ref[0]
        block = block_ref[jnp.where(there, index_ref[at] - last * rcap, 0)]
        share = share - jnp.where(there, scale_ref[at] * wire_ref[pl.ds(at, 1), :] * block, 0.0)
    share_ref[...] = share


def residual_kernel(
    rcap, last, parts, index_ref, near_ref, block_ref, base_ref, inv_ref, guess_ref, wire_ref,
    partial_ref, out_ref, held, sems
):
    step = guess_ref.shape[0] // parts
    copies = []
    for part in range(parts):
        for at in range(part * step, (part + 1) * step):
            slot = index_ref[at] - last * rcap
            missing = (slot >= 0) & (slot < rcap)
            near = jnp.where(missing, block_ref[jnp.where(missing, slot, 0)], near_ref[at])
            residual = base_ref[at] - wire_ref[at : at + 1, :] * near
            held[at] = residual
            partial_ref[at] = guess_ref[at] - residual * inv_ref[at]
        some = pl.ds(part * step, step)
        copies.append(pltpu.make_async_copy(held.at[some], out_ref.at[some], sems.at[part]))
        copies[-1].start(priority=part % 2)
    for copy in copies:
        copy.wait()


def update_kernel(m, parts, *rest):
    shares, (whole_ref, partial_ref, scale_ref, updated_ref, held, sems) = rest[:m], rest[m:]
    total = shares[0][...]
    for share in shares[1:]:
        total = total + share[...]
    region = jnp.dot(
        total, whole_ref[...], precision=lax.Precision.HIGHEST, preferred_element_type=F32
    )
    step = partial_ref.shape[0] // parts
    copies = []
    for part in range(parts):
        for at in range(part * step, (part + 1) * step):
            held[at] = partial_ref[at] + scale_ref[at] * region
        span = pl.ds(part * step, step)
        copies.append(pltpu.make_async_copy(held.at[span], updated_ref.at[span], sems.at[part]))
        copies[-1].start(priority=part % 2)
    for copy in copies:
        copy.wait()


def call(body, outs, ins, in_specs, out_specs, scratch=(), limit=8):
    return pl.pallas_call(
        body,
        out_shape=outs,
        in_specs=in_specs,
        out_specs=out_specs,
        scratch_shapes=list(scratch),
        compiler_params=pltpu.CompilerParams(vmem_limit_bytes=limit << 20),
        cost_estimate=pl.CostEstimate(flops=0, bytes_accessed=0, transcendentals=0),
    )(*ins)


def in_hbm(x):
    return pltpu.with_memory_space_constraint(x, pltpu.HBM)


def swap(x, axes, n, k):
    return lax.ppermute(x, axes, [(d, d ^ k) for d in range(n)])


def shards(
    history,
    new_slot,
    partner,
    coupling,
    cap_rate,
    device_gain,
    wire_gain,
    region_gain,
    drive,
    region_inverse,
):
    blocks, _, scen, nodes = history.shape
    n = lax.axis_size("die")
    nblk = lax.axis_size("blk")
    ncol = lax.axis_size("sub") * nblk
    for size in (n, nblk, ncol):
        assert size & (size - 1) == 0
    assert CAP == 2 and blocks <= 32 and blocks & (blocks - 1) == 0
    rcap = 2 * max(1, blocks // n)
    span = ncol * blocks

    def tiles(count):
        return jax.ShapeDtypeStruct((count, scen, nodes), F32)

    def scalars(count):
        return pltpu.SMEM((count,), I32)

    block = tiles(blocks)
    square = jax.ShapeDtypeStruct((nodes, nodes), F32)
    rows = region_inverse[0]
    message = jax.ShapeDtypeStruct((2 * CAP * scen + 8, nodes), F32)

    rounds = [*range(2, n), 1]
    raw, rows, *leaving = call(
        functools.partial(leave_kernel, rounds, span),
        [jax.ShapeDtypeStruct(history.shape, F32), jax.ShapeDtypeStruct(rows.shape, F32)]
        + [message] * (n - 1),
        [
            in_hbm(new_slot.reshape(1, blocks)),
            in_hbm(partner.reshape(1, blocks)),
            in_hbm(history),
            in_hbm(rows),
        ],
        [HBM] * 4,
        [VMEM] * (n + 1),
        [pltpu.VMEM((1, blocks), I32)] * 2 + [pltpu.SemaphoreType.DMA((7,))],
    )
    arrived = [swap(x, "die", n, k) for x, k in zip(leaving, rounds)]
    inverses = [rows] + [swap(rows, "blk", nblk, k) for k in range(1, nblk)]
    old_guess, old_slope = call(
        functools.partial(place_kernel, span),
        [block, block],
        [in_hbm(new_slot), raw],
        [HBM, VMEM],
        [VMEM, VMEM],
        [scalars(blocks), pltpu.SemaphoreType.DMA],
    )
    guess, slopes, whole, *served = call(
        functools.partial(serve_kernel, n, nblk),
        [block, block, square] + [tiles(rcap)] * (n - 1),
        [*arrived, *inverses, old_guess, old_slope],
        [VMEM] * (n - 1 + nblk + 2),
        [VMEM] * (n + 2),
    )
    others = [swap(x, "die", n, k) for x, k in zip(served, rounds)]
    last = n - 2
    index, late = call(
        functools.partial(where_kernel, rounds, span, rcap, last),
        [scalars(blocks), scalars(1 + blocks)],
        [in_hbm(partner), guess],
        [HBM, ANY],
        [SMEM, SMEM],
        [scalars(blocks), scalars(n), scalars(n), pltpu.SemaphoreType.DMA],
    )
    step = 8 if blocks % 8 == 0 else blocks
    wide = pl.BlockSpec((step, scen, nodes), lambda i: (i, 0, 0))
    flat = pl.BlockSpec((step, nodes), lambda i: (i, 0))
    base, inv, scale, wire = pl.pallas_call(
        local_kernel,
        grid=(blocks // step,),
        out_shape=[block, block, block, jax.ShapeDtypeStruct((blocks, nodes), F32)],
        in_specs=[
            wide,
            wide,
            pl.BlockSpec((step, nodes, nodes), lambda i: (i, 0, 0)),
            flat,
            flat,
            flat,
            flat,
            wide,
        ],
        out_specs=[wide, wide, wide, flat],
        compiler_params=pltpu.CompilerParams(vmem_limit_bytes=8 << 20),
        cost_estimate=pl.CostEstimate(flops=0, bytes_accessed=0, transcendentals=0),
    )(
        guess,
        slopes,
        in_hbm(coupling),
        in_hbm(cap_rate),
        in_hbm(device_gain),
        in_hbm(wire_gain),
        in_hbm(region_gain),
        in_hbm(drive),
    )
    index = pltpu.with_memory_space_constraint(index, pltpu.SMEM)
    late = pltpu.with_memory_space_constraint(late, pltpu.SMEM)
    flat_share = jax.ShapeDtypeStruct((scen, nodes), F32)
    first = others[:last] + others[last + 1 :]
    near, part = call(
        functools.partial(gather_kernel, rcap, last),
        [block, flat_share],
        [index, base, scale, guess, wire, *first],
        [SMEM] + [VMEM] * (4 + len(first)),
        [VMEM] * 2,
        [pltpu.VMEM(((n - 1) * rcap, scen, nodes), F32)],
    )
    (share,) = call(
        functools.partial(share_kernel, rcap, last),
        [flat_share],
        [index, late, scale, wire, part, others[last]],
        [SMEM] * 2 + [VMEM] * 4,
        [VMEM],
    )
    parts = 8 if blocks % 8 == 0 else 1
    partial, residual = call(
        functools.partial(residual_kernel, rcap, last, parts),
        [block, block],
        [index, near, others[last], base, inv, guess, wire],
        [SMEM] + [VMEM] * 6,
        [VMEM, HBM],
        [pltpu.VMEM((blocks, scen, nodes), F32), pltpu.SemaphoreType.DMA((parts,))],
    )
    shares = [share] + [swap(share, ("sub", "blk"), ncol, k) for k in range(1, ncol)]
    (updated,) = call(
        functools.partial(update_kernel, ncol, parts),
        [block],
        [*shares, whole, partial, scale],
        [VMEM] * (ncol + 3),
        [HBM],
        [pltpu.VMEM((blocks, scen, nodes), F32), pltpu.SemaphoreType.DMA((parts,))],
    )
    return (updated, residual)


def solution(mesh):
    every = ("grp", "die", "sub", "blk")
    in_specs = (
        P(every, None, None, None),
        P(every),
        P(every),
        P(every, None, None),
        P(every, None),
        P(every, None),
        P(every, None),
        P(every, None),
        P(every, None, None),
        P(("grp", "die"), "blk", None),
    )
    out_specs = (P(every, None, None), P(every, None, None))
    return jax.shard_map(shards, mesh=mesh, in_specs=in_specs, out_specs=out_specs, check_vma=False)
```

```python
import functools

import jax
import jax.numpy as jnp
from jax import lax
from jax.experimental import pallas as pl
from jax.experimental.pallas import tpu as pltpu
from jax.sharding import PartitionSpec as P

CAP = 2
VMEM = pl.BlockSpec(memory_space=pltpu.VMEM)
SMEM = pl.BlockSpec(memory_space=pltpu.SMEM)
ANY = pl.BlockSpec(memory_space=pl.ANY)
HBM = pl.BlockSpec(memory_space=pltpu.HBM)
F32 = jnp.float32
I32 = jnp.int32


def divmod_static(value, size):
    if size & (size - 1) == 0:
        return lax.shift_right_logical(value, size.bit_length() - 1), value & (size - 1)
    whole = lax.div(value, size)
    return whole, value - whole * size


def bit_of(index):
    return lax.shift_left(jnp.int32(1), index)


def bits_set(x):
    x = x - (lax.shift_right_logical(x, 1) & 0x55555555)
    x = (x & 0x33333333) + (lax.shift_right_logical(x, 2) & 0x33333333)
    x = (x + lax.shift_right_logical(x, 4)) & 0x0F0F0F0F
    x = x + lax.shift_right_logical(x, 8)
    x = x + lax.shift_right_logical(x, 16)
    return x & 63


def lowest(mask):
    return jnp.maximum(31 - lax.clz(mask & -mask), 0)


def halves(mask):
    return [mask & 0xFFFF, lax.shift_right_logical(mask, 16)]


def joined(low, high):
    return low | lax.shift_left(high, 16)


def predict(raw):
    return 3.0 * raw[0] - 3.0 * raw[1] + raw[2]


def slope(raw, guess):
    return 3.0 * guess - (4.0 * raw[0] - raw[1])


def read_masks(n, span, blocks, reads, mine):
    wants = [jnp.int32(0)] * n
    for at in range(n):
        mine[at] = 0
    for at in range(blocks):
        owner, local = divmod_static(reads[at], span)
        bit = bit_of(divmod_static(local, blocks)[1])
        if n > 8:
            mine[owner] = mine[owner] | bit
        else:
            wants = [want | jnp.where(owner == o, bit, 0) for o, want in enumerate(wants)]
    if n <= 8:
        for at in range(n):
            mine[at] = wants[at]


def leave_kernel(
    rounds, span, new_slot_ref, partner_ref, history_ref, rows_ref, raw_ref, inverse_ref, *rest
):
    n = len(rounds) + 1
    outs, (slots, reads, sems) = rest[: n - 1], rest[n - 1 :]
    blocks, _, scen, nodes = history_ref.shape
    pieces = 4 if blocks % 4 == 0 else 1
    piece = blocks // pieces
    die = lax.axis_index("die")
    copies = [
        pltpu.make_async_copy(new_slot_ref, slots, sems.at[0]),
        pltpu.make_async_copy(partner_ref, reads, sems.at[1]),
        pltpu.make_async_copy(rows_ref, inverse_ref, sems.at[2]),
    ]
    for at in range(pieces):
        some = pl.ds(at * piece, piece)
        copies.append(
            pltpu.make_async_copy(history_ref.at[some], raw_ref.at[some], sems.at[3 + at])
        )
    for copy in copies:
        copy.start()
    height = max(8, n)
    turn = lax.broadcasted_iota(I32, (height, blocks), 0)
    lane = lax.broadcasted_iota(I32, (height, blocks), 1)
    line = lax.broadcasted_iota(I32, (8, nodes), 0)
    copies[0].wait()
    copies[1].wait()

    dest, local = divmod_static(jnp.broadcast_to(slots[...], (height, blocks)), span)
    local = divmod_static(local, blocks)[1]
    goes = turn == (dest ^ die)
    key = (lane * blocks + local).astype(F32)
    none = float(blocks * blocks)
    least = jnp.min(jnp.where(goes, key, none), axis=1, keepdims=True).astype(I32)
    most = jnp.max(jnp.where(goes, key, -1.0), axis=1, keepdims=True).astype(I32)
    keys = [jnp.where(least < blocks * blocks, least, -1), jnp.where(most > least, most, -1)]
    stays = jnp.where(dest == die, bit_of(local), 0)
    owner, local = divmod_static(jnp.broadcast_to(reads[...], (height, blocks)), span)
    bits = bit_of(divmod_static(local, blocks)[1])
    bits = jnp.where(turn == 0, stays, jnp.where(turn == (owner ^ die), bits, 0))
    bits = jnp.concatenate([bits, jnp.zeros((height, nodes - blocks), I32)], axis=1)
    shift = 1
    while shift < blocks:
        bits = bits | pltpu.roll(bits, nodes - shift, 1)
        shift *= 2
    values = halves(bits) + [jnp.where(key < 0, -1, key & (blocks - 1)) for key in keys]
    values = [jnp.broadcast_to(value, (height, nodes)) for value in values]
    taken = halves(~bits)
    for k, out in zip(rounds, outs):
        told = jnp.zeros((8, nodes), I32)
        for j, value in enumerate(values):
            told = jnp.where(line == j, value[k : k + 1, :], told)
        for j, value in enumerate(taken):
            told = jnp.where(line == len(values) + j, value[0:1, :], told)
        out[pl.ds(2 * CAP * scen, 8), :] = told.astype(F32)
    for copy in copies[2:]:
        copy.wait()
    for k, out in zip(rounds, outs):
        for rank, key in enumerate(keys):
            raw = raw_ref.at[lax.shift_right_logical(jnp.maximum(key[k, 0], 0), blocks.bit_length() - 1)]
            guess = predict(raw)
            out[pl.ds(rank * scen, scen), :] = guess
            out[pl.ds((CAP + rank) * scen, scen), :] = slope(raw, guess)


def place_kernel(span, new_slot_ref, raw_ref, guess_ref, slope_ref, slots, sem):
    blocks = raw_ref.shape[0]
    die = lax.axis_index("die")
    copy = pltpu.make_async_copy(new_slot_ref, slots, sem)
    copy.start()
    copy.wait()
    for at in range(blocks):
        dest, local = divmod_static(slots[at], span)
        local = divmod_static(local, blocks)[1]

        @pl.when(dest == die)
        def _(at=at, local=local):
            raw = raw_ref.at[at]
            guess = predict(raw)
            guess_ref[local] = guess
            slope_ref[local] = slope(raw, guess)


def told(message, j):
    return message[message.shape[0] - 8 + j, 0].astype(I32)


def read_by(message):
    return joined(told(message, 0), told(message, 1))


def taken_slots(message):
    return joined(told(message, 2 + CAP), told(message, 3 + CAP))


def early_kernel(message, own_message, guess_ref, out):
    still = read_by(message) & ~taken_slots(own_message)
    for slot in range(out.shape[0]):
        out[slot] = guess_ref[lowest(still)]
        still = still & (still - 1)


def serve_kernel(n, nblk, pieces, depth, rcap, _, own_message, *rest):
    arrived, rest = rest[: n - 1], rest[n - 1 :]
    inverses, rest = rest[:nblk], rest[nblk:]
    old_guess, old_slope, guess_ref, slope_ref, whole_ref, *outs = rest
    blocks, scen, nodes = guess_ref.shape
    for at in range(blocks):
        guess_ref[at] = old_guess[at]
        slope_ref[at] = old_slope[at]
    height = inverses[0].shape[0]
    for k in range(nblk):
        at = pl.multiple_of((lax.axis_index("blk") ^ k) * height, height)
        whole_ref[pl.ds(at, height), :] = inverses[k][...]
    for message in arrived:
        for rank in range(CAP):
            place = told(message, 2 + rank)

            @pl.when(place >= 0)
            def _(message=message, rank=rank, place=place):
                guess_ref[place] = message[pl.ds(rank * scen, scen), :]
                slope_ref[place] = message[pl.ds((CAP + rank) * scen, scen), :]

    taken = taken_slots(own_message)
    want = read_by(arrived[0])
    still, come = want & ~taken, want & taken
    for slot in range(depth):
        still = still & (still - 1)
    out = outs[0]
    for slot in range(rcap - depth):

        @pl.when(still != 0)
        def _(still=still, slot=slot):
            out[slot] = guess_ref[lowest(still)]

        still = still & (still - 1)
    for slot in range(rcap - depth - 1, -1, -1):

        @pl.when(come != 0)
        def _(come=come, slot=slot):
            out[slot] = guess_ref[lowest(come)]

        come = come & (come - 1)
    outs = outs[1:]
    for k in range(1, n - 1):
        want = read_by(arrived[k])
        for out in outs[(k - 1) * pieces : k * pieces]:
            for slot in range(out.shape[0]):
                out[slot] = guess_ref[lowest(want)]
                want = want & (want - 1)


def where_kernel(rounds, span, rcap, partner_ref, message, _, index_ref, reads, mine, starts, sem):
    n = len(rounds) + 1
    blocks = index_ref.shape[0]
    die = lax.axis_index("die")
    copy = pltpu.make_async_copy(partner_ref, reads, sem)
    copy.start()
    starts[0] = 0
    for at, k in enumerate(rounds):
        starts[k] = at * rcap
    copy.wait()
    read_masks(n, span, blocks, reads, mine)
    taken = taken_slots(message)

    def step(at, carry):
        owner, local = divmod_static(reads[at], span)
        local = divmod_static(local, blocks)[1]
        k = owner ^ die
        bit = bit_of(local)
        want = mine[owner]
        come = jnp.where(k == rounds[0], taken, 0)
        low = bits_set(want & ~come & (bit - 1))
        high = rcap - 1 - bits_set(want & come & (bit - 1))
        slot = jnp.where((come & bit) != 0, high, low)
        index_ref[at] = jnp.where(k == 0, local - blocks, starts[k] + slot)
        return carry

    lax.fori_loop(0, blocks, step, 0)


def local_kernel(
    guess_ref, slope_ref, coupling_ref, cap_ref, gdev_ref, wire_ref, gain_ref, drive_ref,
    base_ref, inv_ref, scale_ref, kept_ref
):
    nodes = coupling_ref.shape[1]
    rows = lax.broadcasted_iota(I32, (nodes, nodes), 0)
    cols = lax.broadcasted_iota(I32, (nodes, nodes), 1)
    for at in range(guess_ref.shape[0]):
        guess = guess_ref[at]
        coupling = coupling_ref[at]
        cap = cap_ref[at : at + 1, :]
        gdev = gdev_ref[at : at + 1, :]
        wire = wire_ref[at : at + 1, :]
        through = lax.dot_general(
            guess,
            coupling,
            (((1,), (1,)), ((), ())),
            precision=lax.Precision.HIGHEST,
            preferred_element_type=F32,
        )
        diagonal = jnp.sum(jnp.where(rows == cols, coupling, 0.0), axis=0, keepdims=True)
        tnh = jnp.tanh(guess)
        inv = 1.0 / (1.5 * cap + diagonal + gdev * (1.0 - tnh * tnh) + wire)
        inv_ref[at] = inv
        kept_ref[at : at + 1, :] = wire
        scale_ref[at] = gain_ref[at : at + 1, :] * inv
        base_ref[at] = (
            0.5 * cap * slope_ref[at] + through + gdev * tnh + wire * guess - drive_ref[at]
        )


def gather_kernel(depth, index_ref, early_ref, guess_ref, _, first_ref):
    blocks = guess_ref.shape[0]
    for at in range(blocks):
        index = index_ref[at]
        near = guess_ref[jnp.where(index < 0, index + blocks, 0)]
        early = early_ref[jnp.clip(index, 0, max(depth, 1) - 1)]
        first_ref[at] = jnp.where(index < 0, near, early)


def share_kernel(depth, index_ref, first_ref, base_ref, scale_ref, wire_ref, *rest):
    blocks_in, (share_ref, near_ref, pool) = rest[:-3], rest[-3:]
    blocks = first_ref.shape[0]
    start = 0
    for ref in blocks_in:
        for slot in range(ref.shape[0]):
            pool[start + slot] = ref[slot]
        start += ref.shape[0]
    share = jnp.zeros(share_ref.shape, F32)
    for at in range(blocks):
        index = index_ref[at] - depth
        near = jnp.where(index < 0, first_ref[at], pool[jnp.maximum(index, 0)])
        near_ref[at] = near
        share = share + scale_ref[at] * (base_ref[at] - wire_ref[at : at + 1, :] * near)
    share_ref[...] = share


def residual_kernel(
    parts, near_ref, base_ref, inv_ref, guess_ref, wire_ref, partial_ref, out_ref, held, sems
):
    step = guess_ref.shape[0] // parts
    copies = []
    for part in range(parts):
        for at in range(part * step, (part + 1) * step):
            residual = base_ref[at] - wire_ref[at : at + 1, :] * near_ref[at]
            held[at] = residual
            partial_ref[at] = guess_ref[at] - residual * inv_ref[at]
        some = pl.ds(part * step, step)
        copies.append(pltpu.make_async_copy(held.at[some], out_ref.at[some], sems.at[part]))
        copies[-1].start(priority=part % 2)
    for copy in copies:
        copy.wait()


def update_kernel(m, parts, *rest):
    shares, (whole_ref, partial_ref, scale_ref, updated_ref, held, sems) = rest[:m], rest[m:]
    total = shares[0][...]
    for share in shares[1:]:
        total = total + share[...]
    region = jnp.dot(
        total, whole_ref[...], precision=lax.Precision.HIGHEST, preferred_element_type=F32
    )
    step = partial_ref.shape[0] // parts
    copies = []
    for part in range(parts):
        for at in range(part * step, (part + 1) * step):
            held[at] = partial_ref[at] + scale_ref[at] * region
        span = pl.ds(part * step, step)
        copies.append(pltpu.make_async_copy(held.at[span], updated_ref.at[span], sems.at[part]))
        copies[-1].start(priority=part % 2)
    for copy in copies:
        copy.wait()


def call(body, outs, ins, in_specs, out_specs, scratch=(), limit=8):
    return pl.pallas_call(
        body,
        out_shape=outs,
        in_specs=in_specs,
        out_specs=out_specs,
        scratch_shapes=list(scratch),
        compiler_params=pltpu.CompilerParams(vmem_limit_bytes=limit << 20),
        cost_estimate=pl.CostEstimate(flops=0, bytes_accessed=0, transcendentals=0),
    )(*ins)


def in_hbm(x):
    return pltpu.with_memory_space_constraint(x, pltpu.HBM)


def swap(x, axes, n, k):
    return lax.ppermute(x, axes, [(d, d ^ k) for d in range(n)])


def shards(
    history,
    new_slot,
    partner,
    coupling,
    cap_rate,
    device_gain,
    wire_gain,
    region_gain,
    drive,
    region_inverse,
):
    blocks, _, scen, nodes = history.shape
    n = lax.axis_size("die")
    nblk = lax.axis_size("blk")
    ncol = lax.axis_size("sub") * nblk
    for size in (n, nblk, ncol):
        assert size & (size - 1) == 0
    assert CAP == 2 and blocks <= 32 and blocks & (blocks - 1) == 0
    rcap = 2 * max(1, blocks // n)
    span = ncol * blocks

    def tiles(count):
        return jax.ShapeDtypeStruct((count, scen, nodes), F32)

    def scalars(count):
        return pltpu.SMEM((count,), I32)

    block = tiles(blocks)
    square = jax.ShapeDtypeStruct((nodes, nodes), F32)
    rows = region_inverse[0]
    message = jax.ShapeDtypeStruct((2 * CAP * scen + 8, nodes), F32)

    rounds = [*range(2, n), 1]
    raw, rows, *leaving = call(
        functools.partial(leave_kernel, rounds, span),
        [jax.ShapeDtypeStruct(history.shape, F32), jax.ShapeDtypeStruct(rows.shape, F32)]
        + [message] * (n - 1),
        [
            in_hbm(new_slot.reshape(1, blocks)),
            in_hbm(partner.reshape(1, blocks)),
            in_hbm(history),
            in_hbm(rows),
        ],
        [HBM] * 4,
        [VMEM] * (n + 1),
        [pltpu.VMEM((1, blocks), I32)] * 2 + [pltpu.SemaphoreType.DMA((7,))],
    )
    arrived = [swap(x, "die", n, k) for x, k in zip(leaving, rounds)]
    inverses = [rows] + [swap(rows, "blk", nblk, k) for k in range(1, nblk)]
    old_guess, old_slope = call(
        functools.partial(place_kernel, span),
        [block, block],
        [in_hbm(new_slot), raw],
        [HBM, VMEM],
        [VMEM, VMEM],
        [scalars(blocks), pltpu.SemaphoreType.DMA],
    )
    depth = max(0, rcap - CAP * (n - 1))
    pieces = 2 if depth else 1
    sent, early = [], old_guess
    if depth:
        (early,) = call(
            early_kernel,
            [tiles(depth)],
            [arrived[0], leaving[0], old_guess],
            [VMEM] * 3,
            [VMEM],
        )
        sent.append((early, rounds[0]))
    guess, slopes, whole, *served = call(
        functools.partial(serve_kernel, n, nblk, pieces, depth, rcap),
        [block, block, square, tiles(rcap - depth)] + [tiles(rcap // pieces)] * (pieces * (n - 2)),
        [early, leaving[0], *arrived, *inverses, old_guess, old_slope],
        [ANY] + [VMEM] * (n + nblk + 2),
        [VMEM] * (4 + pieces * (n - 2)),
    )
    sent += zip(served, [rounds[0]] + [k for k in rounds[1:] for _ in range(pieces)])
    others = [swap(x, "die", n, k) for x, k in sent]
    (index,) = call(
        functools.partial(where_kernel, rounds, span, rcap),
        [scalars(blocks)],
        [in_hbm(partner), arrived[0], guess],
        [HBM, VMEM, ANY],
        [SMEM],
        [scalars(blocks), scalars(n), scalars(n), pltpu.SemaphoreType.DMA],
    )
    step = 8 if blocks % 8 == 0 else blocks
    wide = pl.BlockSpec((step, scen, nodes), lambda i: (i, 0, 0))
    flat = pl.BlockSpec((step, nodes), lambda i: (i, 0))
    base, inv, scale, wire = pl.pallas_call(
        local_kernel,
        grid=(blocks // step,),
        out_shape=[block, block, block, jax.ShapeDtypeStruct((blocks, nodes), F32)],
        in_specs=[
            wide,
            wide,
            pl.BlockSpec((step, nodes, nodes), lambda i: (i, 0, 0)),
            flat,
            flat,
            flat,
            flat,
            wide,
        ],
        out_specs=[wide, wide, wide, flat],
        compiler_params=pltpu.CompilerParams(vmem_limit_bytes=8 << 20),
        cost_estimate=pl.CostEstimate(flops=0, bytes_accessed=0, transcendentals=0),
    )(
        guess,
        slopes,
        in_hbm(coupling),
        in_hbm(cap_rate),
        in_hbm(device_gain),
        in_hbm(wire_gain),
        in_hbm(region_gain),
        in_hbm(drive),
    )
    index = pltpu.with_memory_space_constraint(index, pltpu.SMEM)
    early, others = (others[0], others[1:]) if depth else (guess, others)
    (first,) = call(
        functools.partial(gather_kernel, depth),
        [block],
        [index, early, guess, base],
        [SMEM, VMEM, VMEM, ANY],
        [VMEM],
    )
    share, near = call(
        functools.partial(share_kernel, depth),
        [jax.ShapeDtypeStruct((scen, nodes), F32), block],
        [index, first, base, scale, wire, *others],
        [SMEM] + [VMEM] * (4 + len(others)),
        [VMEM] * 2,
        [pltpu.VMEM(((n - 1) * rcap - depth, scen, nodes), F32)],
    )
    parts = 8 if blocks % 8 == 0 else 1
    partial, residual = call(
        functools.partial(residual_kernel, parts),
        [block, block],
        [near, base, inv, guess, wire],
        [VMEM] * 5,
        [VMEM, HBM],
        [pltpu.VMEM((blocks, scen, nodes), F32), pltpu.SemaphoreType.DMA((parts,))],
    )
    shares = [share] + [swap(share, ("sub", "blk"), ncol, k) for k in range(1, ncol)]
    (updated,) = call(
        functools.partial(update_kernel, ncol, parts),
        [block],
        [*shares, whole, partial, scale],
        [VMEM] * (ncol + 3),
        [HBM],
        [pltpu.VMEM((blocks, scen, nodes), F32), pltpu.SemaphoreType.DMA((parts,))],
    )
    return (updated, residual)


def solution(mesh):
    every = ("grp", "die", "sub", "blk")
    in_specs = (
        P(every, None, None, None),
        P(every),
        P(every),
        P(every, None, None),
        P(every, None),
        P(every, None),
        P(every, None),
        P(every, None),
        P(every, None, None),
        P(("grp", "die"), "blk", None),
    )
    out_specs = (P(every, None, None), P(every, None, None))
    return jax.shard_map(shards, mesh=mesh, in_specs=in_specs, out_specs=out_specs, check_vma=False)
```

```python
import functools

import jax
import jax.numpy as jnp
from jax import lax
from jax.experimental import pallas as pl
from jax.experimental.pallas import tpu as pltpu
from jax.sharding import PartitionSpec as P

CAP = 2
VMEM = pl.BlockSpec(memory_space=pltpu.VMEM)
SMEM = pl.BlockSpec(memory_space=pltpu.SMEM)
ANY = pl.BlockSpec(memory_space=pl.ANY)
HBM = pl.BlockSpec(memory_space=pltpu.HBM)
F32 = jnp.float32
I32 = jnp.int32


def divmod_static(value, size):
    if size & (size - 1) == 0:
        return lax.shift_right_logical(value, size.bit_length() - 1), value & (size - 1)
    whole = lax.div(value, size)
    return whole, value - whole * size


def bit_of(index):
    return lax.shift_left(jnp.int32(1), index)


def bits_set(x):
    x = x - (lax.shift_right_logical(x, 1) & 0x55555555)
    x = (x & 0x33333333) + (lax.shift_right_logical(x, 2) & 0x33333333)
    x = (x + lax.shift_right_logical(x, 4)) & 0x0F0F0F0F
    x = x + lax.shift_right_logical(x, 8)
    x = x + lax.shift_right_logical(x, 16)
    return x & 63


def lowest(mask):
    return jnp.maximum(31 - lax.clz(mask & -mask), 0)


def halves(mask):
    return [mask & 0xFFFF, lax.shift_right_logical(mask, 16)]


def joined(low, high):
    return low | lax.shift_left(high, 16)


def predict(raw):
    return 3.0 * raw[0] - 3.0 * raw[1] + raw[2]


def slope(raw, guess):
    return 3.0 * guess - (4.0 * raw[0] - raw[1])


def read_masks(n, span, blocks, reads, mine):
    wants = [jnp.int32(0)] * n
    for at in range(n):
        mine[at] = 0
    for at in range(blocks):
        owner, local = divmod_static(reads[at], span)
        bit = bit_of(divmod_static(local, blocks)[1])
        if n > 8:
            mine[owner] = mine[owner] | bit
        else:
            wants = [want | jnp.where(owner == o, bit, 0) for o, want in enumerate(wants)]
    if n <= 8:
        for at in range(n):
            mine[at] = wants[at]


def leave_kernel(
    rounds, span, new_slot_ref, partner_ref, history_ref, rows_ref, raw_ref, inverse_ref, *rest
):
    n = len(rounds) + 1
    outs, (slots, reads, sems) = rest[: n - 1], rest[n - 1 :]
    blocks, _, scen, nodes = history_ref.shape
    pieces = 8 if blocks % 8 == 0 else 1
    piece = blocks // pieces
    die = lax.axis_index("die")
    copies = [
        pltpu.make_async_copy(new_slot_ref, slots, sems.at[0]),
        pltpu.make_async_copy(partner_ref, reads, sems.at[1]),
        pltpu.make_async_copy(rows_ref, inverse_ref, sems.at[2]),
    ]
    for at in range(pieces):
        some = pl.ds(at * piece, piece)
        copies.append(
            pltpu.make_async_copy(history_ref.at[some], raw_ref.at[some], sems.at[3 + at])
        )
    for at, copy in enumerate(copies):
        copy.start(priority=at % 2)
    height = max(8, n)
    turn = lax.broadcasted_iota(I32, (height, blocks), 0)
    lane = lax.broadcasted_iota(I32, (height, blocks), 1)
    line = lax.broadcasted_iota(I32, (8, nodes), 0)
    copies[0].wait()
    copies[1].wait()

    dest, local = divmod_static(jnp.broadcast_to(slots[...], (height, blocks)), span)
    local = divmod_static(local, blocks)[1]
    goes = turn == (dest ^ die)
    key = (lane * blocks + local).astype(F32)
    none = float(blocks * blocks)
    least = jnp.min(jnp.where(goes, key, none), axis=1, keepdims=True).astype(I32)
    most = jnp.max(jnp.where(goes, key, -1.0), axis=1, keepdims=True).astype(I32)
    keys = [jnp.where(least < blocks * blocks, least, -1), jnp.where(most > least, most, -1)]
    owner, local = divmod_static(jnp.broadcast_to(reads[...], (height, blocks)), span)
    bits = bit_of(divmod_static(local, blocks)[1])
    bits = jnp.where(turn == (owner ^ die), bits, 0)
    bits = jnp.concatenate([bits, jnp.zeros((height, nodes - blocks), I32)], axis=1)
    shift = 1
    while shift < blocks:
        bits = bits | pltpu.roll(bits, nodes - shift, 1)
        shift *= 2
    values = halves(bits) + [jnp.where(key < 0, -1, key & (blocks - 1)) for key in keys]
    values = [jnp.broadcast_to(value, (height, nodes)) for value in values]
    for k, out in zip(rounds, outs):
        told = jnp.zeros((8, nodes), I32)
        for j, value in enumerate(values):
            told = jnp.where(line == j, value[k : k + 1, :], told)
        out[pl.ds(2 * CAP * scen, 8), :] = told.astype(F32)
    for copy in copies[2:]:
        copy.wait()
    for k, out in zip(rounds, outs):
        for rank, key in enumerate(keys):
            raw = raw_ref.at[lax.shift_right_logical(jnp.maximum(key[k, 0], 0), blocks.bit_length() - 1)]
            guess = predict(raw)
            out[pl.ds(rank * scen, scen), :] = guess
            out[pl.ds((CAP + rank) * scen, scen), :] = slope(raw, guess)


def place_kernel(span, new_slot_ref, raw_ref, guess_ref, slope_ref, slots, sem):
    blocks = raw_ref.shape[0]
    die = lax.axis_index("die")
    copy = pltpu.make_async_copy(new_slot_ref, slots, sem)
    copy.start()
    copy.wait()
    for at in range(blocks):
        dest, local = divmod_static(slots[at], span)
        local = divmod_static(local, blocks)[1]

        @pl.when(dest == die)
        def _(at=at, local=local):
            raw = raw_ref.at[at]
            guess = predict(raw)
            guess_ref[local] = guess
            slope_ref[local] = slope(raw, guess)


def told(message, j):
    return message[message.shape[0] - 8 + j, 0].astype(I32)


def settle(arrived, first, out):
    scen = out.shape[1]
    for message in arrived:
        for rank in range(CAP):
            place = told(message, 2 + rank)

            @pl.when(place >= 0)
            def _(message=message, rank=rank, place=place):
                out[place] = message[pl.ds((first + rank) * scen, scen), :]


def serve_kernel(n, *rest):
    arrived, (old_guess, guess_ref, *outs) = rest[: n - 1], rest[n - 1 :]
    for at in range(guess_ref.shape[0]):
        guess_ref[at] = old_guess[at]
    settle(arrived, 0, guess_ref)
    for message, out in zip(arrived, outs):
        want = joined(told(message, 0), told(message, 1))
        for slot in range(out.shape[0]):
            out[slot] = guess_ref[lowest(want)]
            want = want & (want - 1)


def merge_kernel(n, nblk, *rest):
    arrived, rest = rest[: n - 1], rest[n - 1 :]
    inverses, (old_slope, _, slope_ref, whole_ref) = rest[:nblk], rest[nblk:]
    height = inverses[0].shape[0]
    for k in range(nblk):
        at = pl.multiple_of((lax.axis_index("blk") ^ k) * height, height)
        whole_ref[pl.ds(at, height), :] = inverses[k][...]
    for at in range(slope_ref.shape[0]):
        slope_ref[at] = old_slope[at]
    settle(arrived, CAP, slope_ref)


def where_kernel(rounds, span, rcap, last, partner_ref, _, index_ref, late_ref, reads, mine, starts, sem):
    n = len(rounds) + 1
    blocks = index_ref.shape[0]
    die = lax.axis_index("die")
    copy = pltpu.make_async_copy(partner_ref, reads, sem)
    copy.start()
    starts[0] = 0
    for at, k in enumerate(rounds):
        starts[k] = at * rcap
    copy.wait()
    read_masks(n, span, blocks, reads, mine)

    def step(at, count):
        owner, local = divmod_static(reads[at], span)
        local = divmod_static(local, blocks)[1]
        k = owner ^ die
        slot = bits_set(mine[owner] & (bit_of(local) - 1))
        index_ref[at] = jnp.where(k == 0, local - blocks, starts[k] + slot)
        late_ref[1 + count] = at
        return count + jnp.where(k == rounds[last], 1, 0)

    for at in range(1 + blocks):
        late_ref[at] = 0
    late_ref[0] = lax.fori_loop(0, blocks, step, jnp.int32(0))


def local_kernel(
    guess_ref, slope_ref, coupling_ref, cap_ref, gdev_ref, wire_ref, gain_ref, drive_ref,
    base_ref, inv_ref, scale_ref, kept_ref
):
    nodes = coupling_ref.shape[1]
    rows = lax.broadcasted_iota(I32, (nodes, nodes), 0)
    cols = lax.broadcasted_iota(I32, (nodes, nodes), 1)
    for at in range(guess_ref.shape[0]):
        guess = guess_ref[at]
        coupling = coupling_ref[at]
        cap = cap_ref[at : at + 1, :]
        gdev = gdev_ref[at : at + 1, :]
        wire = wire_ref[at : at + 1, :]
        through = lax.dot_general(
            guess,
            coupling,
            (((1,), (1,)), ((), ())),
            precision=lax.Precision.HIGHEST,
            preferred_element_type=F32,
        )
        diagonal = jnp.sum(jnp.where(rows == cols, coupling, 0.0), axis=0, keepdims=True)
        tnh = jnp.tanh(guess)
        inv = 1.0 / (1.5 * cap + diagonal + gdev * (1.0 - tnh * tnh) + wire)
        inv_ref[at] = inv
        kept_ref[at : at + 1, :] = wire
        scale_ref[at] = gain_ref[at : at + 1, :] * inv
        base_ref[at] = (
            0.5 * cap * slope_ref[at] + through + gdev * tnh + wire * guess - drive_ref[at]
        )


def gather_kernel(rcap, last, index_ref, base_ref, scale_ref, guess_ref, wire_ref, *rest):
    blocks_in, (near_ref, share_ref, pool) = rest[:-3], rest[-3:]
    blocks = guess_ref.shape[0]
    for at, ref in enumerate(blocks_in):
        for slot in range(rcap):
            pool[(at + (at >= last)) * rcap + slot] = ref[slot]
    share = jnp.zeros(share_ref.shape, F32)
    for at in range(blocks):
        index = index_ref[at]
        own = index < 0
        near = guess_ref[jnp.where(own, index + blocks, 0)]
        near = jnp.where(own, near, pool[jnp.maximum(index, 0)])
        missing = (index >= last * rcap) & (index < (last + 1) * rcap)
        near = jnp.where(missing, 0.0, near)
        near_ref[at] = near
        share = share + scale_ref[at] * (base_ref[at] - wire_ref[at : at + 1, :] * near)
    share_ref[...] = share


def share_kernel(rcap, last, index_ref, late_ref, scale_ref, wire_ref, part_ref, block_ref, share_ref):
    share = part_ref[...]
    for slot in range(min(rcap, wire_ref.shape[0])):
        at = late_ref[1 + slot]
        there = slot < late_ref[0]
        block = block_ref[jnp.where(there, index_ref[at] - last * rcap, 0)]
        share = share - jnp.where(there, scale_ref[at] * wire_ref[pl.ds(at, 1), :] * block, 0.0)
    share_ref[...] = share


def residual_kernel(
    rcap, last, parts, index_ref, near_ref, block_ref, base_ref, inv_ref, guess_ref, wire_ref,
    partial_ref, out_ref, held, sems
):
    step = guess_ref.shape[0] // parts
    copies = []
    for part in range(parts):
        for at in range(part * step, (part + 1) * step):
            slot = index_ref[at] - last * rcap
            missing = (slot >= 0) & (slot < rcap)
            near = jnp.where(missing, block_ref[jnp.where(missing, slot, 0)], near_ref[at])
            residual = base_ref[at] - wire_ref[at : at + 1, :] * near
            held[at] = residual
            partial_ref[at] = guess_ref[at] - residual * inv_ref[at]
        some = pl.ds(part * step, step)
        copies.append(pltpu.make_async_copy(held.at[some], out_ref.at[some], sems.at[part]))
        copies[-1].start(priority=part % 2)
    for copy in copies:
        copy.wait()


def update_kernel(m, parts, *rest):
    shares, (whole_ref, partial_ref, scale_ref, updated_ref, held, sems) = rest[:m], rest[m:]
    total = shares[0][...]
    for share in shares[1:]:
        total = total + share[...]
    region = jnp.dot(
        total, whole_ref[...], precision=lax.Precision.HIGHEST, preferred_element_type=F32
    )
    step = partial_ref.shape[0] // parts
    copies = []
    for part in range(parts):
        for at in range(part * step, (part + 1) * step):
            held[at] = partial_ref[at] + scale_ref[at] * region
        span = pl.ds(part * step, step)
        copies.append(pltpu.make_async_copy(held.at[span], updated_ref.at[span], sems.at[part]))
        copies[-1].start(priority=part % 2)
    for copy in copies:
        copy.wait()


def call(body, outs, ins, in_specs, out_specs, scratch=(), limit=8):
    return pl.pallas_call(
        body,
        out_shape=outs,
        in_specs=in_specs,
        out_specs=out_specs,
        scratch_shapes=list(scratch),
        compiler_params=pltpu.CompilerParams(vmem_limit_bytes=limit << 20),
        cost_estimate=pl.CostEstimate(flops=0, bytes_accessed=0, transcendentals=0),
    )(*ins)


def in_hbm(x):
    return pltpu.with_memory_space_constraint(x, pltpu.HBM)


def swap(x, axes, n, k):
    return lax.ppermute(x, axes, [(d, d ^ k) for d in range(n)])


def shards(
    history,
    new_slot,
    partner,
    coupling,
    cap_rate,
    device_gain,
    wire_gain,
    region_gain,
    drive,
    region_inverse,
):
    blocks, _, scen, nodes = history.shape
    n = lax.axis_size("die")
    nblk = lax.axis_size("blk")
    ncol = lax.axis_size("sub") * nblk
    for size in (n, nblk, ncol):
        assert size & (size - 1) == 0
    assert CAP == 2 and blocks <= 32 and blocks & (blocks - 1) == 0
    rcap = 2 * max(1, blocks // n)
    span = ncol * blocks

    def tiles(count):
        return jax.ShapeDtypeStruct((count, scen, nodes), F32)

    def scalars(count):
        return pltpu.SMEM((count,), I32)

    block = tiles(blocks)
    square = jax.ShapeDtypeStruct((nodes, nodes), F32)
    rows = region_inverse[0]
    message = jax.ShapeDtypeStruct((2 * CAP * scen + 8, nodes), F32)

    rounds = [*range(2, n), 1]
    raw, rows, *leaving = call(
        functools.partial(leave_kernel, rounds, span),
        [jax.ShapeDtypeStruct(history.shape, F32), jax.ShapeDtypeStruct(rows.shape, F32)]
        + [message] * (n - 1),
        [
            in_hbm(new_slot.reshape(1, blocks)),
            in_hbm(partner.reshape(1, blocks)),
            in_hbm(history),
            in_hbm(rows),
        ],
        [HBM] * 4,
        [VMEM] * (n + 1),
        [pltpu.VMEM((1, blocks), I32)] * 2 + [pltpu.SemaphoreType.DMA((11,))],
    )
    arrived = [swap(x, "die", n, k) for x, k in zip(leaving, rounds)]
    inverses = [rows] + [swap(rows, "blk", nblk, k) for k in range(1, nblk)]
    old_guess, old_slope = call(
        functools.partial(place_kernel, span),
        [block, block],
        [in_hbm(new_slot), raw],
        [HBM, VMEM],
        [VMEM, VMEM],
        [scalars(blocks), pltpu.SemaphoreType.DMA],
    )
    guess, *served = call(
        functools.partial(serve_kernel, n),
        [block] + [tiles(rcap)] * (n - 1),
        [*arrived, old_guess],
        [VMEM] * n,
        [VMEM] * n,
    )
    others = [swap(x, "die", n, k) for x, k in zip(served, rounds)]
    slopes, whole = call(
        functools.partial(merge_kernel, n, nblk),
        [block, square],
        [*arrived, *inverses, old_slope, guess],
        [VMEM] * (n + nblk) + [ANY],
        [VMEM] * 2,
    )
    last = n - 2
    index, late = call(
        functools.partial(where_kernel, rounds, span, rcap, last),
        [scalars(blocks), scalars(1 + blocks)],
        [in_hbm(partner), guess],
        [HBM, ANY],
        [SMEM, SMEM],
        [scalars(blocks), scalars(n), scalars(n), pltpu.SemaphoreType.DMA],
    )
    step = 8 if blocks % 8 == 0 else blocks
    wide = pl.BlockSpec((step, scen, nodes), lambda i: (i, 0, 0))
    flat = pl.BlockSpec((step, nodes), lambda i: (i, 0))
    base, inv, scale, wire = pl.pallas_call(
        local_kernel,
        grid=(blocks // step,),
        out_shape=[block, block, block, jax.ShapeDtypeStruct((blocks, nodes), F32)],
        in_specs=[
            wide,
            wide,
            pl.BlockSpec((step, nodes, nodes), lambda i: (i, 0, 0)),
            flat,
            flat,
            flat,
            flat,
            wide,
        ],
        out_specs=[wide, wide, wide, flat],
        compiler_params=pltpu.CompilerParams(vmem_limit_bytes=8 << 20),
        cost_estimate=pl.CostEstimate(flops=0, bytes_accessed=0, transcendentals=0),
    )(
        guess,
        slopes,
        in_hbm(coupling),
        in_hbm(cap_rate),
        in_hbm(device_gain),
        in_hbm(wire_gain),
        in_hbm(region_gain),
        in_hbm(drive),
    )
    index = pltpu.with_memory_space_constraint(index, pltpu.SMEM)
    late = pltpu.with_memory_space_constraint(late, pltpu.SMEM)
    flat_share = jax.ShapeDtypeStruct((scen, nodes), F32)
    first = others[:last] + others[last + 1 :]
    near, part = call(
        functools.partial(gather_kernel, rcap, last),
        [block, flat_share],
        [index, base, scale, guess, wire, *first],
        [SMEM] + [VMEM] * (4 + len(first)),
        [VMEM] * 2,
        [pltpu.VMEM(((n - 1) * rcap, scen, nodes), F32)],
    )
    (share,) = call(
        functools.partial(share_kernel, rcap, last),
        [flat_share],
        [index, late, scale, wire, part, others[last]],
        [SMEM] * 2 + [VMEM] * 4,
        [VMEM],
    )
    parts = 8 if blocks % 8 == 0 else 1
    partial, residual = call(
        functools.partial(residual_kernel, rcap, last, parts),
        [block, block],
        [index, near, others[last], base, inv, guess, wire],
        [SMEM] + [VMEM] * 6,
        [VMEM, HBM],
        [pltpu.VMEM((blocks, scen, nodes), F32), pltpu.SemaphoreType.DMA((parts,))],
    )
    shares = [share] + [swap(share, ("sub", "blk"), ncol, k) for k in range(1, ncol)]
    (updated,) = call(
        functools.partial(update_kernel, ncol, parts),
        [block],
        [*shares, whole, partial, scale],
        [VMEM] * (ncol + 3),
        [HBM],
        [pltpu.VMEM((blocks, scen, nodes), F32), pltpu.SemaphoreType.DMA((parts,))],
    )
    return (updated, residual)


def solution(mesh):
    every = ("grp", "die", "sub", "blk")
    in_specs = (
        P(every, None, None, None),
        P(every),
        P(every),
        P(every, None, None),
        P(every, None),
        P(every, None),
        P(every, None),
        P(every, None),
        P(every, None, None),
        P(("grp", "die"), "blk", None),
    )
    out_specs = (P(every, None, None), P(every, None, None))
    return jax.shard_map(shards, mesh=mesh, in_specs=in_specs, out_specs=out_specs, check_vma=False)
```

```python
import functools

import jax
import jax.numpy as jnp
from jax import lax
from jax.experimental import pallas as pl
from jax.experimental.pallas import tpu as pltpu
from jax.sharding import PartitionSpec as P

CAP = 2
VMEM = pl.BlockSpec(memory_space=pltpu.VMEM)
SMEM = pl.BlockSpec(memory_space=pltpu.SMEM)
ANY = pl.BlockSpec(memory_space=pl.ANY)
HBM = pl.BlockSpec(memory_space=pltpu.HBM)
F32 = jnp.float32
I32 = jnp.int32


def divmod_static(value, size):
    if size & (size - 1) == 0:
        return lax.shift_right_logical(value, size.bit_length() - 1), value & (size - 1)
    whole = lax.div(value, size)
    return whole, value - whole * size


def bit_of(index):
    return lax.shift_left(jnp.int32(1), index)


def bits_set(x):
    x = x - (lax.shift_right_logical(x, 1) & 0x55555555)
    x = (x & 0x33333333) + (lax.shift_right_logical(x, 2) & 0x33333333)
    x = (x + lax.shift_right_logical(x, 4)) & 0x0F0F0F0F
    x = x + lax.shift_right_logical(x, 8)
    x = x + lax.shift_right_logical(x, 16)
    return x & 63


def lowest(mask):
    return jnp.maximum(31 - lax.clz(mask & -mask), 0)


def halves(mask):
    return [mask & 0xFFFF, lax.shift_right_logical(mask, 16)]


def joined(low, high):
    return low | lax.shift_left(high, 16)


def predict(raw):
    return 3.0 * raw[0] - 3.0 * raw[1] + raw[2]


def slope(raw, guess):
    return 3.0 * guess - (4.0 * raw[0] - raw[1])


def read_masks(n, span, blocks, reads, mine):
    wants = [jnp.int32(0)] * n
    for at in range(n):
        mine[at] = 0
    for at in range(blocks):
        owner, local = divmod_static(reads[at], span)
        bit = bit_of(divmod_static(local, blocks)[1])
        if n > 8:
            mine[owner] = mine[owner] | bit
        else:
            wants = [want | jnp.where(owner == o, bit, 0) for o, want in enumerate(wants)]
    if n <= 8:
        for at in range(n):
            mine[at] = wants[at]


def leave_kernel(
    rounds, span, new_slot_ref, partner_ref, history_ref, rows_ref, raw_ref, inverse_ref, *rest
):
    n = len(rounds) + 1
    outs, (slots, reads, sems) = rest[: n - 1], rest[n - 1 :]
    blocks, _, scen, nodes = history_ref.shape
    pieces = 2 if blocks % 2 == 0 else 1
    piece = blocks // pieces
    die = lax.axis_index("die")
    copies = [
        pltpu.make_async_copy(new_slot_ref, slots, sems.at[0]),
        pltpu.make_async_copy(partner_ref, reads, sems.at[1]),
        pltpu.make_async_copy(rows_ref, inverse_ref, sems.at[2]),
    ]
    for at in range(pieces):
        some = pl.ds(at * piece, piece)
        copies.append(
            pltpu.make_async_copy(history_ref.at[some], raw_ref.at[some], sems.at[3 + at])
        )
    for copy in copies:
        copy.start()
    height = max(8, n)
    turn = lax.broadcasted_iota(I32, (height, blocks), 0)
    lane = lax.broadcasted_iota(I32, (height, blocks), 1)
    line = lax.broadcasted_iota(I32, (8, nodes), 0)
    copies[0].wait()
    copies[1].wait()

    dest, local = divmod_static(jnp.broadcast_to(slots[...], (height, blocks)), span)
    local = divmod_static(local, blocks)[1]
    goes = turn == (dest ^ die)
    key = (lane * blocks + local).astype(F32)
    none = float(blocks * blocks)
    least = jnp.min(jnp.where(goes, key, none), axis=1, keepdims=True).astype(I32)
    most = jnp.max(jnp.where(goes, key, -1.0), axis=1, keepdims=True).astype(I32)
    keys = [jnp.where(least < blocks * blocks, least, -1), jnp.where(most > least, most, -1)]
    owner, local = divmod_static(jnp.broadcast_to(reads[...], (height, blocks)), span)
    bits = bit_of(divmod_static(local, blocks)[1])
    bits = jnp.where(turn == (owner ^ die), bits, 0)
    bits = jnp.concatenate([bits, jnp.zeros((height, nodes - blocks), I32)], axis=1)
    shift = 1
    while shift < blocks:
        bits = bits | pltpu.roll(bits, nodes - shift, 1)
        shift *= 2
    values = halves(bits) + [jnp.where(key < 0, -1, key & (blocks - 1)) for key in keys]
    values = [jnp.broadcast_to(value, (height, nodes)) for value in values]
    for k, out in zip(rounds, outs):
        told = jnp.zeros((8, nodes), I32)
        for j, value in enumerate(values):
            told = jnp.where(line == j, value[k : k + 1, :], told)
        out[pl.ds(2 * CAP * scen, 8), :] = told.astype(F32)
    for copy in copies[2:]:
        copy.wait()
    for k, out in zip(rounds, outs):
        for rank, key in enumerate(keys):
            raw = raw_ref.at[lax.shift_right_logical(jnp.maximum(key[k, 0], 0), blocks.bit_length() - 1)]
            guess = predict(raw)
            out[pl.ds(rank * scen, scen), :] = guess
            out[pl.ds((CAP + rank) * scen, scen), :] = slope(raw, guess)


def place_kernel(span, new_slot_ref, raw_ref, guess_ref, slope_ref, slots, sem):
    blocks = raw_ref.shape[0]
    die = lax.axis_index("die")
    copy = pltpu.make_async_copy(new_slot_ref, slots, sem)
    copy.start()
    copy.wait()
    for at in range(blocks):
        dest, local = divmod_static(slots[at], span)
        local = divmod_static(local, blocks)[1]

        @pl.when(dest == die)
        def _(at=at, local=local):
            raw = raw_ref.at[at]
            guess = predict(raw)
            guess_ref[local] = guess
            slope_ref[local] = slope(raw, guess)


def told(message, j):
    return message[message.shape[0] - 8 + j, 0].astype(I32)


def settle(arrived, first, out):
    scen = out.shape[1]
    for message in arrived:
        for rank in range(CAP):
            place = told(message, 2 + rank)

            @pl.when(place >= 0)
            def _(message=message, rank=rank, place=place):
                out[place] = message[pl.ds((first + rank) * scen, scen), :]


def serve_kernel(n, *rest):
    arrived, (old_guess, guess_ref, *outs) = rest[: n - 1], rest[n - 1 :]
    for at in range(guess_ref.shape[0]):
        guess_ref[at] = old_guess[at]
    settle(arrived, 0, guess_ref)
    for message, out in zip(arrived, outs):
        want = joined(told(message, 0), told(message, 1))
        for slot in range(out.shape[0]):
            out[slot] = guess_ref[lowest(want)]
            want = want & (want - 1)


def merge_kernel(n, nblk, *rest):
    arrived, rest = rest[: n - 1], rest[n - 1 :]
    inverses, (old_slope, _, slope_ref, whole_ref) = rest[:nblk], rest[nblk:]
    height = inverses[0].shape[0]
    for k in range(nblk):
        at = pl.multiple_of((lax.axis_index("blk") ^ k) * height, height)
        whole_ref[pl.ds(at, height), :] = inverses[k][...]
    for at in range(slope_ref.shape[0]):
        slope_ref[at] = old_slope[at]
    settle(arrived, CAP, slope_ref)


def where_kernel(rounds, span, rcap, last, partner_ref, _, index_ref, late_ref, reads, mine, starts, sem):
    n = len(rounds) + 1
    blocks = index_ref.shape[0]
    die = lax.axis_index("die")
    copy = pltpu.make_async_copy(partner_ref, reads, sem)
    copy.start()
    starts[0] = 0
    for at, k in enumerate(rounds):
        starts[k] = at * rcap
    copy.wait()
    read_masks(n, span, blocks, reads, mine)

    def step(at, count):
        owner, local = divmod_static(reads[at], span)
        local = divmod_static(local, blocks)[1]
        k = owner ^ die
        slot = bits_set(mine[owner] & (bit_of(local) - 1))
        index_ref[at] = jnp.where(k == 0, local - blocks, starts[k] + slot)
        late_ref[1 + count] = at
        return count + jnp.where(k == rounds[last], 1, 0)

    for at in range(1 + blocks):
        late_ref[at] = 0
    late_ref[0] = lax.fori_loop(0, blocks, step, jnp.int32(0))


def local_kernel(
    guess_ref, slope_ref, coupling_ref, cap_ref, gdev_ref, wire_ref, gain_ref, drive_ref,
    base_ref, inv_ref, scale_ref, kept_ref
):
    nodes = coupling_ref.shape[1]
    rows = lax.broadcasted_iota(I32, (nodes, nodes), 0)
    cols = lax.broadcasted_iota(I32, (nodes, nodes), 1)
    for at in range(guess_ref.shape[0]):
        guess = guess_ref[at]
        coupling = coupling_ref[at]
        cap = cap_ref[at : at + 1, :]
        gdev = gdev_ref[at : at + 1, :]
        wire = wire_ref[at : at + 1, :]
        through = lax.dot_general(
            guess,
            coupling,
            (((1,), (1,)), ((), ())),
            precision=lax.Precision.HIGHEST,
            preferred_element_type=F32,
        )
        diagonal = jnp.sum(jnp.where(rows == cols, coupling, 0.0), axis=0, keepdims=True)
        tnh = jnp.tanh(guess)
        inv = 1.0 / (1.5 * cap + diagonal + gdev * (1.0 - tnh * tnh) + wire)
        inv_ref[at] = inv
        kept_ref[at : at + 1, :] = wire
        scale_ref[at] = gain_ref[at : at + 1, :] * inv
        base_ref[at] = (
            0.5 * cap * slope_ref[at] + through + gdev * tnh + wire * guess - drive_ref[at]
        )


def gather_kernel(rcap, last, index_ref, base_ref, scale_ref, guess_ref, wire_ref, *rest):
    blocks_in, (near_ref, share_ref, pool) = rest[:-3], rest[-3:]
    blocks = guess_ref.shape[0]
    for at, ref in enumerate(blocks_in):
        for slot in range(rcap):
            pool[(at + (at >= last)) * rcap + slot] = ref[slot]
    share = jnp.zeros(share_ref.shape, F32)
    for at in range(blocks):
        index = index_ref[at]
        own = index < 0
        near = guess_ref[jnp.where(own, index + blocks, 0)]
        near = jnp.where(own, near, pool[jnp.maximum(index, 0)])
        missing = (index >= last * rcap) & (index < (last + 1) * rcap)
        near = jnp.where(missing, 0.0, near)
        near_ref[at] = near
        share = share + scale_ref[at] * (base_ref[at] - wire_ref[at : at + 1, :] * near)
    share_ref[...] = share


def share_kernel(rcap, last, index_ref, late_ref, scale_ref, wire_ref, part_ref, block_ref, share_ref):
    share = part_ref[...]
    for slot in range(min(rcap, wire_ref.shape[0])):
        at = late_ref[1 + slot]
        there = slot < late_ref[0]
        block = block_ref[jnp.where(there, index_ref[at] - last * rcap, 0)]
        share = share - jnp.where(there, scale_ref[at] * wire_ref[pl.ds(at, 1), :] * block, 0.0)
    share_ref[...] = share


def residual_kernel(
    rcap, last, parts, index_ref, near_ref, block_ref, base_ref, inv_ref, guess_ref, wire_ref,
    partial_ref, out_ref, held, sems
):
    step = guess_ref.shape[0] // parts
    copies = []
    for part in range(parts):
        for at in range(part * step, (part + 1) * step):
            slot = index_ref[at] - last * rcap
            missing = (slot >= 0) & (slot < rcap)
            near = jnp.where(missing, block_ref[jnp.where(missing, slot, 0)], near_ref[at])
            residual = base_ref[at] - wire_ref[at : at + 1, :] * near
            held[at] = residual
            partial_ref[at] = guess_ref[at] - residual * inv_ref[at]
        some = pl.ds(part * step, step)
        copies.append(pltpu.make_async_copy(held.at[some], out_ref.at[some], sems.at[part]))
        copies[-1].start()
    for copy in copies:
        copy.wait()


def update_kernel(m, parts, *rest):
    shares, (whole_ref, partial_ref, scale_ref, updated_ref, held, sems) = rest[:m], rest[m:]
    total = shares[0][...]
    for share in shares[1:]:
        total = total + share[...]
    region = jnp.dot(
        total, whole_ref[...], precision=lax.Precision.HIGHEST, preferred_element_type=F32
    )
    step = partial_ref.shape[0] // parts
    copies = []
    for part in range(parts):
        for at in range(part * step, (part + 1) * step):
            held[at] = partial_ref[at] + scale_ref[at] * region
        span = pl.ds(part * step, step)
        copies.append(pltpu.make_async_copy(held.at[span], updated_ref.at[span], sems.at[part]))
        copies[-1].start()
    for copy in copies:
        copy.wait()


def call(body, outs, ins, in_specs, out_specs, scratch=(), limit=8):
    return pl.pallas_call(
        body,
        out_shape=outs,
        in_specs=in_specs,
        out_specs=out_specs,
        scratch_shapes=list(scratch),
        compiler_params=pltpu.CompilerParams(vmem_limit_bytes=limit << 20),
        cost_estimate=pl.CostEstimate(flops=0, bytes_accessed=0, transcendentals=0),
    )(*ins)


def in_hbm(x):
    return pltpu.with_memory_space_constraint(x, pltpu.HBM)


def swap(x, axes, n, k):
    return lax.ppermute(x, axes, [(d, d ^ k) for d in range(n)])


def shards(
    history,
    new_slot,
    partner,
    coupling,
    cap_rate,
    device_gain,
    wire_gain,
    region_gain,
    drive,
    region_inverse,
):
    blocks, _, scen, nodes = history.shape
    n = lax.axis_size("die")
    nblk = lax.axis_size("blk")
    ncol = lax.axis_size("sub") * nblk
    for size in (n, nblk, ncol):
        assert size & (size - 1) == 0
    assert CAP == 2 and blocks <= 32 and blocks & (blocks - 1) == 0
    rcap = 2 * max(1, blocks // n)
    span = ncol * blocks

    def tiles(count):
        return jax.ShapeDtypeStruct((count, scen, nodes), F32)

    def scalars(count):
        return pltpu.SMEM((count,), I32)

    block = tiles(blocks)
    square = jax.ShapeDtypeStruct((nodes, nodes), F32)
    rows = region_inverse[0]
    message = jax.ShapeDtypeStruct((2 * CAP * scen + 8, nodes), F32)

    rounds = [*range(2, n), 1]
    raw, rows, *leaving = call(
        functools.partial(leave_kernel, rounds, span),
        [jax.ShapeDtypeStruct(history.shape, F32), jax.ShapeDtypeStruct(rows.shape, F32)]
        + [message] * (n - 1),
        [
            in_hbm(new_slot.reshape(1, blocks)),
            in_hbm(partner.reshape(1, blocks)),
            in_hbm(history),
            in_hbm(rows),
        ],
        [HBM] * 4,
        [VMEM] * (n + 1),
        [pltpu.VMEM((1, blocks), I32)] * 2 + [pltpu.SemaphoreType.DMA((5,))],
    )
    arrived = [swap(x, "die", n, k) for x, k in zip(leaving, rounds)]
    inverses = [rows] + [swap(rows, "blk", nblk, k) for k in range(1, nblk)]
    old_guess, old_slope = call(
        functools.partial(place_kernel, span),
        [block, block],
        [in_hbm(new_slot), raw],
        [HBM, VMEM],
        [VMEM, VMEM],
        [scalars(blocks), pltpu.SemaphoreType.DMA],
    )
    guess, *served = call(
        functools.partial(serve_kernel, n),
        [block] + [tiles(rcap)] * (n - 1),
        [*arrived, old_guess],
        [VMEM] * n,
        [VMEM] * n,
    )
    others = [swap(x, "die", n, k) for x, k in zip(served, rounds)]
    slopes, whole = call(
        functools.partial(merge_kernel, n, nblk),
        [block, square],
        [*arrived, *inverses, old_slope, guess],
        [VMEM] * (n + nblk) + [ANY],
        [VMEM] * 2,
    )
    last = n - 2
    index, late = call(
        functools.partial(where_kernel, rounds, span, rcap, last),
        [scalars(blocks), scalars(1 + blocks)],
        [in_hbm(partner), guess],
        [HBM, ANY],
        [SMEM, SMEM],
        [scalars(blocks), scalars(n), scalars(n), pltpu.SemaphoreType.DMA],
    )
    step = 8 if blocks % 8 == 0 else blocks
    wide = pl.BlockSpec((step, scen, nodes), lambda i: (i, 0, 0))
    flat = pl.BlockSpec((step, nodes), lambda i: (i, 0))
    base, inv, scale, wire = pl.pallas_call(
        local_kernel,
        grid=(blocks // step,),
        out_shape=[block, block, block, jax.ShapeDtypeStruct((blocks, nodes), F32)],
        in_specs=[
            wide,
            wide,
            pl.BlockSpec((step, nodes, nodes), lambda i: (i, 0, 0)),
            flat,
            flat,
            flat,
            flat,
            wide,
        ],
        out_specs=[wide, wide, wide, flat],
        compiler_params=pltpu.CompilerParams(vmem_limit_bytes=8 << 20),
        cost_estimate=pl.CostEstimate(flops=0, bytes_accessed=0, transcendentals=0),
    )(
        guess,
        slopes,
        in_hbm(coupling),
        in_hbm(cap_rate),
        in_hbm(device_gain),
        in_hbm(wire_gain),
        in_hbm(region_gain),
        in_hbm(drive),
    )
    index = pltpu.with_memory_space_constraint(index, pltpu.SMEM)
    late = pltpu.with_memory_space_constraint(late, pltpu.SMEM)
    flat_share = jax.ShapeDtypeStruct((scen, nodes), F32)
    first = others[:last] + others[last + 1 :]
    near, part = call(
        functools.partial(gather_kernel, rcap, last),
        [block, flat_share],
        [index, base, scale, guess, wire, *first],
        [SMEM] + [VMEM] * (4 + len(first)),
        [VMEM] * 2,
        [pltpu.VMEM(((n - 1) * rcap, scen, nodes), F32)],
    )
    (share,) = call(
        functools.partial(share_kernel, rcap, last),
        [flat_share],
        [index, late, scale, wire, part, others[last]],
        [SMEM] * 2 + [VMEM] * 4,
        [VMEM],
    )
    parts = 4 if blocks % 4 == 0 else 1
    partial, residual = call(
        functools.partial(residual_kernel, rcap, last, parts),
        [block, block],
        [index, near, others[last], base, inv, guess, wire],
        [SMEM] + [VMEM] * 6,
        [VMEM, HBM],
        [pltpu.VMEM((blocks, scen, nodes), F32), pltpu.SemaphoreType.DMA((parts,))],
    )
    shares = [share] + [swap(share, ("sub", "blk"), ncol, k) for k in range(1, ncol)]
    (updated,) = call(
        functools.partial(update_kernel, ncol, parts),
        [block],
        [*shares, whole, partial, scale],
        [VMEM] * (ncol + 3),
        [HBM],
        [pltpu.VMEM((blocks, scen, nodes), F32), pltpu.SemaphoreType.DMA((parts,))],
    )
    return (updated, residual)


def solution(mesh):
    every = ("grp", "die", "sub", "blk")
    in_specs = (
        P(every, None, None, None),
        P(every),
        P(every),
        P(every, None, None),
        P(every, None),
        P(every, None),
        P(every, None),
        P(every, None),
        P(every, None, None),
        P(("grp", "die"), "blk", None),
    )
    out_specs = (P(every, None, None), P(every, None, None))
    return jax.shard_map(shards, mesh=mesh, in_specs=in_specs, out_specs=out_specs, check_vma=False)
```

```python
import functools

import jax
import jax.numpy as jnp
from jax import lax
from jax.experimental import pallas as pl
from jax.experimental.pallas import tpu as pltpu
from jax.sharding import PartitionSpec as P

CAP = 2
VMEM = pl.BlockSpec(memory_space=pltpu.VMEM)
SMEM = pl.BlockSpec(memory_space=pltpu.SMEM)
ANY = pl.BlockSpec(memory_space=pl.ANY)
HBM = pl.BlockSpec(memory_space=pltpu.HBM)
F32 = jnp.float32
I32 = jnp.int32


def divmod_static(value, size):
    if size & (size - 1) == 0:
        return lax.shift_right_logical(value, size.bit_length() - 1), value & (size - 1)
    whole = lax.div(value, size)
    return whole, value - whole * size


def bit_of(index):
    return lax.shift_left(jnp.int32(1), index)


def bits_set(x):
    x = x - (lax.shift_right_logical(x, 1) & 0x55555555)
    x = (x & 0x33333333) + (lax.shift_right_logical(x, 2) & 0x33333333)
    x = (x + lax.shift_right_logical(x, 4)) & 0x0F0F0F0F
    x = x + lax.shift_right_logical(x, 8)
    x = x + lax.shift_right_logical(x, 16)
    return x & 63


def lowest(mask):
    return jnp.maximum(31 - lax.clz(mask & -mask), 0)


def halves(mask):
    return [mask & 0xFFFF, lax.shift_right_logical(mask, 16)]


def joined(low, high):
    return low | lax.shift_left(high, 16)


def predict(raw):
    return 3.0 * raw[0] - 3.0 * raw[1] + raw[2]


def slope(raw, guess):
    return 3.0 * guess - (4.0 * raw[0] - raw[1])


def read_masks(n, span, blocks, reads, mine):
    wants = [jnp.int32(0)] * n
    for at in range(n):
        mine[at] = 0
    for at in range(blocks):
        owner, local = divmod_static(reads[at], span)
        bit = bit_of(divmod_static(local, blocks)[1])
        if n > 8:
            mine[owner] = mine[owner] | bit
        else:
            wants = [want | jnp.where(owner == o, bit, 0) for o, want in enumerate(wants)]
    if n <= 8:
        for at in range(n):
            mine[at] = wants[at]


def leave_kernel(
    rounds, span, new_slot_ref, partner_ref, history_ref, rows_ref, raw_ref, inverse_ref, *rest
):
    n = len(rounds) + 1
    outs, (slots, reads, sems) = rest[: n - 1], rest[n - 1 :]
    blocks, _, scen, nodes = history_ref.shape
    pieces = 2 if blocks % 2 == 0 else 1
    piece = blocks // pieces
    die = lax.axis_index("die")
    copies = [
        pltpu.make_async_copy(new_slot_ref, slots, sems.at[0]),
        pltpu.make_async_copy(partner_ref, reads, sems.at[1]),
        pltpu.make_async_copy(rows_ref, inverse_ref, sems.at[2]),
    ]
    for at in range(pieces):
        some = pl.ds(at * piece, piece)
        copies.append(
            pltpu.make_async_copy(history_ref.at[some], raw_ref.at[some], sems.at[3 + at])
        )
    for copy in copies:
        copy.start()
    height = max(8, n)
    turn = lax.broadcasted_iota(I32, (height, blocks), 0)
    lane = lax.broadcasted_iota(I32, (height, blocks), 1)
    line = lax.broadcasted_iota(I32, (8, nodes), 0)
    copies[0].wait()
    copies[1].wait()

    dest, local = divmod_static(jnp.broadcast_to(slots[...], (height, blocks)), span)
    local = divmod_static(local, blocks)[1]
    goes = turn == (dest ^ die)
    key = (lane * blocks + local).astype(F32)
    none = float(blocks * blocks)
    least = jnp.min(jnp.where(goes, key, none), axis=1, keepdims=True).astype(I32)
    most = jnp.max(jnp.where(goes, key, -1.0), axis=1, keepdims=True).astype(I32)
    keys = [jnp.where(least < blocks * blocks, least, -1), jnp.where(most > least, most, -1)]
    owner, local = divmod_static(jnp.broadcast_to(reads[...], (height, blocks)), span)
    bits = bit_of(divmod_static(local, blocks)[1])
    bits = jnp.where(turn == (owner ^ die), bits, 0)
    bits = jnp.concatenate([bits, jnp.zeros((height, nodes - blocks), I32)], axis=1)
    shift = 1
    while shift < blocks:
        bits = bits | pltpu.roll(bits, nodes - shift, 1)
        shift *= 2
    values = halves(bits) + [jnp.where(key < 0, -1, key & (blocks - 1)) for key in keys]
    values = [jnp.broadcast_to(value, (height, nodes)) for value in values]
    for k, out in zip(rounds, outs):
        told = jnp.zeros((8, nodes), I32)
        for j, value in enumerate(values):
            told = jnp.where(line == j, value[k : k + 1, :], told)
        out[pl.ds(2 * CAP * scen, 8), :] = told.astype(F32)
    for copy in copies[2:]:
        copy.wait()
    for k, out in zip(rounds, outs):
        for rank, key in enumerate(keys):
            raw = raw_ref.at[lax.shift_right_logical(jnp.maximum(key[k, 0], 0), blocks.bit_length() - 1)]
            guess = predict(raw)
            out[pl.ds(rank * scen, scen), :] = guess
            out[pl.ds((CAP + rank) * scen, scen), :] = slope(raw, guess)


def place_kernel(span, new_slot_ref, raw_ref, guess_ref, slope_ref, slots, sem):
    blocks = raw_ref.shape[0]
    die = lax.axis_index("die")
    copy = pltpu.make_async_copy(new_slot_ref, slots, sem)
    copy.start()
    copy.wait()
    for at in range(blocks):
        dest, local = divmod_static(slots[at], span)
        local = divmod_static(local, blocks)[1]

        @pl.when(dest == die)
        def _(at=at, local=local):
            raw = raw_ref.at[at]
            guess = predict(raw)
            guess_ref[local] = guess
            slope_ref[local] = slope(raw, guess)


def told(message, j):
    return message[message.shape[0] - 8 + j, 0].astype(I32)


def settle(arrived, first, out):
    scen = out.shape[1]
    for message in arrived:
        for rank in range(CAP):
            place = told(message, 2 + rank)

            @pl.when(place >= 0)
            def _(message=message, rank=rank, place=place):
                out[place] = message[pl.ds((first + rank) * scen, scen), :]


def serve_kernel(n, *rest):
    arrived, (old_guess, guess_ref, *outs) = rest[: n - 1], rest[n - 1 :]
    for at in range(guess_ref.shape[0]):
        guess_ref[at] = old_guess[at]
    settle(arrived, 0, guess_ref)
    for message, out in zip(arrived, outs):
        want = joined(told(message, 0), told(message, 1))
        for slot in range(out.shape[0]):
            out[slot] = guess_ref[lowest(want)]
            want = want & (want - 1)


def merge_kernel(n, nblk, *rest):
    arrived, rest = rest[: n - 1], rest[n - 1 :]
    inverses, (old_slope, _, slope_ref, whole_ref) = rest[:nblk], rest[nblk:]
    height = inverses[0].shape[0]
    for k in range(nblk):
        at = pl.multiple_of((lax.axis_index("blk") ^ k) * height, height)
        whole_ref[pl.ds(at, height), :] = inverses[k][...]
    for at in range(slope_ref.shape[0]):
        slope_ref[at] = old_slope[at]
    settle(arrived, CAP, slope_ref)


def where_kernel(rounds, span, rcap, last, partner_ref, _, index_ref, late_ref, reads, mine, starts, sem):
    n = len(rounds) + 1
    blocks = index_ref.shape[0]
    die = lax.axis_index("die")
    copy = pltpu.make_async_copy(partner_ref, reads, sem)
    copy.start()
    starts[0] = 0
    for at, k in enumerate(rounds):
        starts[k] = at * rcap
    copy.wait()
    read_masks(n, span, blocks, reads, mine)

    def step(at, count):
        owner, local = divmod_static(reads[at], span)
        local = divmod_static(local, blocks)[1]
        k = owner ^ die
        slot = bits_set(mine[owner] & (bit_of(local) - 1))
        index_ref[at] = jnp.where(k == 0, local - blocks, starts[k] + slot)
        late_ref[1 + count] = at
        return count + jnp.where(k == rounds[last], 1, 0)

    for at in range(1 + blocks):
        late_ref[at] = 0
    late_ref[0] = lax.fori_loop(0, blocks, step, jnp.int32(0))


def local_kernel(
    guess_ref, slope_ref, coupling_ref, cap_ref, gdev_ref, wire_ref, gain_ref, drive_ref,
    base_ref, inv_ref, scale_ref, kept_ref
):
    nodes = coupling_ref.shape[1]
    rows = lax.broadcasted_iota(I32, (nodes, nodes), 0)
    cols = lax.broadcasted_iota(I32, (nodes, nodes), 1)
    for at in range(guess_ref.shape[0]):
        guess = guess_ref[at]
        coupling = coupling_ref[at]
        cap = cap_ref[at : at + 1, :]
        gdev = gdev_ref[at : at + 1, :]
        wire = wire_ref[at : at + 1, :]
        through = lax.dot_general(
            guess,
            coupling,
            (((1,), (1,)), ((), ())),
            precision=lax.Precision.HIGHEST,
            preferred_element_type=F32,
        )
        diagonal = jnp.sum(jnp.where(rows == cols, coupling, 0.0), axis=0, keepdims=True)
        tnh = jnp.tanh(guess)
        inv = 1.0 / (1.5 * cap + diagonal + gdev * (1.0 - tnh * tnh) + wire)
        inv_ref[at] = inv
        kept_ref[at : at + 1, :] = wire
        scale_ref[at] = gain_ref[at : at + 1, :] * inv
        base_ref[at] = (
            0.5 * cap * slope_ref[at] + through + gdev * tnh + wire * guess - drive_ref[at]
        )


def gather_kernel(rcap, last, index_ref, base_ref, scale_ref, guess_ref, wire_ref, *rest):
    blocks_in, (near_ref, share_ref, pool) = rest[:-3], rest[-3:]
    blocks = guess_ref.shape[0]
    for at, ref in enumerate(blocks_in):
        for slot in range(rcap):
            pool[(at + (at >= last)) * rcap + slot] = ref[slot]
    share = jnp.zeros(share_ref.shape, F32)
    for at in range(blocks):
        index = index_ref[at]
        own = index < 0
        near = guess_ref[jnp.where(own, index + blocks, 0)]
        near = jnp.where(own, near, pool[jnp.maximum(index, 0)])
        missing = (index >= last * rcap) & (index < (last + 1) * rcap)
        near = jnp.where(missing, 0.0, near)
        near_ref[at] = near
        share = share + scale_ref[at] * (base_ref[at] - wire_ref[at : at + 1, :] * near)
    share_ref[...] = share


def share_kernel(rcap, last, index_ref, late_ref, scale_ref, wire_ref, part_ref, block_ref, share_ref):
    share = part_ref[...]
    for slot in range(min(rcap, wire_ref.shape[0])):
        at = late_ref[1 + slot]
        there = slot < late_ref[0]
        block = block_ref[jnp.where(there, index_ref[at] - last * rcap, 0)]
        share = share - jnp.where(there, scale_ref[at] * wire_ref[pl.ds(at, 1), :] * block, 0.0)
    share_ref[...] = share


def residual_kernel(
    rcap, last, parts, index_ref, near_ref, block_ref, base_ref, inv_ref, guess_ref, wire_ref,
    partial_ref, out_ref, held, sems
):
    step = guess_ref.shape[0] // parts
    copies = []
    for part in range(parts):
        for at in range(part * step, (part + 1) * step):
            slot = index_ref[at] - last * rcap
            missing = (slot >= 0) & (slot < rcap)
            near = jnp.where(missing, block_ref[jnp.where(missing, slot, 0)], near_ref[at])
            residual = base_ref[at] - wire_ref[at : at + 1, :] * near
            held[at] = residual
            partial_ref[at] = guess_ref[at] - residual * inv_ref[at]
        some = pl.ds(part * step, step)
        copies.append(pltpu.make_async_copy(held.at[some], out_ref.at[some], sems.at[part]))
        copies[-1].start()
    for copy in copies:
        copy.wait()


def update_kernel(m, parts, *rest):
    shares, (whole_ref, partial_ref, scale_ref, updated_ref, held, sems) = rest[:m], rest[m:]
    total = shares[0][...]
    for share in shares[1:]:
        total = total + share[...]
    region = jnp.dot(
        total, whole_ref[...], precision=lax.Precision.HIGHEST, preferred_element_type=F32
    )
    step = partial_ref.shape[0] // parts
    copies = []
    for part in range(parts):
        for at in range(part * step, (part + 1) * step):
            held[at] = partial_ref[at] + scale_ref[at] * region
        span = pl.ds(part * step, step)
        copies.append(pltpu.make_async_copy(held.at[span], updated_ref.at[span], sems.at[part]))
        copies[-1].start()
    for copy in copies:
        copy.wait()


def call(body, outs, ins, in_specs, out_specs, scratch=(), limit=8):
    return pl.pallas_call(
        body,
        out_shape=outs,
        in_specs=in_specs,
        out_specs=out_specs,
        scratch_shapes=list(scratch),
        compiler_params=pltpu.CompilerParams(vmem_limit_bytes=limit << 20),
        cost_estimate=pl.CostEstimate(flops=0, bytes_accessed=0, transcendentals=0),
    )(*ins)


def in_hbm(x):
    return pltpu.with_memory_space_constraint(x, pltpu.HBM)


def swap(x, axes, n, k):
    return lax.ppermute(x, axes, [(d, d ^ k) for d in range(n)])


def shards(
    history,
    new_slot,
    partner,
    coupling,
    cap_rate,
    device_gain,
    wire_gain,
    region_gain,
    drive,
    region_inverse,
):
    blocks, _, scen, nodes = history.shape
    n = lax.axis_size("die")
    nblk = lax.axis_size("blk")
    ncol = lax.axis_size("sub") * nblk
    for size in (n, nblk, ncol):
        assert size & (size - 1) == 0
    assert CAP == 2 and blocks <= 32 and blocks & (blocks - 1) == 0
    rcap = 2 * max(1, blocks // n)
    span = ncol * blocks

    def tiles(count):
        return jax.ShapeDtypeStruct((count, scen, nodes), F32)

    def scalars(count):
        return pltpu.SMEM((count,), I32)

    block = tiles(blocks)
    square = jax.ShapeDtypeStruct((nodes, nodes), F32)
    rows = region_inverse[0]
    message = jax.ShapeDtypeStruct((2 * CAP * scen + 8, nodes), F32)

    rounds = [*range(2, n), 1]
    raw, rows, *leaving = call(
        functools.partial(leave_kernel, rounds, span),
        [jax.ShapeDtypeStruct(history.shape, F32), jax.ShapeDtypeStruct(rows.shape, F32)]
        + [message] * (n - 1),
        [
            in_hbm(new_slot.reshape(1, blocks)),
            in_hbm(partner.reshape(1, blocks)),
            in_hbm(history),
            in_hbm(rows),
        ],
        [HBM] * 4,
        [VMEM] * (n + 1),
        [pltpu.VMEM((1, blocks), I32)] * 2 + [pltpu.SemaphoreType.DMA((5,))],
    )
    arrived = [swap(x, "die", n, k) for x, k in zip(leaving, rounds)]
    inverses = [rows] + [swap(rows, "blk", nblk, k) for k in range(1, nblk)]
    old_guess, old_slope = call(
        functools.partial(place_kernel, span),
        [block, block],
        [in_hbm(new_slot), raw],
        [HBM, VMEM],
        [VMEM, VMEM],
        [scalars(blocks), pltpu.SemaphoreType.DMA],
    )
    guess, *served = call(
        functools.partial(serve_kernel, n),
        [block] + [tiles(rcap)] * (n - 1),
        [*arrived, old_guess],
        [VMEM] * n,
        [VMEM] * n,
    )
    others = [swap(x, "die", n, k) for x, k in zip(served, rounds)]
    slopes, whole = call(
        functools.partial(merge_kernel, n, nblk),
        [block, square],
        [*arrived, *inverses, old_slope, guess],
        [VMEM] * (n + nblk) + [ANY],
        [VMEM] * 2,
    )
    last = n - 2
    index, late = call(
        functools.partial(where_kernel, rounds, span, rcap, last),
        [scalars(blocks), scalars(1 + blocks)],
        [in_hbm(partner), guess],
        [HBM, ANY],
        [SMEM, SMEM],
        [scalars(blocks), scalars(n), scalars(n), pltpu.SemaphoreType.DMA],
    )
    step = 8 if blocks % 8 == 0 else blocks
    wide = pl.BlockSpec((step, scen, nodes), lambda i: (i, 0, 0))
    flat = pl.BlockSpec((step, nodes), lambda i: (i, 0))
    base, inv, scale, wire = pl.pallas_call(
        local_kernel,
        grid=(blocks // step,),
        out_shape=[block, block, block, jax.ShapeDtypeStruct((blocks, nodes), F32)],
        in_specs=[
            wide,
            wide,
            pl.BlockSpec((step, nodes, nodes), lambda i: (i, 0, 0)),
            flat,
            flat,
            flat,
            flat,
            wide,
        ],
        out_specs=[wide, wide, wide, flat],
        compiler_params=pltpu.CompilerParams(vmem_limit_bytes=8 << 20),
        cost_estimate=pl.CostEstimate(flops=0, bytes_accessed=0, transcendentals=0),
    )(
        guess,
        slopes,
        in_hbm(coupling),
        in_hbm(cap_rate),
        in_hbm(device_gain),
        in_hbm(wire_gain),
        in_hbm(region_gain),
        in_hbm(drive),
    )
    index = pltpu.with_memory_space_constraint(index, pltpu.SMEM)
    late = pltpu.with_memory_space_constraint(late, pltpu.SMEM)
    flat_share = jax.ShapeDtypeStruct((scen, nodes), F32)
    first = others[:last] + others[last + 1 :]
    near, part = call(
        functools.partial(gather_kernel, rcap, last),
        [block, flat_share],
        [index, base, scale, guess, wire, *first],
        [SMEM] + [VMEM] * (4 + len(first)),
        [VMEM] * 2,
        [pltpu.VMEM(((n - 1) * rcap, scen, nodes), F32)],
    )
    (share,) = call(
        functools.partial(share_kernel, rcap, last),
        [flat_share],
        [index, late, scale, wire, part, others[last]],
        [SMEM] * 2 + [VMEM] * 4,
        [VMEM],
    )
    parts = 4 if blocks % 4 == 0 else 1
    partial, residual = call(
        functools.partial(residual_kernel, rcap, last, parts),
        [block, block],
        [index, near, others[last], base, inv, guess, wire],
        [SMEM] + [VMEM] * 6,
        [VMEM, HBM],
        [pltpu.VMEM((blocks, scen, nodes), F32), pltpu.SemaphoreType.DMA((parts,))],
    )
    column = ("sub", "blk")
    shares = [share] + [swap(share, column, ncol, k) for k in range(1, nblk)]
    for up in (True, False):
        for k in range(nblk, ncol):
            pairs = [(d, d ^ k) for d in range(ncol) if (d < d ^ k) == up]
            shares.append(lax.ppermute(share, column, pairs))
    (updated,) = call(
        functools.partial(update_kernel, len(shares), parts),
        [block],
        [*shares, whole, partial, scale],
        [VMEM] * (len(shares) + 3),
        [HBM],
        [pltpu.VMEM((blocks, scen, nodes), F32), pltpu.SemaphoreType.DMA((parts,))],
    )
    return (updated, residual)


def solution(mesh):
    every = ("grp", "die", "sub", "blk")
    in_specs = (
        P(every, None, None, None),
        P(every),
        P(every),
        P(every, None, None),
        P(every, None),
        P(every, None),
        P(every, None),
        P(every, None),
        P(every, None, None),
        P(("grp", "die"), "blk", None),
    )
    out_specs = (P(every, None, None), P(every, None, None))
    return jax.shard_map(shards, mesh=mesh, in_specs=in_specs, out_specs=out_specs, check_vma=False)
```

```python
import functools

import jax
import jax.numpy as jnp
from jax import lax
from jax.experimental import pallas as pl
from jax.experimental.pallas import tpu as pltpu
from jax.sharding import PartitionSpec as P

CAP = 2
VMEM = pl.BlockSpec(memory_space=pltpu.VMEM)
SMEM = pl.BlockSpec(memory_space=pltpu.SMEM)
ANY = pl.BlockSpec(memory_space=pl.ANY)
HBM = pl.BlockSpec(memory_space=pltpu.HBM)
F32 = jnp.float32
I32 = jnp.int32


def divmod_static(value, size):
    if size & (size - 1) == 0:
        return lax.shift_right_logical(value, size.bit_length() - 1), value & (size - 1)
    whole = lax.div(value, size)
    return whole, value - whole * size


def bit_of(index):
    return lax.shift_left(jnp.int32(1), index)


def bits_set(x):
    x = x - (lax.shift_right_logical(x, 1) & 0x55555555)
    x = (x & 0x33333333) + (lax.shift_right_logical(x, 2) & 0x33333333)
    x = (x + lax.shift_right_logical(x, 4)) & 0x0F0F0F0F
    x = x + lax.shift_right_logical(x, 8)
    x = x + lax.shift_right_logical(x, 16)
    return x & 63


def lowest(mask):
    return jnp.maximum(31 - lax.clz(mask & -mask), 0)


def halves(mask):
    return [mask & 0xFFFF, lax.shift_right_logical(mask, 16)]


def joined(low, high):
    return low | lax.shift_left(high, 16)


def predict(raw):
    return 3.0 * raw[0] - 3.0 * raw[1] + raw[2]


def slope(raw, guess):
    return 3.0 * guess - (4.0 * raw[0] - raw[1])


def read_masks(n, span, blocks, reads, mine):
    wants = [jnp.int32(0)] * n
    for at in range(n):
        mine[at] = 0
    for at in range(blocks):
        owner, local = divmod_static(reads[at], span)
        bit = bit_of(divmod_static(local, blocks)[1])
        if n > 8:
            mine[owner] = mine[owner] | bit
        else:
            wants = [want | jnp.where(owner == o, bit, 0) for o, want in enumerate(wants)]
    if n <= 8:
        for at in range(n):
            mine[at] = wants[at]


def leave_kernel(
    rounds, span, new_slot_ref, partner_ref, history_ref, rows_ref, raw_ref, inverse_ref, *rest
):
    n = len(rounds) + 1
    outs, (slots, reads, mine, source, place, count, sems) = rest[: n - 1], rest[n - 1 :]
    blocks, _, scen, nodes = history_ref.shape
    pieces = 4 if blocks % 4 == 0 else 1
    piece = blocks // pieces
    die = lax.axis_index("die")
    copies = [
        pltpu.make_async_copy(new_slot_ref, slots, sems.at[0]),
        pltpu.make_async_copy(partner_ref, reads, sems.at[1]),
        pltpu.make_async_copy(rows_ref, inverse_ref, sems.at[2]),
    ]
    for at in range(pieces):
        some = pl.ds(at * piece, piece)
        copies.append(
            pltpu.make_async_copy(history_ref.at[some], raw_ref.at[some], sems.at[3 + at])
        )
    for copy in copies:
        copy.start()
    for at in range(n):
        count[at] = 0
    for at in range(n * CAP):
        source[at] = 0
        place[at] = -1
    copies[0].wait()
    copies[1].wait()

    for at in range(blocks):
        dest, local = divmod_static(slots[at], span)
        local = divmod_static(local, blocks)[1]

        @pl.when(dest != die)
        def _(at=at, dest=dest, local=local):
            rank = count[dest]
            count[dest] = rank + 1
            turn = (dest ^ die) * CAP + rank
            source[turn] = at
            place[turn] = local

    read_masks(n, span, blocks, reads, mine)
    for copy in copies[2:]:
        copy.wait()
    line = lax.broadcasted_iota(I32, (8, nodes), 0)
    for k, out in zip(rounds, outs):
        for rank in range(CAP):
            raw = raw_ref.at[source[k * CAP + rank]]
            guess = predict(raw)
            out[pl.ds(rank * scen, scen), :] = guess
            out[pl.ds((CAP + rank) * scen, scen), :] = slope(raw, guess)
        row = jnp.zeros((8, nodes), I32)
        values = halves(mine[die ^ k])
        values += [place[k * CAP + rank] for rank in range(CAP)]
        for j, value in enumerate(values):
            row = jnp.where(line == j, value, row)
        out[pl.ds(2 * CAP * scen, 8), :] = row.astype(F32)


def place_kernel(span, new_slot_ref, raw_ref, guess_ref, slope_ref, slots, sem):
    blocks = raw_ref.shape[0]
    die = lax.axis_index("die")
    copy = pltpu.make_async_copy(new_slot_ref, slots, sem)
    copy.start()
    copy.wait()
    for at in range(blocks):
        dest, local = divmod_static(slots[at], span)
        local = divmod_static(local, blocks)[1]

        @pl.when(dest == die)
        def _(at=at, local=local):
            raw = raw_ref.at[at]
            guess = predict(raw)
            guess_ref[local] = guess
            slope_ref[local] = slope(raw, guess)


def told(message, j):
    return message[message.shape[0] - 8 + j, 0].astype(I32)


def settle(arrived, first, out):
    scen = out.shape[1]
    for message in arrived:
        for rank in range(CAP):
            place = told(message, 2 + rank)

            @pl.when(place >= 0)
            def _(message=message, rank=rank, place=place):
                out[place] = message[pl.ds((first + rank) * scen, scen), :]


def serve_kernel(n, *rest):
    arrived, (old_guess, guess_ref, *outs) = rest[: n - 1], rest[n - 1 :]
    for at in range(guess_ref.shape[0]):
        guess_ref[at] = old_guess[at]
    settle(arrived, 0, guess_ref)
    for message, out in zip(arrived, outs):
        want = joined(told(message, 0), told(message, 1))
        for slot in range(out.shape[0]):
            out[slot] = guess_ref[lowest(want)]
            want = want & (want - 1)


def merge_kernel(n, nblk, *rest):
    arrived, rest = rest[: n - 1], rest[n - 1 :]
    inverses, (old_slope, _, slope_ref, whole_ref) = rest[:nblk], rest[nblk:]
    height = inverses[0].shape[0]
    for k in range(nblk):
        at = pl.multiple_of((lax.axis_index("blk") ^ k) * height, height)
        whole_ref[pl.ds(at, height), :] = inverses[k][...]
    for at in range(slope_ref.shape[0]):
        slope_ref[at] = old_slope[at]
    settle(arrived, CAP, slope_ref)


def where_kernel(rounds, span, rcap, last, partner_ref, _, index_ref, late_ref, reads, mine, starts, sem):
    n = len(rounds) + 1
    blocks = index_ref.shape[0]
    die = lax.axis_index("die")
    copy = pltpu.make_async_copy(partner_ref, reads, sem)
    copy.start()
    starts[0] = 0
    for at, k in enumerate(rounds):
        starts[k] = at * rcap
    copy.wait()
    read_masks(n, span, blocks, reads, mine)

    def step(at, count):
        owner, local = divmod_static(reads[at], span)
        local = divmod_static(local, blocks)[1]
        k = owner ^ die
        slot = bits_set(mine[owner] & (bit_of(local) - 1))
        index_ref[at] = jnp.where(k == 0, local - blocks, starts[k] + slot)
        late_ref[1 + count] = at
        return count + jnp.where(k == rounds[last], 1, 0)

    for at in range(1 + blocks):
        late_ref[at] = 0
    late_ref[0] = lax.fori_loop(0, blocks, step, jnp.int32(0))


def local_kernel(
    guess_ref, slope_ref, coupling_ref, cap_ref, gdev_ref, wire_ref, gain_ref, drive_ref,
    base_ref, inv_ref, scale_ref, kept_ref
):
    nodes = coupling_ref.shape[1]
    rows = lax.broadcasted_iota(I32, (nodes, nodes), 0)
    cols = lax.broadcasted_iota(I32, (nodes, nodes), 1)
    for at in range(guess_ref.shape[0]):
        guess = guess_ref[at]
        coupling = coupling_ref[at]
        cap = cap_ref[at : at + 1, :]
        gdev = gdev_ref[at : at + 1, :]
        wire = wire_ref[at : at + 1, :]
        through = lax.dot_general(
            guess,
            coupling,
            (((1,), (1,)), ((), ())),
            precision=lax.Precision.HIGHEST,
            preferred_element_type=F32,
        )
        diagonal = jnp.sum(jnp.where(rows == cols, coupling, 0.0), axis=0, keepdims=True)
        tnh = jnp.tanh(guess)
        inv = 1.0 / (1.5 * cap + diagonal + gdev * (1.0 - tnh * tnh) + wire)
        inv_ref[at] = inv
        kept_ref[at : at + 1, :] = wire
        scale_ref[at] = gain_ref[at : at + 1, :] * inv
        base_ref[at] = (
            0.5 * cap * slope_ref[at] + through + gdev * tnh + wire * guess - drive_ref[at]
        )


def gather_kernel(rcap, last, index_ref, base_ref, scale_ref, guess_ref, wire_ref, *rest):
    blocks_in, (near_ref, share_ref, pool) = rest[:-3], rest[-3:]
    blocks = guess_ref.shape[0]
    for at, ref in enumerate(blocks_in):
        for slot in range(rcap):
            pool[(at + (at >= last)) * rcap + slot] = ref[slot]
    share = jnp.zeros(share_ref.shape, F32)
    for at in range(blocks):
        index = index_ref[at]
        own = index < 0
        near = guess_ref[jnp.where(own, index + blocks, 0)]
        near = jnp.where(own, near, pool[jnp.maximum(index, 0)])
        missing = (index >= last * rcap) & (index < (last + 1) * rcap)
        near = jnp.where(missing, 0.0, near)
        near_ref[at] = near
        share = share + scale_ref[at] * (base_ref[at] - wire_ref[at : at + 1, :] * near)
    share_ref[...] = share


def share_kernel(rcap, last, index_ref, late_ref, scale_ref, wire_ref, part_ref, block_ref, share_ref):
    share = part_ref[...]
    for slot in range(min(rcap, wire_ref.shape[0])):
        at = late_ref[1 + slot]
        there = slot < late_ref[0]
        block = block_ref[jnp.where(there, index_ref[at] - last * rcap, 0)]
        share = share - jnp.where(there, scale_ref[at] * wire_ref[pl.ds(at, 1), :] * block, 0.0)
    share_ref[...] = share


def residual_kernel(
    rcap, last, parts, index_ref, near_ref, block_ref, base_ref, inv_ref, guess_ref, wire_ref,
    partial_ref, out_ref, held, sems
):
    step = guess_ref.shape[0] // parts
    copies = []
    for part in range(parts):
        for at in range(part * step, (part + 1) * step):
            slot = index_ref[at] - last * rcap
            missing = (slot >= 0) & (slot < rcap)
            near = jnp.where(missing, block_ref[jnp.where(missing, slot, 0)], near_ref[at])
            residual = base_ref[at] - wire_ref[at : at + 1, :] * near
            held[at] = residual
            partial_ref[at] = guess_ref[at] - residual * inv_ref[at]
        some = pl.ds(part * step, step)
        copies.append(pltpu.make_async_copy(held.at[some], out_ref.at[some], sems.at[part]))
        copies[-1].start()
    for copy in copies:
        copy.wait()


def update_kernel(m, parts, *rest):
    shares, (whole_ref, partial_ref, scale_ref, updated_ref, held, sems) = rest[:m], rest[m:]
    total = shares[0][...]
    for share in shares[1:]:
        total = total + share[...]
    region = jnp.dot(
        total, whole_ref[...], precision=lax.Precision.HIGHEST, preferred_element_type=F32
    )
    step = partial_ref.shape[0] // parts
    copies = []
    for part in range(parts):
        for at in range(part * step, (part + 1) * step):
            held[at] = partial_ref[at] + scale_ref[at] * region
        span = pl.ds(part * step, step)
        copies.append(pltpu.make_async_copy(held.at[span], updated_ref.at[span], sems.at[part]))
        copies[-1].start()
    for copy in copies:
        copy.wait()


def call(body, outs, ins, in_specs, out_specs, scratch=(), limit=8):
    return pl.pallas_call(
        body,
        out_shape=outs,
        in_specs=in_specs,
        out_specs=out_specs,
        scratch_shapes=list(scratch),
        compiler_params=pltpu.CompilerParams(vmem_limit_bytes=limit << 20),
        cost_estimate=pl.CostEstimate(flops=0, bytes_accessed=0, transcendentals=0),
    )(*ins)


def in_hbm(x):
    return pltpu.with_memory_space_constraint(x, pltpu.HBM)


def swap(x, axes, n, k):
    return lax.ppermute(x, axes, [(d, d ^ k) for d in range(n)])


def shards(
    history,
    new_slot,
    partner,
    coupling,
    cap_rate,
    device_gain,
    wire_gain,
    region_gain,
    drive,
    region_inverse,
):
    blocks, _, scen, nodes = history.shape
    n = lax.axis_size("die")
    nblk = lax.axis_size("blk")
    ncol = lax.axis_size("sub") * nblk
    for size in (n, nblk, ncol):
        assert size & (size - 1) == 0
    assert CAP == 2 and blocks <= 32 and blocks & (blocks - 1) == 0
    rcap = 2 * max(1, blocks // n)
    span = ncol * blocks

    def tiles(count):
        return jax.ShapeDtypeStruct((count, scen, nodes), F32)

    def scalars(count):
        return pltpu.SMEM((count,), I32)

    block = tiles(blocks)
    square = jax.ShapeDtypeStruct((nodes, nodes), F32)
    rows = region_inverse[0]
    message = jax.ShapeDtypeStruct((2 * CAP * scen + 8, nodes), F32)

    rounds = [*range(2, n), 1]
    new_slot, partner = in_hbm(new_slot), in_hbm(partner)
    raw, rows, *leaving = call(
        functools.partial(leave_kernel, rounds, span),
        [jax.ShapeDtypeStruct(history.shape, F32), jax.ShapeDtypeStruct(rows.shape, F32)]
        + [message] * (n - 1),
        [new_slot, partner, in_hbm(history), in_hbm(rows)],
        [HBM] * 4,
        [VMEM] * (n + 1),
        [scalars(blocks)] * 2
        + [scalars(n)]
        + [scalars(n * CAP)] * 2
        + [scalars(n), pltpu.SemaphoreType.DMA((7,))],
    )
    arrived = [swap(x, "die", n, k) for x, k in zip(leaving, rounds)]
    inverses = [rows] + [swap(rows, "blk", nblk, k) for k in range(1, nblk)]
    old_guess, old_slope = call(
        functools.partial(place_kernel, span),
        [block, block],
        [new_slot, raw],
        [HBM, VMEM],
        [VMEM, VMEM],
        [scalars(blocks), pltpu.SemaphoreType.DMA],
    )
    guess, *served = call(
        functools.partial(serve_kernel, n),
        [block] + [tiles(rcap)] * (n - 1),
        [*arrived, old_guess],
        [VMEM] * n,
        [VMEM] * n,
    )
    others = [swap(x, "die", n, k) for x, k in zip(served, rounds)]
    slopes, whole = call(
        functools.partial(merge_kernel, n, nblk),
        [block, square],
        [*arrived, *inverses, old_slope, guess],
        [VMEM] * (n + nblk) + [ANY],
        [VMEM] * 2,
    )
    last = n - 2
    index, late = call(
        functools.partial(where_kernel, rounds, span, rcap, last),
        [scalars(blocks), scalars(1 + blocks)],
        [partner, guess],
        [HBM, ANY],
        [SMEM, SMEM],
        [scalars(blocks), scalars(n), scalars(n), pltpu.SemaphoreType.DMA],
    )
    step = 8 if blocks % 8 == 0 else blocks
    wide = pl.BlockSpec((step, scen, nodes), lambda i: (i, 0, 0))
    flat = pl.BlockSpec((step, nodes), lambda i: (i, 0))
    base, inv, scale, wire = pl.pallas_call(
        local_kernel,
        grid=(blocks // step,),
        out_shape=[block, block, block, jax.ShapeDtypeStruct((blocks, nodes), F32)],
        in_specs=[
            wide,
            wide,
            pl.BlockSpec((step, nodes, nodes), lambda i: (i, 0, 0)),
            flat,
            flat,
            flat,
            flat,
            wide,
        ],
        out_specs=[wide, wide, wide, flat],
        compiler_params=pltpu.CompilerParams(vmem_limit_bytes=8 << 20),
        cost_estimate=pl.CostEstimate(flops=0, bytes_accessed=0, transcendentals=0),
    )(
        guess,
        slopes,
        in_hbm(coupling),
        in_hbm(cap_rate),
        in_hbm(device_gain),
        in_hbm(wire_gain),
        in_hbm(region_gain),
        in_hbm(drive),
    )
    index = pltpu.with_memory_space_constraint(index, pltpu.SMEM)
    late = pltpu.with_memory_space_constraint(late, pltpu.SMEM)
    flat_share = jax.ShapeDtypeStruct((scen, nodes), F32)
    first = others[:last] + others[last + 1 :]
    near, part = call(
        functools.partial(gather_kernel, rcap, last),
        [block, flat_share],
        [index, base, scale, guess, wire, *first],
        [SMEM] + [VMEM] * (4 + len(first)),
        [VMEM] * 2,
        [pltpu.VMEM(((n - 1) * rcap, scen, nodes), F32)],
    )
    (share,) = call(
        functools.partial(share_kernel, rcap, last),
        [flat_share],
        [index, late, scale, wire, part, others[last]],
        [SMEM] * 2 + [VMEM] * 4,
        [VMEM],
    )
    parts = 4 if blocks % 4 == 0 else 1
    partial, residual = call(
        functools.partial(residual_kernel, rcap, last, parts),
        [block, block],
        [index, near, others[last], base, inv, guess, wire],
        [SMEM] + [VMEM] * 6,
        [VMEM, HBM],
        [pltpu.VMEM((blocks, scen, nodes), F32), pltpu.SemaphoreType.DMA((parts,))],
    )
    shares = [share] + [swap(share, ("sub", "blk"), ncol, k) for k in range(1, ncol)]
    (updated,) = call(
        functools.partial(update_kernel, ncol, parts),
        [block],
        [*shares, whole, partial, scale],
        [VMEM] * (ncol + 3),
        [HBM],
        [pltpu.VMEM((blocks, scen, nodes), F32), pltpu.SemaphoreType.DMA((parts,))],
    )
    return (updated, residual)


def solution(mesh):
    every = ("grp", "die", "sub", "blk")
    in_specs = (
        P(every, None, None, None),
        P(every),
        P(every),
        P(every, None, None),
        P(every, None),
        P(every, None),
        P(every, None),
        P(every, None),
        P(every, None, None),
        P(("grp", "die"), "blk", None),
    )
    out_specs = (P(every, None, None), P(every, None, None))
    return jax.shard_map(shards, mesh=mesh, in_specs=in_specs, out_specs=out_specs, check_vma=False)
```

```python
import functools

import jax
import jax.numpy as jnp
from jax import lax
from jax.experimental import pallas as pl
from jax.experimental.pallas import tpu as pltpu
from jax.sharding import PartitionSpec as P

CAP = 2
VMEM = pl.BlockSpec(memory_space=pltpu.VMEM)
SMEM = pl.BlockSpec(memory_space=pltpu.SMEM)
ANY = pl.BlockSpec(memory_space=pl.ANY)
HBM = pl.BlockSpec(memory_space=pltpu.HBM)
F32 = jnp.float32
I32 = jnp.int32


def divmod_static(value, size):
    if size & (size - 1) == 0:
        return lax.shift_right_logical(value, size.bit_length() - 1), value & (size - 1)
    whole = lax.div(value, size)
    return whole, value - whole * size


def bit_of(index):
    return lax.shift_left(jnp.int32(1), index)


def bits_set(x):
    x = x - (lax.shift_right_logical(x, 1) & 0x55555555)
    x = (x & 0x33333333) + (lax.shift_right_logical(x, 2) & 0x33333333)
    x = (x + lax.shift_right_logical(x, 4)) & 0x0F0F0F0F
    x = x + lax.shift_right_logical(x, 8)
    x = x + lax.shift_right_logical(x, 16)
    return x & 63


def lowest(mask):
    return jnp.maximum(31 - lax.clz(mask & -mask), 0)


def halves(mask):
    return [mask & 0xFFFF, lax.shift_right_logical(mask, 16)]


def joined(low, high):
    return low | lax.shift_left(high, 16)


def predict(raw):
    return 3.0 * raw[0] - 3.0 * raw[1] + raw[2]


def slope(raw, guess):
    return 3.0 * guess - (4.0 * raw[0] - raw[1])


def read_masks(n, span, blocks, reads, mine):
    wants = [jnp.int32(0)] * n
    for at in range(n):
        mine[at] = 0
    for at in range(blocks):
        owner, local = divmod_static(reads[at], span)
        bit = bit_of(divmod_static(local, blocks)[1])
        if n > 8:
            mine[owner] = mine[owner] | bit
        else:
            wants = [want | jnp.where(owner == o, bit, 0) for o, want in enumerate(wants)]
    if n <= 8:
        for at in range(n):
            mine[at] = wants[at]


def leave_kernel(
    rounds, span, new_slot_ref, partner_ref, history_ref, rows_ref, raw_ref, inverse_ref, *rest
):
    n = len(rounds) + 1
    outs, (slots, reads, mine, source, place, count, sems) = rest[: n - 1], rest[n - 1 :]
    blocks, _, scen, nodes = history_ref.shape
    pieces = 4 if blocks % 4 == 0 else 1
    piece = blocks // pieces
    die = lax.axis_index("die")
    copies = [
        pltpu.make_async_copy(new_slot_ref, slots, sems.at[0]),
        pltpu.make_async_copy(partner_ref, reads, sems.at[1]),
        pltpu.make_async_copy(rows_ref, inverse_ref, sems.at[2]),
    ]
    for at in range(pieces):
        some = pl.ds(at * piece, piece)
        copies.append(
            pltpu.make_async_copy(history_ref.at[some], raw_ref.at[some], sems.at[3 + at])
        )
    for copy in copies:
        copy.start()
    for at in range(n):
        count[at] = 0
    for at in range(n * CAP):
        source[at] = 0
        place[at] = -1
    copies[0].wait()
    copies[1].wait()

    for at in range(blocks):
        dest, local = divmod_static(slots[at], span)
        local = divmod_static(local, blocks)[1]

        @pl.when(dest != die)
        def _(at=at, dest=dest, local=local):
            rank = count[dest]
            count[dest] = rank + 1
            turn = (dest ^ die) * CAP + rank
            source[turn] = at
            place[turn] = local

    read_masks(n, span, blocks, reads, mine)
    for copy in copies[2:]:
        copy.wait()
    line = lax.broadcasted_iota(I32, (8, nodes), 0)
    for k, out in zip(rounds, outs):
        for rank in range(CAP):
            raw = raw_ref.at[source[k * CAP + rank]]
            guess = predict(raw)
            out[pl.ds(rank * scen, scen), :] = guess
            out[pl.ds((CAP + rank) * scen, scen), :] = slope(raw, guess)
        row = jnp.zeros((8, nodes), I32)
        values = halves(mine[die ^ k])
        values += [place[k * CAP + rank] for rank in range(CAP)]
        for j, value in enumerate(values):
            row = jnp.where(line == j, value, row)
        out[pl.ds(2 * CAP * scen, 8), :] = row.astype(F32)


def place_kernel(span, new_slot_ref, raw_ref, guess_ref, slope_ref, slots, sem):
    blocks = raw_ref.shape[0]
    die = lax.axis_index("die")
    copy = pltpu.make_async_copy(new_slot_ref, slots, sem)
    copy.start()
    copy.wait()
    for at in range(blocks):
        dest, local = divmod_static(slots[at], span)
        local = divmod_static(local, blocks)[1]

        @pl.when(dest == die)
        def _(at=at, local=local):
            raw = raw_ref.at[at]
            guess = predict(raw)
            guess_ref[local] = guess
            slope_ref[local] = slope(raw, guess)


def told(message, j):
    return message[message.shape[0] - 8 + j, 0].astype(I32)


def settle(arrived, first, out):
    scen = out.shape[1]
    for message in arrived:
        for rank in range(CAP):
            place = told(message, 2 + rank)

            @pl.when(place >= 0)
            def _(message=message, rank=rank, place=place):
                out[place] = message[pl.ds((first + rank) * scen, scen), :]


def serve_kernel(n, *rest):
    arrived, (old_guess, guess_ref, *outs) = rest[: n - 1], rest[n - 1 :]
    for at in range(guess_ref.shape[0]):
        guess_ref[at] = old_guess[at]
    settle(arrived, 0, guess_ref)
    for message, out in zip(arrived, outs):
        want = joined(told(message, 0), told(message, 1))
        for slot in range(out.shape[0]):
            out[slot] = guess_ref[lowest(want)]
            want = want & (want - 1)


def merge_kernel(n, nblk, *rest):
    arrived, rest = rest[: n - 1], rest[n - 1 :]
    inverses, (old_slope, _, slope_ref, whole_ref) = rest[:nblk], rest[nblk:]
    height = inverses[0].shape[0]
    for k in range(nblk):
        at = pl.multiple_of((lax.axis_index("blk") ^ k) * height, height)
        whole_ref[pl.ds(at, height), :] = inverses[k][...]
    for at in range(slope_ref.shape[0]):
        slope_ref[at] = old_slope[at]
    settle(arrived, CAP, slope_ref)


def where_kernel(rounds, span, rcap, last, partner_ref, _, index_ref, late_ref, reads, mine, starts, sem):
    n = len(rounds) + 1
    blocks = index_ref.shape[0]
    die = lax.axis_index("die")
    copy = pltpu.make_async_copy(partner_ref, reads, sem)
    copy.start()
    starts[0] = 0
    for at, k in enumerate(rounds):
        starts[k] = at * rcap
    copy.wait()
    read_masks(n, span, blocks, reads, mine)

    def step(at, count):
        owner, local = divmod_static(reads[at], span)
        local = divmod_static(local, blocks)[1]
        k = owner ^ die
        slot = bits_set(mine[owner] & (bit_of(local) - 1))
        index_ref[at] = jnp.where(k == 0, local - blocks, starts[k] + slot)
        late_ref[1 + count] = at
        return count + jnp.where(k == rounds[last], 1, 0)

    for at in range(1 + blocks):
        late_ref[at] = 0
    late_ref[0] = lax.fori_loop(0, blocks, step, jnp.int32(0))


def local_kernel(
    guess_ref, slope_ref, coupling_ref, cap_ref, gdev_ref, wire_ref, gain_ref, drive_ref,
    base_ref, inv_ref, scale_ref, kept_ref
):
    nodes = coupling_ref.shape[1]
    rows = lax.broadcasted_iota(I32, (nodes, nodes), 0)
    cols = lax.broadcasted_iota(I32, (nodes, nodes), 1)
    for at in range(guess_ref.shape[0]):
        guess = guess_ref[at]
        coupling = coupling_ref[at]
        cap = cap_ref[at : at + 1, :]
        gdev = gdev_ref[at : at + 1, :]
        wire = wire_ref[at : at + 1, :]
        through = lax.dot_general(
            guess,
            coupling,
            (((1,), (1,)), ((), ())),
            precision=lax.Precision.HIGHEST,
            preferred_element_type=F32,
        )
        diagonal = jnp.sum(jnp.where(rows == cols, coupling, 0.0), axis=0, keepdims=True)
        tnh = jnp.tanh(guess)
        inv = 1.0 / (1.5 * cap + diagonal + gdev * (1.0 - tnh * tnh) + wire)
        inv_ref[at] = inv
        kept_ref[at : at + 1, :] = wire
        scale_ref[at] = gain_ref[at : at + 1, :] * inv
        base_ref[at] = (
            0.5 * cap * slope_ref[at] + through + gdev * tnh + wire * guess - drive_ref[at]
        )


def gather_kernel(rcap, last, index_ref, base_ref, scale_ref, guess_ref, wire_ref, *rest):
    blocks_in, (near_ref, share_ref, pool) = rest[:-3], rest[-3:]
    blocks = guess_ref.shape[0]
    for at, ref in enumerate(blocks_in):
        for slot in range(rcap):
            pool[(at + (at >= last)) * rcap + slot] = ref[slot]
    share = jnp.zeros(share_ref.shape, F32)
    for at in range(blocks):
        index = index_ref[at]
        own = index < 0
        near = guess_ref[jnp.where(own, index + blocks, 0)]
        near = jnp.where(own, near, pool[jnp.maximum(index, 0)])
        missing = (index >= last * rcap) & (index < (last + 1) * rcap)
        near = jnp.where(missing, 0.0, near)
        near_ref[at] = near
        share = share + scale_ref[at] * (base_ref[at] - wire_ref[at : at + 1, :] * near)
    share_ref[...] = share


def share_kernel(rcap, last, index_ref, late_ref, scale_ref, wire_ref, part_ref, block_ref, share_ref):
    share = part_ref[...]
    for slot in range(min(rcap, wire_ref.shape[0])):
        at = late_ref[1 + slot]
        there = slot < late_ref[0]
        block = block_ref[jnp.where(there, index_ref[at] - last * rcap, 0)]
        share = share - jnp.where(there, scale_ref[at] * wire_ref[pl.ds(at, 1), :] * block, 0.0)
    share_ref[...] = share


def residual_kernel(
    rcap, last, parts, index_ref, near_ref, block_ref, base_ref, inv_ref, guess_ref, wire_ref,
    partial_ref, out_ref, held, sems
):
    step = guess_ref.shape[0] // parts
    copies = []
    for part in range(parts):
        for at in range(part * step, (part + 1) * step):
            slot = index_ref[at] - last * rcap
            missing = (slot >= 0) & (slot < rcap)
            near = jnp.where(missing, block_ref[jnp.where(missing, slot, 0)], near_ref[at])
            residual = base_ref[at] - wire_ref[at : at + 1, :] * near
            held[at] = residual
            partial_ref[at] = guess_ref[at] - residual * inv_ref[at]
        some = pl.ds(part * step, step)
        copies.append(pltpu.make_async_copy(held.at[some], out_ref.at[some], sems.at[part]))
        copies[-1].start()
    for copy in copies:
        copy.wait()


def update_kernel(m, parts, *rest):
    shares, (whole_ref, partial_ref, scale_ref, updated_ref, held, sems) = rest[:m], rest[m:]
    total = shares[0][...]
    for share in shares[1:]:
        total = total + share[...]
    region = jnp.dot(
        total, whole_ref[...], precision=lax.Precision.HIGHEST, preferred_element_type=F32
    )
    step = partial_ref.shape[0] // parts
    copies = []
    for part in range(parts):
        for at in range(part * step, (part + 1) * step):
            held[at] = partial_ref[at] + scale_ref[at] * region
        span = pl.ds(part * step, step)
        copies.append(pltpu.make_async_copy(held.at[span], updated_ref.at[span], sems.at[part]))
        copies[-1].start()
    for copy in copies:
        copy.wait()


def call(body, outs, ins, in_specs, out_specs, scratch=(), limit=8):
    return pl.pallas_call(
        body,
        out_shape=outs,
        in_specs=in_specs,
        out_specs=out_specs,
        scratch_shapes=list(scratch),
        compiler_params=pltpu.CompilerParams(vmem_limit_bytes=limit << 20),
        cost_estimate=pl.CostEstimate(flops=0, bytes_accessed=0, transcendentals=0),
    )(*ins)


def in_hbm(x):
    return pltpu.with_memory_space_constraint(x, pltpu.HBM)


def swap(x, axes, n, k):
    return lax.ppermute(x, axes, [(d, d ^ k) for d in range(n)])


def shards(
    history,
    new_slot,
    partner,
    coupling,
    cap_rate,
    device_gain,
    wire_gain,
    region_gain,
    drive,
    region_inverse,
):
    blocks, _, scen, nodes = history.shape
    n = lax.axis_size("die")
    nblk = lax.axis_size("blk")
    ncol = lax.axis_size("sub") * nblk
    for size in (n, nblk, ncol):
        assert size & (size - 1) == 0
    assert CAP == 2 and blocks <= 32 and blocks & (blocks - 1) == 0
    rcap = 2 * max(1, blocks // n)
    span = ncol * blocks

    def tiles(count):
        return jax.ShapeDtypeStruct((count, scen, nodes), F32)

    def scalars(count):
        return pltpu.SMEM((count,), I32)

    block = tiles(blocks)
    square = jax.ShapeDtypeStruct((nodes, nodes), F32)
    rows = region_inverse[0]
    message = jax.ShapeDtypeStruct((2 * CAP * scen + 8, nodes), F32)

    rounds = [*range(2, n), 1]
    new_slot, partner = in_hbm(new_slot), in_hbm(partner)
    raw, rows, *leaving = call(
        functools.partial(leave_kernel, rounds, span),
        [jax.ShapeDtypeStruct(history.shape, F32), jax.ShapeDtypeStruct(rows.shape, F32)]
        + [message] * (n - 1),
        [new_slot, partner, in_hbm(history), in_hbm(rows)],
        [HBM] * 4,
        [VMEM] * (n + 1),
        [scalars(blocks)] * 2
        + [scalars(n)]
        + [scalars(n * CAP)] * 2
        + [scalars(n), pltpu.SemaphoreType.DMA((7,))],
    )
    arrived = [swap(x, "die", n, k) for x, k in zip(leaving, rounds)]
    inverses = [rows] + [swap(rows, "blk", nblk, k) for k in range(1, nblk)]
    old_guess, old_slope = call(
        functools.partial(place_kernel, span),
        [block, block],
        [new_slot, raw],
        [HBM, VMEM],
        [VMEM, VMEM],
        [scalars(blocks), pltpu.SemaphoreType.DMA],
    )
    guess, *served = call(
        functools.partial(serve_kernel, n),
        [block] + [tiles(rcap)] * (n - 1),
        [*arrived, old_guess],
        [VMEM] * n,
        [VMEM] * n,
    )
    others = [swap(x, "die", n, k) for x, k in zip(served, rounds)]
    slopes, whole = call(
        functools.partial(merge_kernel, n, nblk),
        [block, square],
        [*arrived, *inverses, old_slope, guess],
        [VMEM] * (n + nblk) + [ANY],
        [VMEM] * 2,
    )
    last = n - 2
    index, late = call(
        functools.partial(where_kernel, rounds, span, rcap, last),
        [scalars(blocks), scalars(1 + blocks)],
        [partner, guess],
        [HBM, ANY],
        [SMEM, SMEM],
        [scalars(blocks), scalars(n), scalars(n), pltpu.SemaphoreType.DMA],
    )
    step = 8 if blocks % 8 == 0 else blocks
    wide = pl.BlockSpec((step, scen, nodes), lambda i: (i, 0, 0))
    flat = pl.BlockSpec((step, nodes), lambda i: (i, 0))
    base, inv, scale, wire = pl.pallas_call(
        local_kernel,
        grid=(blocks // step,),
        out_shape=[block, block, block, jax.ShapeDtypeStruct((blocks, nodes), F32)],
        in_specs=[
            wide,
            wide,
            pl.BlockSpec((step, nodes, nodes), lambda i: (i, 0, 0)),
            flat,
            flat,
            flat,
            flat,
            wide,
        ],
        out_specs=[wide, wide, wide, flat],
        compiler_params=pltpu.CompilerParams(vmem_limit_bytes=8 << 20),
        cost_estimate=pl.CostEstimate(flops=0, bytes_accessed=0, transcendentals=0),
    )(
        guess,
        slopes,
        in_hbm(coupling),
        in_hbm(cap_rate),
        in_hbm(device_gain),
        in_hbm(wire_gain),
        in_hbm(region_gain),
        in_hbm(drive),
    )
    index = pltpu.with_memory_space_constraint(index, pltpu.SMEM)
    late = pltpu.with_memory_space_constraint(late, pltpu.SMEM)
    flat_share = jax.ShapeDtypeStruct((scen, nodes), F32)
    first = others[:last] + others[last + 1 :]
    near, part = call(
        functools.partial(gather_kernel, rcap, last),
        [block, flat_share],
        [index, base, scale, guess, wire, *first],
        [SMEM] + [VMEM] * (4 + len(first)),
        [VMEM] * 2,
        [pltpu.VMEM(((n - 1) * rcap, scen, nodes), F32)],
    )
    (share,) = call(
        functools.partial(share_kernel, rcap, last),
        [flat_share],
        [index, late, scale, wire, part, others[last]],
        [SMEM] * 2 + [VMEM] * 4,
        [VMEM],
    )
    parts = 4 if blocks % 4 == 0 else 1
    partial, residual = call(
        functools.partial(residual_kernel, rcap, last, parts),
        [block, block],
        [index, near, others[last], base, inv, guess, wire],
        [SMEM] + [VMEM] * 6,
        [VMEM, HBM],
        [pltpu.VMEM((blocks, scen, nodes), F32), pltpu.SemaphoreType.DMA((parts,))],
    )
    turns = [*range(1, nblk), *range(ncol - 1, nblk - 1, -1)]
    shares = [share] + [swap(share, ("sub", "blk"), ncol, k) for k in turns]
    (updated,) = call(
        functools.partial(update_kernel, ncol, parts),
        [block],
        [*shares, whole, partial, scale],
        [VMEM] * (ncol + 3),
        [HBM],
        [pltpu.VMEM((blocks, scen, nodes), F32), pltpu.SemaphoreType.DMA((parts,))],
    )
    return (updated, residual)


def solution(mesh):
    every = ("grp", "die", "sub", "blk")
    in_specs = (
        P(every, None, None, None),
        P(every),
        P(every),
        P(every, None, None),
        P(every, None),
        P(every, None),
        P(every, None),
        P(every, None),
        P(every, None, None),
        P(("grp", "die"), "blk", None),
    )
    out_specs = (P(every, None, None), P(every, None, None))
    return jax.shard_map(shards, mesh=mesh, in_specs=in_specs, out_specs=out_specs, check_vma=False)
```
